256 devices in a mesh: seq: 64 (over y, z, core), ffn: 4 (over x).
Axes of the slice: x: 4, y: 4, z: 8, core: 2. Of those that a mesh axis runs over, the one named last changes fastest.
Arguments:
- frames_in: bfloat16 [64, 512, 2048], P('seq'), may hold values from -6 to 6
- step_index: int32 [64], P('seq'), may hold values from 0 to 15
- modulation: float32 [16, 12288], replicated, may hold values from -3 to 3
- qkv_weight: bfloat16 [2048, 3, 1024], P(None, None, 'ffn'), may hold values from -0.125 to 0.125
- qk_gain: float32 [2, 128], replicated, may hold values from 0.5 to 2
- out_weight: bfloat16 [1024, 2048], P('ffn'), may hold values from -0.1875 to 0.1875
- router_weight: bfloat16 [2048, 64], replicated, may hold values from -0.125 to 0.125
- expert_up: bfloat16 [64, 2048, 2048], P('seq', None, 'ffn'), may hold values from -0.125 to 0.125
- expert_down: bfloat16 [64, 2048, 2048], P('seq', 'ffn'), may hold values from -0.125 to 0.125
- picks: int32 [64, 64, 16], P(None, 'seq'), may hold values from 0 to 511, as said below
- counts: int32 [64, 64], P(None, 'seq'), may hold values from 0 to 16, as said below
Outputs:
- block_out: bfloat16 [64, 512, 2048], P('seq', 'ffn')
The draws below stay inside these ranges and needn't reach their ends.
Inputs may be any that keep to these rules, and one draw needn't show every extreme that they name: picks and counts are the output of an upstream expert-choice router, with a capacity of 16 tokens per expert and frame shard. For j below counts[e, s] the entries picks[e, s, j] are distinct token numbers of shard s; later entries are filler token numbers. `counts`: some expert has 16 valid slots from every shard.
All inputs are finite; a program needn't handle non-finite values.
Results may differ from the reference program's by a relative error of at most 0.012.
Values may be sent and summed in bfloat16 or wider, within the bound.
No kernel may reach another device: no remote copies, remote signals or barrier semaphores. Data moves between devices by JAX's collectives and lax.ppermute only.
A program may use at most 128 MiB of HBM per device.

```python
import math
import jax
import jax.numpy as jnp
from jax import lax

D = 2048
HEADS = 8
HD = 128
HID = 2048
STEPS = 16
SLOT = 16
FRAMES = 64
POS = 512
TOK_SRC = 512
EXPERTS = 64
SOURCES = 64


def draw_picks(key, part):
    key = jax.random.fold_in(key, 11)
    many = jax.random.split(key, EXPERTS * SOURCES)
    orders = jax.vmap(lambda single: jax.random.permutation(single, TOK_SRC))(many)
    return orders[:, :SLOT].reshape(EXPERTS, SOURCES, SLOT).astype(jnp.int32)


def draw_counts(key, part):
    key = jax.random.fold_in(key, 23)
    first, second = jax.random.split(key)
    base = jax.random.randint(first, (EXPERTS, SOURCES), 0, SLOT + 1)
    busiest = jax.random.randint(second, (), 0, EXPERTS)
    rows = jnp.arange(EXPERTS, dtype=jnp.int32)[:, None]
    return jnp.where(rows == busiest, SLOT, base).astype(jnp.int32)


def plant(values, stream_key, smallest, top_value):
    place = [jax.random.randint(jax.random.fold_in(stream_key, axis), (), 0, length) for axis, length in enumerate(values.shape)]
    main_axis = values.shape.index(max(values.shape))
    next_to = place[:main_axis] + [(place[main_axis] + 1) % values.shape[main_axis]] + place[main_axis + 1:]
    return values.at[tuple(place)].set(smallest).at[tuple(next_to)].set(top_value)


def block_levels(key, shape, pieces, least, high):
    factor_of = 1.0
    for position, shards_of in pieces:
        steps = jax.random.uniform(jax.random.fold_in(jax.random.fold_in(key, 6), position), (shards_of,), jnp.float32, least / len(pieces), high / len(pieces))
        factor_of = factor_of * jnp.repeat(jnp.exp(steps), shape[position] // shards_of).reshape((-1,) + (1,) * (len(shape) - 1 - position))
    return factor_of


def noise(own_key, dims, deviation, reach, cuts=(), kind=jnp.bfloat16):
    result = jax.random.normal(own_key, dims, jnp.float32) * deviation
    if len(cuts) > 0:
        result = block_levels(own_key, dims, cuts, -0.22, 0.18) * result
    return jnp.clip(result, min=-reach, max=reach).astype(kind)


def setup_inputs(seed: int = 0) -> dict:
    streams_of = jax.random.split(jax.random.key(seed), 12)
    return {
        "frames_in": noise(streams_of[0], (FRAMES, POS, D), 1.0, 6.0, ((0, 64),)),
        "step_index": plant(jax.random.randint(streams_of[1], (FRAMES,), 0, STEPS), jax.random.fold_in(streams_of[1], 1), 0, STEPS - 1).astype(jnp.int32),
        "modulation": noise(streams_of[2], (STEPS, 6 * D), 0.5, 3.0, (), jnp.float32),
        "qkv_weight": noise(streams_of[3], (D, 3, HEADS * HD), D ** -0.5, 0.125, ((2, 4),)),
        "qk_gain": jnp.clip(jnp.exp(jax.random.uniform(streams_of[4], (2, HD), jnp.float32, math.log(0.5), math.log(2.0))), 0.5, 2.0),
        "out_weight": noise(streams_of[5], (HEADS * HD, D), (HEADS * HD) ** -0.5, 0.1875, ((0, 4),)),
        "router_weight": noise(streams_of[6], (D, EXPERTS), D ** -0.5, 0.125),
        "expert_up": noise(streams_of[7], (EXPERTS, D, HID), D ** -0.5, 0.125, ((0, 64), (2, 4))),
        "expert_down": noise(streams_of[8], (EXPERTS, HID, D), HID ** -0.5, 0.125, ((0, 64), (1, 4))),
        "picks": draw_picks(jax.random.fold_in(streams_of[11], 71), 0),
        "counts": draw_counts(jax.random.fold_in(streams_of[11], 71), 0),
    }


def layer_norm(values):
    mean = lax.optimization_barrier(jnp.mean(values, -1, keepdims=True))
    centred = values - mean
    variance = lax.optimization_barrier(jnp.mean(centred * centred, -1, keepdims=True))
    return centred * lax.rsqrt(variance + 1e-06)

def rms_scale(values, gain):
    return values * lax.rsqrt(lax.optimization_barrier(jnp.mean(values * values, -1, keepdims=True)) + 1e-06) * gain

def reference(frames_in, step_index, modulation, qkv_weight, qk_gain, out_weight, router_weight, expert_up, expert_down, picks, counts):
    frame_count, position_count, model_width = frames_in.shape
    head_size = qk_gain.shape[1]
    inner = qkv_weight.shape[2]
    head_count = inner // head_size
    table = modulation[step_index].reshape(frame_count, 6, model_width)
    shift_one = table[:, 0][:, None]
    scale_one = table[:, 1][:, None]
    gate_one = table[:, 2][:, None]
    shift_two = table[:, 3][:, None]
    scale_two = table[:, 4][:, None]
    gate_two = table[:, 5][:, None]
    source = frames_in.astype(jnp.float32)
    normed_one = (layer_norm(source) * (1.0 + scale_one) + shift_one).astype(jnp.bfloat16)
    projected = jnp.dot(normed_one.reshape(-1, model_width), qkv_weight.reshape(model_width, -1), preferred_element_type=jnp.float32)
    projected = projected.reshape(frame_count, position_count, 3, head_count, head_size)
    queries = rms_scale(projected[:, :, 0], qk_gain[0]).astype(jnp.bfloat16)
    keys = rms_scale(projected[:, :, 1], qk_gain[1]).astype(jnp.bfloat16)
    values = projected[:, :, 2].astype(jnp.bfloat16)
    scores = jnp.einsum('fphd,gphd->phfg', queries.astype(jnp.float32), keys.astype(jnp.float32)) * head_size ** (-0.5)
    raised = jnp.exp(scores)
    probs = (raised / lax.optimization_barrier(jnp.sum(raised, -1, keepdims=True))).astype(jnp.bfloat16)
    attended = jnp.einsum('phfg,gphd->fphd', probs.astype(jnp.float32), values.astype(jnp.float32)).astype(jnp.bfloat16)
    mixed = jnp.dot(attended.reshape(-1, inner), out_weight, preferred_element_type=jnp.float32)
    hidden_state = source + gate_one * mixed.reshape(frame_count, position_count, model_width)
    normed_two = (layer_norm(hidden_state) * (1.0 + scale_two) + shift_two).astype(jnp.bfloat16)
    tokens = normed_two.reshape(-1, model_width)
    gates = jax.nn.sigmoid(jnp.dot(tokens, router_weight, preferred_element_type=jnp.float32))
    expert_count, source_count, slot_count = picks.shape
    tok_src = frame_count * position_count // source_count
    offsets = (jnp.arange(source_count, dtype=jnp.int32) * tok_src).astype(jnp.int32)
    global_picks = (picks + offsets[None, :, None]).astype(jnp.int32).reshape(expert_count, -1)
    live = (jnp.arange(slot_count, dtype=jnp.int32)[None, None, :] < counts[:, :, None]).reshape(expert_count, -1)

    def one_expert(total, inputs):
        index_row, live_row, up_matrix, down_matrix, gate_column = inputs
        rows = tokens[index_row]
        expert_hidden = jax.nn.gelu(jnp.dot(rows, up_matrix, preferred_element_type=jnp.float32)).astype(jnp.bfloat16)
        expert_result = jnp.dot(expert_hidden, down_matrix, preferred_element_type=jnp.float32)
        weight = jnp.where(live_row, gate_column[index_row], jnp.zeros((), jnp.float32))
        return (total.at[index_row].add(weight[:, None] * expert_result), None)
    start = jnp.zeros((tokens.shape[0], model_width), jnp.float32)
    mixture, unused = lax.scan(one_expert, start, (global_picks, live, expert_up, expert_down, gates.T))
    block_out = hidden_state + gate_two * mixture.reshape(frame_count, position_count, model_width)
    return block_out.astype(jnp.bfloat16)
```

```python
import functools

import jax
import jax.numpy as jnp
from jax import lax
from jax.experimental import pallas as pl
from jax.experimental.pallas import tpu as pltpu
from jax.sharding import PartitionSpec as P

BF16 = jnp.bfloat16
F32 = jnp.float32
MIB = 1 << 20


def dot(a, b):
    return jnp.dot(a, b, preferred_element_type=F32)


def dot_t(a, b):
    return lax.dot_general(a, b, (((1,), (1,)), ((), ())), preferred_element_type=F32)


def dot_l(a, b):
    return lax.dot_general(a, b, (((0,), (0,)), ((), ())), preferred_element_type=F32)


def layer_norm(values):
    mean = jnp.mean(values, -1, keepdims=True)
    centred = values - mean
    variance = jnp.mean(centred * centred, -1, keepdims=True)
    return centred * lax.rsqrt(variance + 1e-06)


def smem():
    return pl.BlockSpec(memory_space=pltpu.SMEM)


def params(mib, **kw):
    return pltpu.CompilerParams(vmem_limit_bytes=mib * MIB, **kw)


def qkv_kernel(step_ref, x_ref, mod_ref, w_ref, gain_ref, out_ref):
    step = step_ref[0]
    width = x_ref.shape[1]
    shift = mod_ref[pl.ds(step, 1), :width]
    scale = mod_ref[pl.ds(step, 1), width:]
    normed = (layer_norm(x_ref[...].astype(F32)) * (1.0 + scale) + shift).astype(BF16)
    inner = w_ref.shape[2]
    head = gain_ref.shape[1]
    for part in range(3):
        proj = dot(normed, w_ref[part])
        if part < 2:
            gain = gain_ref[part : part + 1, :]
            for h in range(inner // head):
                one = proj[:, h * head : (h + 1) * head]
                one = one * lax.rsqrt(jnp.mean(one * one, -1, keepdims=True) + 1e-06) * gain
                lo = part * inner + h * head
                out_ref[:, lo : lo + head] = one.astype(BF16)
        else:
            out_ref[:, part * inner : (part + 1) * inner] = proj.astype(BF16)


def qkv_call(step, x, modulation, w, gain):
    tokens, width = x.shape
    inner = w.shape[2]
    rows = 256
    return pl.pallas_call(
        qkv_kernel,
        grid=(tokens // rows,),
        in_specs=[
            smem(),
            pl.BlockSpec((rows, width), lambda i: (i, 0)),
            pl.BlockSpec((modulation.shape[0], 2 * width), lambda i: (0, 0)),
            pl.BlockSpec(w.shape, lambda i: (0, 0, 0)),
            pl.BlockSpec(gain.shape, lambda i: (0, 0)),
        ],
        out_specs=pl.BlockSpec((rows, 3 * inner), lambda i: (i, 0)),
        out_shape=jax.ShapeDtypeStruct((tokens, 3 * inner), BF16),
        compiler_params=params(40),
        name="qkv",
    )(step, x, modulation, w, gain)


def attention_kernel(few, head, in_ref, out_ref):
    rows = in_ref.shape[0]
    inner = out_ref.shape[1]
    row_pos = lax.broadcasted_iota(jnp.int32, (rows, rows), 0) % few
    col_pos = lax.broadcasted_iota(jnp.int32, (rows, rows), 1) % few
    same = row_pos == col_pos
    for h in range(inner // head):
        lo = h * head
        q = in_ref[:, lo : lo + head]
        k = in_ref[:, inner + lo : inner + lo + head]
        v = in_ref[:, 2 * inner + lo : 2 * inner + lo + head]
        raised = jnp.where(same, jnp.exp(dot_t(q, k) * head ** (-0.5)), 0.0)
        probs = (raised / jnp.sum(raised, -1, keepdims=True)).astype(BF16)
        out_ref[:, lo : lo + head] = dot(probs, v).astype(BF16)


def attention_call(stacked, few, head):
    rows, wide = stacked.shape
    return pl.pallas_call(
        functools.partial(attention_kernel, few, head),
        out_shape=jax.ShapeDtypeStruct((rows, wide // 3), BF16),
        compiler_params=params(40),
        name="attention",
    )(stacked)


def spread(values, per):
    experts = values.shape[1]
    shape = (experts, experts * per)
    expand = (
        lax.broadcasted_iota(jnp.int32, shape, 1) // per
        == lax.broadcasted_iota(jnp.int32, shape, 0)
    ).astype(F32)
    return jnp.dot(values, expand, precision=lax.Precision.HIGHEST, preferred_element_type=F32)


def slot_row(picks_f32, counts_f32, first, per):
    wide = spread(picks_f32, per)
    slot = lax.broadcasted_iota(jnp.int32, wide.shape, 0)
    wanted = first + lax.broadcasted_iota(jnp.int32, wide.shape, 1) % per
    mine = slot == wanted
    if counts_f32 is not None:
        limit = spread(counts_f32, per)
        wide = jnp.where(slot.astype(F32) < limit, wide, -1.0)
    return jnp.sum(jnp.where(mine, wide, 0.0), axis=0, keepdims=True).astype(jnp.int32)


def mix_kernel(
    per, rank_ref, step_ref, att_ref, w_ref, x_ref, gate_ref, shift_ref, scale_ref,
    router_ref, picks_ref, disp_ref, gates_ref, share_ref, hidden_ref, normed_ref,
):
    step = step_ref[0]
    rank = rank_ref[0]
    tile = pl.program_id(0)
    rows = x_ref.shape[0]
    gate = gate_ref[pl.ds(step, 1), :]
    shift = shift_ref[pl.ds(step, 1), :]
    scale = scale_ref[pl.ds(step, 1), :]
    parts = att_ref.shape[0]
    inner = att_ref.shape[2]
    mixed = dot(att_ref[0], w_ref[:inner])
    for part in range(1, parts):
        mixed += dot(att_ref[part], w_ref[part * inner : (part + 1) * inner])
    hidden = x_ref[...].astype(F32) + gate * mixed
    hidden_ref[...] = hidden
    normed = (layer_norm(hidden) * (1.0 + scale) + shift).astype(BF16)
    normed_ref[pl.ds(pl.multiple_of(tile * rows, rows), rows), :] = normed
    gates_ref[...] = jax.nn.sigmoid(dot_t(normed, router_ref[...]))
    share = share_ref.shape[0]
    each = rows // share

    @pl.when(tile == rank // each)
    def _():
        start = pl.multiple_of((rank % each) * share, share)
        share_ref[...] = hidden_ref[pl.ds(start, share), :]

    @pl.when(tile == pl.num_programs(0) - 1)
    def _():
        row = slot_row(picks_ref[...].astype(F32), None, rank * per, per)
        tokens = normed_ref.shape[0]
        shape = (tokens, row.shape[1])
        onehot = (lax.broadcasted_iota(jnp.int32, shape, 0) == row).astype(F32).astype(BF16)
        disp_ref[...] = dot_l(onehot, normed_ref[...]).astype(BF16)


def mix_call(rank, step, att, w, x, modulation, router_t, picks_t, per, share):
    tokens, width = x.shape
    parts, _, inner = att.shape
    experts = router_t.shape[0]
    steps = modulation.shape[0]
    rows = 256
    return pl.pallas_call(
        functools.partial(mix_kernel, per),
        grid=(tokens // rows,),
        in_specs=[
            smem(),
            smem(),
            pl.BlockSpec((parts, rows, inner), lambda i: (0, i, 0)),
            pl.BlockSpec(w.shape, lambda i: (0, 0)),
            pl.BlockSpec((rows, width), lambda i: (i, 0)),
            pl.BlockSpec((steps, width), lambda i: (0, 2)),
            pl.BlockSpec((steps, width), lambda i: (0, 3)),
            pl.BlockSpec((steps, width), lambda i: (0, 4)),
            pl.BlockSpec(router_t.shape, lambda i: (0, 0)),
            pl.BlockSpec(picks_t.shape, lambda i: (0, 0)),
        ],
        out_specs=[
            pl.BlockSpec((experts * per, width), lambda i: (0, 0)),
            pl.BlockSpec((rows, experts), lambda i: (i, 0)),
            pl.BlockSpec((share, width), lambda i: (0, 0)),
        ],
        out_shape=[
            jax.ShapeDtypeStruct((experts * per, width), BF16),
            jax.ShapeDtypeStruct((tokens, experts), F32),
            jax.ShapeDtypeStruct((share, width), F32),
        ],
        scratch_shapes=[pltpu.VMEM((rows, width), F32), pltpu.VMEM((tokens, width), BF16)],
        compiler_params=params(44),
        name="mix",
    )(rank, step, att, w, x, modulation, modulation, modulation, router_t, picks_t)


def up_kernel(tok_ref, w_ref, out_ref):
    out_ref[...] = jax.nn.gelu(dot(tok_ref[...], w_ref[0])).astype(BF16)


def up_call(tokens, w):
    rows, width = tokens.shape
    parts, _, units = w.shape
    return pl.pallas_call(
        up_kernel,
        grid=(parts,),
        in_specs=[
            pl.BlockSpec((rows, width), lambda i: (0, 0)),
            pl.BlockSpec((1, width, units), lambda i: (i, 0, 0)),
        ],
        out_specs=pl.BlockSpec((rows, units), lambda i: (0, i)),
        out_shape=jax.ShapeDtypeStruct((rows, parts * units), BF16),
        compiler_params=params(40),
        name="up",
    )(tokens, w)


def down_kernel(rank_ref, hid_ref, *refs):
    out_ref = refs[-1]
    blocks = refs[:-1]
    units = blocks[0].shape[0]
    total = None
    for turn, block in enumerate(blocks):
        at = lax.rem(rank_ref[0] + turn, len(blocks))
        some = hid_ref[:, pl.ds(pl.multiple_of(at * units, units), units)]
        term = dot(some, block[...])
        total = term if total is None else total + term
    out_ref[...] = total.astype(BF16)


def down_call(rank, hidden, blocks):
    rows, units = hidden.shape
    few, half = blocks[0].shape
    cols = 512
    return pl.pallas_call(
        down_kernel,
        grid=(half // cols,),
        in_specs=[smem(), pl.BlockSpec((rows, units), lambda i: (0, 0))]
        + [pl.BlockSpec((few, cols), lambda i: (0, i))] * len(blocks),
        out_specs=pl.BlockSpec((rows, cols), lambda i: (0, i)),
        out_shape=jax.ShapeDtypeStruct((rows, half), BF16),
        compiler_params=params(40),
        name="down",
    )(rank, hidden, *blocks)


def combine_kernel(per, rank_ref, gates_ref, picks_ref, counts_ref, own_ref, other_ref, out_ref):
    rank = rank_ref[0]
    tokens = gates_ref.shape[0]
    experts = gates_ref.shape[1]
    picks = picks_ref[...].astype(F32)
    counts = counts_ref[...].astype(F32)
    shape = (experts, experts * per)
    expand = (
        lax.broadcasted_iota(jnp.int32, shape, 1) // per
        == lax.broadcasted_iota(jnp.int32, shape, 0)
    ).astype(F32).astype(BF16)
    wide = dot(gates_ref[...].astype(BF16), expand)
    token = lax.broadcasted_iota(jnp.int32, (tokens, experts * per), 0)
    partner = rank + 1 - 2 * lax.rem(rank, 2)
    weights = []
    for who in (rank, partner):
        row = slot_row(picks, counts, who * per, per)
        weights.append(jnp.where(token == row, wide, 0.0).astype(BF16))
    out_ref[...] = (dot(weights[0], own_ref[...]) + dot(weights[1], other_ref[...])).astype(BF16)


def combine_call(rank, gates, picks_t, counts_t, own, other, per):
    half = own.shape[1]
    vmem = pl.BlockSpec(memory_space=pltpu.VMEM)
    return pl.pallas_call(
        functools.partial(combine_kernel, per),
        in_specs=[smem()] + [vmem] * 5,
        out_specs=vmem,
        out_shape=jax.ShapeDtypeStruct((gates.shape[0], half), BF16),
        compiler_params=params(40),
        name="combine",
    )(rank, gates, picks_t, counts_t, own, other)


def final_kernel(step_ref, share_ref, gate_ref, parts_ref, out_ref):
    gate = gate_ref[pl.ds(step_ref[0], 1), :]
    half = parts_ref.shape[2]
    for b in range(2):
        cols = slice(b * half, (b + 1) * half)
        mixture = parts_ref[b].astype(F32) + parts_ref[b + 2].astype(F32)
        out_ref[:, cols] = (share_ref[:, cols] + gate[:, cols] * mixture).astype(BF16)


def final_call(step, share, modulation, parts):
    rows, width = share.shape
    return pl.pallas_call(
        final_kernel,
        grid=(1,),
        in_specs=[
            smem(),
            pl.BlockSpec((rows, width), lambda i: (0, 0)),
            pl.BlockSpec((modulation.shape[0], width), lambda i: (0, 5)),
            pl.BlockSpec(parts.shape, lambda i: (0, 0, 0)),
        ],
        out_specs=pl.BlockSpec((rows, width), lambda i: (0, 0)),
        out_shape=jax.ShapeDtypeStruct((rows, width), BF16),
        compiler_params=params(40),
        name="final",
    )(step, share, modulation, parts)


def on_device(
    frames_in,
    step_index,
    modulation,
    qkv_weight,
    qk_gain,
    out_weight,
    router_weight,
    expert_up,
    expert_down,
    picks,
    counts,
):
    _, position_count, model_width = frames_in.shape
    ffn = lax.axis_size("ffn")
    seq = lax.axis_size("seq")
    rank = lax.axis_index("ffn").astype(jnp.int32)
    rank_arr = rank.reshape(1)
    head_size = qk_gain.shape[1]
    share_len = position_count // ffn
    slot_count = picks.shape[2]
    per = slot_count // ffn
    half = model_width // 2
    x = frames_in[0]
    picks_t = jnp.transpose(picks, (1, 2, 0))[0]
    counts_t = jnp.transpose(counts, (1, 0))

    def over_seq(values):
        return lax.all_to_all(values, "seq", split_axis=0, concat_axis=0, tiled=True)

    def over_ffn(values):
        return lax.all_to_all(values, "ffn", split_axis=0, concat_axis=0, tiled=True)

    out_full = lax.all_gather(out_weight, "ffn", axis=0, tiled=True)
    up_full = lax.all_gather(expert_up, "ffn", axis=0, tiled=True)
    down = expert_down[0]
    side = lax.rem(rank, 2)
    same_half = lax.dynamic_slice_in_dim(down, side * half, half, 1)
    other_half = lax.dynamic_slice_in_dim(down, (1 - side) * half, half, 1)

    def from_turn(values, turn):
        return lax.ppermute(values, "ffn", [((i + turn) % ffn, i) for i in range(ffn)])

    blocks = [
        same_half,
        from_turn(other_half, 1),
        from_turn(same_half, 2),
        from_turn(other_half, 3),
    ]

    stacked = qkv_call(step_index, x, modulation, jnp.transpose(qkv_weight, (1, 0, 2)), qk_gain)
    stacked = over_seq(stacked)
    attended = attention_call(stacked, position_count // seq, head_size)
    attended = over_seq(attended)
    every = over_ffn(jnp.broadcast_to(attended[None], (ffn,) + attended.shape))
    outgoing, gates, share = mix_call(
        rank_arr, step_index, every, out_full, x, modulation,
        jnp.transpose(router_weight, (1, 0)), picks_t, per, share_len,
    )
    expert_tokens = over_seq(outgoing)
    hidden = up_call(expert_tokens, up_full)
    hidden_other = lax.ppermute(hidden, "ffn", [(i, i ^ 1) for i in range(ffn)])
    own = over_seq(down_call(rank_arr, hidden, blocks))
    other = over_seq(down_call(rank_arr, hidden_other, blocks))
    mixture = combine_call(rank_arr, gates, picks_t, counts_t, own, other, per)
    parts = over_ffn(mixture).reshape(ffn, share_len, half)
    return final_call(step_index, share, modulation, parts)[None]


def solution(mesh):
    in_specs = (
        P("seq", None, None),
        P("seq"),
        P(),
        P(None, None, "ffn"),
        P(),
        P("ffn", None),
        P(),
        P("seq", None, "ffn"),
        P("seq", "ffn", None),
        P(None, "seq", None),
        P(None, "seq"),
    )
    out_specs = P("seq", "ffn", None)
    return jax.shard_map(
        on_device, mesh=mesh, in_specs=in_specs, out_specs=out_specs, check_vma=False
    )
```

```python
import functools

import jax
import jax.numpy as jnp
from jax import lax
from jax.experimental import pallas as pl
from jax.experimental.pallas import tpu as pltpu
from jax.sharding import PartitionSpec as P

BF16 = jnp.bfloat16
F32 = jnp.float32
MIB = 1 << 20


def dot(a, b):
    return jnp.dot(a, b, preferred_element_type=F32)


def dot_t(a, b):
    return lax.dot_general(a, b, (((1,), (1,)), ((), ())), preferred_element_type=F32)


def dot_l(a, b):
    return lax.dot_general(a, b, (((0,), (0,)), ((), ())), preferred_element_type=F32)


def layer_norm(values):
    mean = jnp.mean(values, -1, keepdims=True)
    centred = values - mean
    variance = jnp.mean(centred * centred, -1, keepdims=True)
    return centred * lax.rsqrt(variance + 1e-06)


def smem():
    return pl.BlockSpec(memory_space=pltpu.SMEM)


def params(mib, **kw):
    return pltpu.CompilerParams(vmem_limit_bytes=mib * MIB, **kw)


def qkv_kernel(step_ref, x_ref, mod_ref, w_ref, gain_ref, out_ref):
    step = step_ref[0]
    width = x_ref.shape[1]
    shift = mod_ref[pl.ds(step, 1), :width]
    scale = mod_ref[pl.ds(step, 1), width:]
    normed = (layer_norm(x_ref[...].astype(F32)) * (1.0 + scale) + shift).astype(BF16)
    inner = w_ref.shape[2]
    head = gain_ref.shape[1]
    for part in range(3):
        proj = dot(normed, w_ref[part])
        if part < 2:
            gain = gain_ref[part : part + 1, :]
            for h in range(inner // head):
                one = proj[:, h * head : (h + 1) * head]
                one = one * lax.rsqrt(jnp.mean(one * one, -1, keepdims=True) + 1e-06) * gain
                lo = part * inner + h * head
                out_ref[:, lo : lo + head] = one.astype(BF16)
        else:
            out_ref[:, part * inner : (part + 1) * inner] = proj.astype(BF16)


def qkv_call(step, x, modulation, w, gain):
    tokens, width = x.shape
    inner = w.shape[2]
    rows = 256
    return pl.pallas_call(
        qkv_kernel,
        grid=(tokens // rows,),
        in_specs=[
            smem(),
            pl.BlockSpec((rows, width), lambda i: (i, 0)),
            pl.BlockSpec((modulation.shape[0], 2 * width), lambda i: (0, 0)),
            pl.BlockSpec(w.shape, lambda i: (0, 0, 0)),
            pl.BlockSpec(gain.shape, lambda i: (0, 0)),
        ],
        out_specs=pl.BlockSpec((rows, 3 * inner), lambda i: (i, 0)),
        out_shape=jax.ShapeDtypeStruct((tokens, 3 * inner), BF16),
        compiler_params=params(56),
        name="qkv",
    )(step, x, modulation, w, gain)


def attention_kernel(few, head, in_ref, out_ref):
    rows = in_ref.shape[0]
    inner = out_ref.shape[1]
    row_pos = lax.broadcasted_iota(jnp.int32, (rows, rows), 0) % few
    col_pos = lax.broadcasted_iota(jnp.int32, (rows, rows), 1) % few
    same = row_pos == col_pos
    for h in range(inner // head):
        lo = h * head
        q = in_ref[:, lo : lo + head]
        k = in_ref[:, inner + lo : inner + lo + head]
        v = in_ref[:, 2 * inner + lo : 2 * inner + lo + head]
        raised = jnp.where(same, jnp.exp(dot_t(q, k) * head ** (-0.5)), 0.0)
        probs = (raised / jnp.sum(raised, -1, keepdims=True)).astype(BF16)
        out_ref[:, lo : lo + head] = dot(probs, v).astype(BF16)


def attention_call(stacked, few, head):
    rows, wide = stacked.shape
    return pl.pallas_call(
        functools.partial(attention_kernel, few, head),
        out_shape=jax.ShapeDtypeStruct((rows, wide // 3), BF16),
        compiler_params=params(16),
        name="attention",
    )(stacked)


def spread(values, per):
    experts = values.shape[1]
    shape = (experts, experts * per)
    expand = (
        lax.broadcasted_iota(jnp.int32, shape, 1) // per
        == lax.broadcasted_iota(jnp.int32, shape, 0)
    ).astype(F32)
    return jnp.dot(values, expand, precision=lax.Precision.HIGHEST, preferred_element_type=F32)


def slot_row(picks_f32, counts_f32, first, per):
    wide = spread(picks_f32, 2 * per)
    slot = lax.broadcasted_iota(jnp.int32, wide.shape, 0)
    wanted = first + lax.broadcasted_iota(jnp.int32, wide.shape, 1) % per
    mine = slot == wanted
    if counts_f32 is not None:
        limit = spread(counts_f32, 2 * per)
        wide = jnp.where(slot.astype(F32) < limit, wide, -1.0)
    return jnp.sum(jnp.where(mine, wide, 0.0), axis=0, keepdims=True).astype(jnp.int32)


def row_half(shape, per, dim):
    return (lax.broadcasted_iota(jnp.int32, shape, dim) // per) % 2


def ones_where(mask):
    return mask.astype(F32).astype(BF16)


def halves_to_rows(count, per, half):
    shape = (2 * count, count)
    row = lax.broadcasted_iota(jnp.int32, shape, 0)
    col = lax.broadcasted_iota(jnp.int32, shape, 1)
    return ones_where(row == (col // per * 2 + half) * per + col % per)


def mix_kernel(
    per, rank_ref, core_ref, step_ref, att_ref, *refs
):
    weights = refs[:8]
    (x_ref, gate_ref, shift_ref, scale_ref, router_ref, picks_ref,
     disp_ref, gates_ref, share_ref, hidden_ref, normed_ref) = refs[8:]
    step = step_ref[0]
    rank = rank_ref[0]
    tile = pl.program_id(0)
    rows = x_ref.shape[0]
    gate = gate_ref[pl.ds(step, 1), :]
    shift = shift_ref[pl.ds(step, 1), :]
    scale = scale_ref[pl.ds(step, 1), :]
    parts = att_ref.shape[0]
    some = att_ref.shape[2] // 2
    core = core_ref[0]
    mixed = None
    for turn in range(parts):
        part = lax.rem(rank + turn, parts)
        for which in range(2):
            at = lax.rem(core + which, 2) * some
            rows_of = att_ref[part, :, pl.ds(pl.multiple_of(at, some), some)]
            term = dot(rows_of, weights[which * parts + turn][...])
            mixed = term if mixed is None else mixed + term
    hidden = x_ref[...].astype(F32) + gate * mixed
    hidden_ref[...] = hidden
    normed = (layer_norm(hidden) * (1.0 + scale) + shift).astype(BF16)
    normed_ref[pl.ds(pl.multiple_of(tile * rows, rows), rows), :] = normed
    gates_ref[...] = jax.nn.sigmoid(dot_t(normed, router_ref[...]))
    share = share_ref.shape[0]
    each = rows // share

    @pl.when(tile == rank // each)
    def _():
        start = pl.multiple_of((rank % each) * share, share)
        share_ref[...] = hidden_ref[pl.ds(start, share), :]

    @pl.when(tile == pl.num_programs(0) - 1)
    def _():
        row = slot_row(picks_ref[...].astype(F32), None, rank * per, per)
        tokens = normed_ref.shape[0]
        shape = (tokens, row.shape[1])
        picked = lax.broadcasted_iota(jnp.int32, shape, 0) == row
        half = row_half(shape, per, 1)
        cols = disp_ref.shape[1]
        disp_ref[...] = (
            dot_l(ones_where(picked & (half == 0)), normed_ref[:, :cols])
            + dot_l(ones_where(picked & (half == 1)), normed_ref[:, cols:])
        ).astype(BF16)


def mix_call(rank, core, step, att, weights, x, modulation, router_t, picks_t, per, share):
    tokens, width = x.shape
    parts, _, inner = att.shape
    experts = router_t.shape[0]
    steps = modulation.shape[0]
    rows = 256
    return pl.pallas_call(
        functools.partial(mix_kernel, per),
        grid=(tokens // rows,),
        in_specs=[
            smem(),
            smem(),
            smem(),
            pl.BlockSpec((parts, rows, inner), lambda i: (0, i, 0)),
        ]
        + [pl.BlockSpec(w.shape, lambda i: (0, 0)) for w in weights]
        + [
            pl.BlockSpec((rows, width), lambda i: (i, 0)),
            pl.BlockSpec((steps, width), lambda i: (0, 2)),
            pl.BlockSpec((steps, width), lambda i: (0, 3)),
            pl.BlockSpec((steps, width), lambda i: (0, 4)),
            pl.BlockSpec(router_t.shape, lambda i: (0, 0)),
            pl.BlockSpec(picks_t.shape, lambda i: (0, 0)),
        ],
        out_specs=[
            pl.BlockSpec((2 * experts * per, width // 2), lambda i: (0, 0)),
            pl.BlockSpec((rows, experts), lambda i: (i, 0)),
            pl.BlockSpec((share, width), lambda i: (0, 0)),
        ],
        out_shape=[
            jax.ShapeDtypeStruct((2 * experts * per, width // 2), BF16),
            jax.ShapeDtypeStruct((tokens, experts), F32),
            jax.ShapeDtypeStruct((share, width), F32),
        ],
        scratch_shapes=[pltpu.VMEM((rows, width), F32), pltpu.VMEM((tokens, width), BF16)],
        compiler_params=params(56),
        name="mix",
    )(rank, core, step, att, *weights, x, modulation, modulation, modulation, router_t, picks_t)


def up_kernel(per, rows_ref, w_ref, out_ref, tok_ref):
    @pl.when(pl.program_id(0) == 0)
    def _():
        count = tok_ref.shape[0]
        cols = rows_ref.shape[1]
        for half in range(2):
            pick = halves_to_rows(count, per, half)
            tok_ref[:, half * cols : (half + 1) * cols] = dot_l(pick, rows_ref[...]).astype(BF16)

    out_ref[...] = jax.nn.gelu(dot(tok_ref[...], w_ref[0])).astype(BF16)


def up_call(rows, w, per):
    parts, width, units = w.shape
    count = rows.shape[0] // 2
    return pl.pallas_call(
        functools.partial(up_kernel, per),
        grid=(parts,),
        in_specs=[
            pl.BlockSpec(rows.shape, lambda i: (0, 0)),
            pl.BlockSpec((1, width, units), lambda i: (i, 0, 0)),
        ],
        out_specs=pl.BlockSpec((count, units), lambda i: (0, i)),
        out_shape=jax.ShapeDtypeStruct((count, parts * units), BF16),
        scratch_shapes=[pltpu.VMEM((count, width), BF16)],
        compiler_params=params(56),
        name="up",
    )(rows, w)


def down_kernel(per, rank_ref, hid_ref, *refs):
    out_ref = refs[-1]
    blocks = refs[:-1]
    units = blocks[0].shape[0]
    total = None
    for turn, block in enumerate(blocks):
        at = lax.rem(rank_ref[0] + turn, len(blocks))
        some = hid_ref[:, pl.ds(pl.multiple_of(at * units, units), units)]
        term = dot(some, block[...])
        total = term if total is None else total + term
    total = total.astype(BF16)
    count = total.shape[0]

    @pl.when(pl.program_id(0) == 0)
    def _():
        out_ref[...] = dot(halves_to_rows(count, per, 0), total).astype(BF16)

    @pl.when(pl.program_id(0) == 1)
    def _():
        out_ref[...] += dot(halves_to_rows(count, per, 1), total).astype(BF16)


def down_call(rank, hidden, blocks, per):
    rows, units = hidden.shape
    few, half = blocks[0].shape
    cols = half // 2
    return pl.pallas_call(
        functools.partial(down_kernel, per),
        grid=(2,),
        in_specs=[smem(), pl.BlockSpec((rows, units), lambda i: (0, 0))]
        + [pl.BlockSpec((few, cols), lambda i: (0, i))] * len(blocks),
        out_specs=pl.BlockSpec((2 * rows, cols), lambda i: (0, 0)),
        out_shape=jax.ShapeDtypeStruct((2 * rows, cols), BF16),
        compiler_params=params(56),
        name="down",
    )(rank, hidden, *blocks)


def combine_kernel(per, rank_ref, gates_ref, picks_ref, counts_ref, own_ref, other_ref, out_ref):
    rank = rank_ref[0]
    tokens = gates_ref.shape[0]
    experts = gates_ref.shape[1]
    picks = picks_ref[...].astype(F32)
    counts = counts_ref[...].astype(F32)
    shape = (experts, 2 * experts * per)
    expand = ones_where(
        lax.broadcasted_iota(jnp.int32, shape, 1) // (2 * per)
        == lax.broadcasted_iota(jnp.int32, shape, 0)
    )
    wide = dot(gates_ref[...].astype(BF16), expand)
    token = lax.broadcasted_iota(jnp.int32, wide.shape, 0)
    which = row_half(wide.shape, per, 1)
    partner = rank + 1 - 2 * lax.rem(rank, 2)
    cols = own_ref.shape[1]
    sums = [None, None]
    for who, rows_ref in ((rank, own_ref), (partner, other_ref)):
        row = slot_row(picks, counts, who * per, per)
        weight = jnp.where(token == row, wide, 0.0)
        for half in range(2):
            term = dot(jnp.where(which == half, weight, 0.0).astype(BF16), rows_ref[...])
            sums[half] = term if sums[half] is None else sums[half] + term
    for half in range(2):
        out_ref[:, half * cols : (half + 1) * cols] = sums[half].astype(BF16)


def combine_call(rank, gates, picks_t, counts_t, own, other, per):
    half = 2 * own.shape[1]
    vmem = pl.BlockSpec(memory_space=pltpu.VMEM)
    return pl.pallas_call(
        functools.partial(combine_kernel, per),
        in_specs=[smem()] + [vmem] * 5,
        out_specs=vmem,
        out_shape=jax.ShapeDtypeStruct((gates.shape[0], half), BF16),
        compiler_params=params(16),
        name="combine",
    )(rank, gates, picks_t, counts_t, own, other)


def final_kernel(step_ref, share_ref, gate_ref, parts_ref, out_ref):
    gate = gate_ref[pl.ds(step_ref[0], 1), :]
    half = parts_ref.shape[2]
    for b in range(2):
        cols = slice(b * half, (b + 1) * half)
        mixture = parts_ref[b].astype(F32) + parts_ref[b + 2].astype(F32)
        out_ref[:, cols] = (share_ref[:, cols] + gate[:, cols] * mixture).astype(BF16)


def final_call(step, share, modulation, parts):
    rows, width = share.shape
    return pl.pallas_call(
        final_kernel,
        grid=(1,),
        in_specs=[
            smem(),
            pl.BlockSpec((rows, width), lambda i: (0, 0)),
            pl.BlockSpec((modulation.shape[0], width), lambda i: (0, 5)),
            pl.BlockSpec(parts.shape, lambda i: (0, 0, 0)),
        ],
        out_specs=pl.BlockSpec((rows, width), lambda i: (0, 0)),
        out_shape=jax.ShapeDtypeStruct((rows, width), BF16),
        compiler_params=params(16),
        name="final",
    )(step, share, modulation, parts)


def on_device(
    frames_in,
    step_index,
    modulation,
    qkv_weight,
    qk_gain,
    out_weight,
    router_weight,
    expert_up,
    expert_down,
    picks,
    counts,
):
    _, position_count, model_width = frames_in.shape
    ffn = lax.axis_size("ffn")
    seq = lax.axis_size("seq")
    rank = lax.axis_index("ffn").astype(jnp.int32)
    rank_arr = rank.reshape(1)
    head_size = qk_gain.shape[1]
    share_len = position_count // ffn
    slot_count = picks.shape[2]
    per = slot_count // ffn
    half = model_width // 2
    x = frames_in[0]
    picks_t = jnp.transpose(picks, (1, 2, 0))[0]
    counts_t = jnp.transpose(counts, (1, 0))

    def over_seq(values):
        return lax.all_to_all(values, "seq", split_axis=0, concat_axis=0, tiled=True)

    def over_ffn(values):
        return lax.all_to_all(values, "ffn", split_axis=0, concat_axis=0, tiled=True)

    core = lax.rem(lax.axis_index("seq").astype(jnp.int32), 2)
    core_arr = core.reshape(1)
    out_rows = out_weight.shape[0] // 2
    out_own = lax.dynamic_slice_in_dim(out_weight, core * out_rows, out_rows, 0)
    up_full = lax.all_gather(expert_up, "ffn", axis=0, tiled=True)
    down = expert_down[0]
    side = lax.rem(rank, 2)
    same_half = lax.dynamic_slice_in_dim(down, side * half, half, 1)
    other_half = lax.dynamic_slice_in_dim(down, (1 - side) * half, half, 1)

    def from_turn(values, turn):
        return lax.ppermute(values, "ffn", [((i + turn) % ffn, i) for i in range(ffn)])

    out_blocks = [out_own] + [from_turn(out_own, turn) for turn in range(1, ffn)]
    blocks = [
        same_half,
        from_turn(other_half, 1),
        from_turn(same_half, 2),
        from_turn(other_half, 3),
    ]

    stacked = qkv_call(step_index, x, modulation, jnp.transpose(qkv_weight, (1, 0, 2)), qk_gain)
    stacked = over_seq(stacked)
    stacked, out_blocks = lax.optimization_barrier((stacked, out_blocks))
    swap = [(i, i ^ 1) for i in range(seq)]
    out_blocks = out_blocks + [lax.ppermute(b, "seq", swap) for b in out_blocks]
    attended = attention_call(stacked, position_count // seq, head_size)
    attended = over_seq(attended)
    every = over_ffn(jnp.broadcast_to(attended[None], (ffn,) + attended.shape))
    outgoing, gates, share = mix_call(
        rank_arr, core_arr, step_index, every, out_blocks, x, modulation,
        jnp.transpose(router_weight, (1, 0)), picks_t, per, share_len,
    )
    expert_tokens = over_seq(outgoing)
    hidden = up_call(expert_tokens, up_full, per)
    hidden_other = lax.ppermute(hidden, "ffn", [(i, i ^ 1) for i in range(ffn)])
    own = over_seq(down_call(rank_arr, hidden, blocks, per))
    other = over_seq(down_call(rank_arr, hidden_other, blocks, per))
    mixture = combine_call(rank_arr, gates, picks_t, counts_t, own, other, per)
    parts = over_ffn(mixture).reshape(ffn, share_len, half)
    return final_call(step_index, share, modulation, parts)[None]


def solution(mesh):
    in_specs = (
        P("seq", None, None),
        P("seq"),
        P(),
        P(None, None, "ffn"),
        P(),
        P("ffn", None),
        P(),
        P("seq", None, "ffn"),
        P("seq", "ffn", None),
        P(None, "seq", None),
        P(None, "seq"),
    )
    out_specs = P("seq", "ffn", None)
    return jax.shard_map(
        on_device, mesh=mesh, in_specs=in_specs, out_specs=out_specs, check_vma=False
    )
```

```python
import functools

import jax
import jax.numpy as jnp
from jax import lax
from jax.experimental import pallas as pl
from jax.experimental.pallas import tpu as pltpu
from jax.sharding import PartitionSpec as P

BF16 = jnp.bfloat16
F32 = jnp.float32
MIB = 1 << 20


def dot(a, b):
    return jnp.dot(a, b, preferred_element_type=F32)


def dot_t(a, b):
    return lax.dot_general(a, b, (((1,), (1,)), ((), ())), preferred_element_type=F32)


def dot_l(a, b):
    return lax.dot_general(a, b, (((0,), (0,)), ((), ())), preferred_element_type=F32)


def layer_norm(values):
    mean = jnp.mean(values, -1, keepdims=True)
    centred = values - mean
    variance = jnp.mean(centred * centred, -1, keepdims=True)
    return centred * lax.rsqrt(variance + 1e-06)


def smem():
    return pl.BlockSpec(memory_space=pltpu.SMEM)


def params(mib, **kw):
    return pltpu.CompilerParams(vmem_limit_bytes=mib * MIB, **kw)


def qkv_kernel(step_ref, x_ref, mod_ref, w_ref, gain_ref, out_ref):
    step = step_ref[0]
    width = x_ref.shape[1]
    shift = mod_ref[pl.ds(step, 1), :width]
    scale = mod_ref[pl.ds(step, 1), width:]
    normed = (layer_norm(x_ref[...].astype(F32)) * (1.0 + scale) + shift).astype(BF16)
    inner = w_ref.shape[2]
    head = gain_ref.shape[1]
    for part in range(3):
        proj = dot(normed, w_ref[part])
        if part < 2:
            gain = gain_ref[part : part + 1, :]
            for h in range(inner // head):
                one = proj[:, h * head : (h + 1) * head]
                one = one * lax.rsqrt(jnp.mean(one * one, -1, keepdims=True) + 1e-06) * gain
                lo = part * inner + h * head
                out_ref[:, lo : lo + head] = one.astype(BF16)
        else:
            out_ref[:, part * inner : (part + 1) * inner] = proj.astype(BF16)


def qkv_call(step, x, modulation, w, gain):
    tokens, width = x.shape
    inner = w.shape[2]
    rows = 256
    return pl.pallas_call(
        qkv_kernel,
        grid=(tokens // rows,),
        in_specs=[
            smem(),
            pl.BlockSpec((rows, width), lambda i: (i, 0)),
            pl.BlockSpec((modulation.shape[0], 2 * width), lambda i: (0, 0)),
            pl.BlockSpec(w.shape, lambda i: (0, 0, 0)),
            pl.BlockSpec(gain.shape, lambda i: (0, 0)),
        ],
        out_specs=pl.BlockSpec((rows, 3 * inner), lambda i: (i, 0)),
        out_shape=jax.ShapeDtypeStruct((tokens, 3 * inner), BF16),
        compiler_params=params(56),
        name="qkv",
    )(step, x, modulation, w, gain)


def attention_kernel(few, head, in_ref, out_ref):
    rows = in_ref.shape[0]
    inner = out_ref.shape[1]
    row_pos = lax.broadcasted_iota(jnp.int32, (rows, rows), 0) % few
    col_pos = lax.broadcasted_iota(jnp.int32, (rows, rows), 1) % few
    same = row_pos == col_pos
    for h in range(inner // head):
        lo = h * head
        q = in_ref[:, lo : lo + head]
        k = in_ref[:, inner + lo : inner + lo + head]
        v = in_ref[:, 2 * inner + lo : 2 * inner + lo + head]
        raised = jnp.where(same, jnp.exp(dot_t(q, k) * head ** (-0.5)), 0.0)
        probs = (raised / jnp.sum(raised, -1, keepdims=True)).astype(BF16)
        out_ref[:, lo : lo + head] = dot(probs, v).astype(BF16)


def attention_call(stacked, few, head):
    rows, wide = stacked.shape
    return pl.pallas_call(
        functools.partial(attention_kernel, few, head),
        out_shape=jax.ShapeDtypeStruct((rows, wide // 3), BF16),
        compiler_params=params(16),
        name="attention",
    )(stacked)


def spread(values, per):
    experts = values.shape[1]
    shape = (experts, experts * per)
    expand = (
        lax.broadcasted_iota(jnp.int32, shape, 1) // per
        == lax.broadcasted_iota(jnp.int32, shape, 0)
    ).astype(F32)
    return jnp.dot(values, expand, precision=lax.Precision.HIGHEST, preferred_element_type=F32)


def slot_row(picks_f32, counts_f32, first, per):
    wide = spread(picks_f32, 2 * per)
    slot = lax.broadcasted_iota(jnp.int32, wide.shape, 0)
    wanted = first + lax.broadcasted_iota(jnp.int32, wide.shape, 1) % per
    mine = slot == wanted
    if counts_f32 is not None:
        limit = spread(counts_f32, 2 * per)
        wide = jnp.where(slot.astype(F32) < limit, wide, -1.0)
    return jnp.sum(jnp.where(mine, wide, 0.0), axis=0, keepdims=True).astype(jnp.int32)


def row_half(shape, per, dim):
    return (lax.broadcasted_iota(jnp.int32, shape, dim) // per) % 2


def ones_where(mask):
    return mask.astype(F32).astype(BF16)


def halves_to_rows(count, per, half):
    shape = (2 * count, count)
    row = lax.broadcasted_iota(jnp.int32, shape, 0)
    col = lax.broadcasted_iota(jnp.int32, shape, 1)
    return ones_where(row == (col // per * 2 + half) * per + col % per)


def mix_kernel(
    per, pieces, rank_ref, core_ref, lane_ref, step_ref, att_ref, x_ref, gate_ref, shift_ref,
    scale_ref, router_ref, picks_ref, *refs
):
    blocks = refs[: 2 * pieces]
    disp_ref, gates_ref, share_ref, hidden_ref, normed_ref, w_ref, sems = refs[2 * pieces :]
    step = step_ref[0]
    rank = rank_ref[0]
    tile = pl.program_id(0)
    rows = x_ref.shape[0]
    parts = att_ref.shape[0]
    inner = att_ref.shape[2]

    @pl.when(tile == 0)
    def _():
        some = blocks[0].shape[0] // parts
        copies = []
        for number, block in enumerate(blocks):
            which, turn = divmod(number, pieces)
            half = lax.rem(core_ref[0] + which, 2)
            place = lax.rem(lane_ref[0] + turn, pieces)
            for part_turn in range(parts):
                part = lax.rem(rank + part_turn, parts)
                to = pl.multiple_of(part * inner + half * (inner // 2) + place * some, some)
                copies.append(
                    pltpu.make_async_copy(
                        block.at[pl.ds(part_turn * some, some), :],
                        w_ref.at[pl.ds(to, some), :],
                        sems.at[number * parts + part_turn],
                    )
                )
        for copy in copies:
            copy.start()
        for copy in copies:
            copy.wait()

    gate = gate_ref[pl.ds(step, 1), :]
    shift = shift_ref[pl.ds(step, 1), :]
    scale = scale_ref[pl.ds(step, 1), :]
    mixed = dot(att_ref[0], w_ref[:inner, :])
    for part in range(1, parts):
        mixed += dot(att_ref[part], w_ref[part * inner : (part + 1) * inner, :])
    hidden = x_ref[...].astype(F32) + gate * mixed
    hidden_ref[...] = hidden
    normed = (layer_norm(hidden) * (1.0 + scale) + shift).astype(BF16)
    normed_ref[pl.ds(pl.multiple_of(tile * rows, rows), rows), :] = normed
    gates_ref[...] = jax.nn.sigmoid(dot_t(normed, router_ref[...]))
    share = share_ref.shape[0]
    each = rows // share

    @pl.when(tile == rank // each)
    def _():
        start = pl.multiple_of((rank % each) * share, share)
        share_ref[...] = hidden_ref[pl.ds(start, share), :]

    @pl.when(tile == pl.num_programs(0) - 1)
    def _():
        row = slot_row(picks_ref[...].astype(F32), None, rank * per, per)
        tokens = normed_ref.shape[0]
        shape = (tokens, row.shape[1])
        picked = lax.broadcasted_iota(jnp.int32, shape, 0) == row
        half = row_half(shape, per, 1)
        cols = disp_ref.shape[1]
        disp_ref[...] = (
            dot_l(ones_where(picked & (half == 0)), normed_ref[:, :cols])
            + dot_l(ones_where(picked & (half == 1)), normed_ref[:, cols:])
        ).astype(BF16)


def mix_call(
    rank, core, lane, step, att, blocks, x, modulation, router_t, picks_t, per, share
):
    tokens, width = x.shape
    parts, _, inner = att.shape
    experts = router_t.shape[0]
    steps = modulation.shape[0]
    rows = 256
    return pl.pallas_call(
        functools.partial(mix_kernel, per, len(blocks) // 2),
        grid=(tokens // rows,),
        in_specs=[smem()] * 4
        + [
            pl.BlockSpec((parts, rows, inner), lambda i: (0, i, 0)),
            pl.BlockSpec((rows, width), lambda i: (i, 0)),
            pl.BlockSpec((steps, width), lambda i: (0, 2)),
            pl.BlockSpec((steps, width), lambda i: (0, 3)),
            pl.BlockSpec((steps, width), lambda i: (0, 4)),
            pl.BlockSpec(router_t.shape, lambda i: (0, 0)),
            pl.BlockSpec(picks_t.shape, lambda i: (0, 0)),
        ]
        + [pl.BlockSpec(memory_space=pl.ANY)] * len(blocks),
        out_specs=[
            pl.BlockSpec((2 * experts * per, width // 2), lambda i: (0, 0)),
            pl.BlockSpec((rows, experts), lambda i: (i, 0)),
            pl.BlockSpec((share, width), lambda i: (0, 0)),
        ],
        out_shape=[
            jax.ShapeDtypeStruct((2 * experts * per, width // 2), BF16),
            jax.ShapeDtypeStruct((tokens, experts), F32),
            jax.ShapeDtypeStruct((share, width), F32),
        ],
        scratch_shapes=[
            pltpu.VMEM((rows, width), F32),
            pltpu.VMEM((tokens, width), BF16),
            pltpu.VMEM((parts * inner, width), BF16),
            pltpu.SemaphoreType.DMA((len(blocks) * parts,)),
        ],
        compiler_params=params(48),
        name="mix",
    )(
        rank, core, lane, step, att, x, modulation, modulation, modulation, router_t, picks_t,
        *blocks,
    )


def up_kernel(per, rows_ref, w_ref, out_ref, tok_ref):
    @pl.when(pl.program_id(0) == 0)
    def _():
        count = tok_ref.shape[0]
        cols = rows_ref.shape[1]
        for half in range(2):
            pick = halves_to_rows(count, per, half)
            tok_ref[:, half * cols : (half + 1) * cols] = dot_l(pick, rows_ref[...]).astype(BF16)

    out_ref[...] = jax.nn.gelu(dot(tok_ref[...], w_ref[0])).astype(BF16)


def up_call(rows, w, per):
    parts, width, units = w.shape
    count = rows.shape[0] // 2
    return pl.pallas_call(
        functools.partial(up_kernel, per),
        grid=(parts,),
        in_specs=[
            pl.BlockSpec(rows.shape, lambda i: (0, 0)),
            pl.BlockSpec((1, width, units), lambda i: (i, 0, 0)),
        ],
        out_specs=pl.BlockSpec((count, units), lambda i: (0, i)),
        out_shape=jax.ShapeDtypeStruct((count, parts * units), BF16),
        scratch_shapes=[pltpu.VMEM((count, width), BF16)],
        compiler_params=params(56),
        name="up",
    )(rows, w)


def down_kernel(per, rank_ref, hid_ref, *refs):
    out_ref = refs[-1]
    blocks = refs[:-1]
    units = blocks[0].shape[0]
    total = None
    for turn, block in enumerate(blocks):
        at = lax.rem(rank_ref[0] + turn, len(blocks))
        some = hid_ref[:, pl.ds(pl.multiple_of(at * units, units), units)]
        term = dot(some, block[...])
        total = term if total is None else total + term
    total = total.astype(BF16)
    count = total.shape[0]

    @pl.when(pl.program_id(0) == 0)
    def _():
        out_ref[...] = dot(halves_to_rows(count, per, 0), total).astype(BF16)

    @pl.when(pl.program_id(0) == 1)
    def _():
        out_ref[...] += dot(halves_to_rows(count, per, 1), total).astype(BF16)


def down_call(rank, hidden, blocks, per):
    rows, units = hidden.shape
    few, half = blocks[0].shape
    cols = half // 2
    return pl.pallas_call(
        functools.partial(down_kernel, per),
        grid=(2,),
        in_specs=[smem(), pl.BlockSpec((rows, units), lambda i: (0, 0))]
        + [pl.BlockSpec((few, cols), lambda i: (0, i))] * len(blocks),
        out_specs=pl.BlockSpec((2 * rows, cols), lambda i: (0, 0)),
        out_shape=jax.ShapeDtypeStruct((2 * rows, cols), BF16),
        compiler_params=params(56),
        name="down",
    )(rank, hidden, *blocks)


def combine_kernel(per, rank_ref, gates_ref, picks_ref, counts_ref, own_ref, other_ref, out_ref):
    rank = rank_ref[0]
    tokens = gates_ref.shape[0]
    experts = gates_ref.shape[1]
    picks = picks_ref[...].astype(F32)
    counts = counts_ref[...].astype(F32)
    shape = (experts, 2 * experts * per)
    expand = ones_where(
        lax.broadcasted_iota(jnp.int32, shape, 1) // (2 * per)
        == lax.broadcasted_iota(jnp.int32, shape, 0)
    )
    wide = dot(gates_ref[...].astype(BF16), expand)
    token = lax.broadcasted_iota(jnp.int32, wide.shape, 0)
    which = row_half(wide.shape, per, 1)
    partner = rank + 1 - 2 * lax.rem(rank, 2)
    cols = own_ref.shape[1]
    sums = [None, None]
    for who, rows_ref in ((rank, own_ref), (partner, other_ref)):
        row = slot_row(picks, counts, who * per, per)
        weight = jnp.where(token == row, wide, 0.0)
        for half in range(2):
            term = dot(jnp.where(which == half, weight, 0.0).astype(BF16), rows_ref[...])
            sums[half] = term if sums[half] is None else sums[half] + term
    for half in range(2):
        out_ref[:, half * cols : (half + 1) * cols] = sums[half].astype(BF16)


def combine_call(rank, gates, picks_t, counts_t, own, other, per):
    half = 2 * own.shape[1]
    vmem = pl.BlockSpec(memory_space=pltpu.VMEM)
    return pl.pallas_call(
        functools.partial(combine_kernel, per),
        in_specs=[smem()] + [vmem] * 5,
        out_specs=vmem,
        out_shape=jax.ShapeDtypeStruct((gates.shape[0], half), BF16),
        compiler_params=params(16),
        name="combine",
    )(rank, gates, picks_t, counts_t, own, other)


def final_kernel(step_ref, share_ref, gate_ref, parts_ref, out_ref):
    gate = gate_ref[pl.ds(step_ref[0], 1), :]
    half = parts_ref.shape[2]
    for b in range(2):
        cols = slice(b * half, (b + 1) * half)
        mixture = parts_ref[b].astype(F32) + parts_ref[b + 2].astype(F32)
        out_ref[:, cols] = (share_ref[:, cols] + gate[:, cols] * mixture).astype(BF16)


def final_call(step, share, modulation, parts):
    rows, width = share.shape
    return pl.pallas_call(
        final_kernel,
        grid=(1,),
        in_specs=[
            smem(),
            pl.BlockSpec((rows, width), lambda i: (0, 0)),
            pl.BlockSpec((modulation.shape[0], width), lambda i: (0, 5)),
            pl.BlockSpec(parts.shape, lambda i: (0, 0, 0)),
        ],
        out_specs=pl.BlockSpec((rows, width), lambda i: (0, 0)),
        out_shape=jax.ShapeDtypeStruct((rows, width), BF16),
        compiler_params=params(16),
        name="final",
    )(step, share, modulation, parts)


def on_device(
    frames_in,
    step_index,
    modulation,
    qkv_weight,
    qk_gain,
    out_weight,
    router_weight,
    expert_up,
    expert_down,
    picks,
    counts,
):
    _, position_count, model_width = frames_in.shape
    ffn = lax.axis_size("ffn")
    seq = lax.axis_size("seq")
    rank = lax.axis_index("ffn").astype(jnp.int32)
    rank_arr = rank.reshape(1)
    head_size = qk_gain.shape[1]
    share_len = position_count // ffn
    slot_count = picks.shape[2]
    per = slot_count // ffn
    half = model_width // 2
    x = frames_in[0]
    picks_t = jnp.transpose(picks, (1, 2, 0))[0]
    counts_t = jnp.transpose(counts, (1, 0))

    def over_seq(values):
        return lax.all_to_all(values, "seq", split_axis=0, concat_axis=0, tiled=True)

    def over_ffn(values):
        return lax.all_to_all(values, "ffn", split_axis=0, concat_axis=0, tiled=True)

    place = lax.axis_index("seq").astype(jnp.int32)
    core = lax.rem(place, 2)
    lanes = 4
    stride = seq // lanes
    lane = place // stride
    some = out_weight.shape[0] // (2 * lanes)
    out_own = lax.dynamic_slice_in_dim(out_weight, (core * lanes + lane) * some, some, 0)
    up_full = lax.all_gather(expert_up, "ffn", axis=0, tiled=True)
    down = expert_down[0]
    side = lax.rem(rank, 2)
    same_half = lax.dynamic_slice_in_dim(down, side * half, half, 1)
    other_half = lax.dynamic_slice_in_dim(down, (1 - side) * half, half, 1)

    def from_turn(values, turn):
        return lax.ppermute(values, "ffn", [((i + turn) % ffn, i) for i in range(ffn)])

    out_rows = [out_own] + [from_turn(out_own, turn) for turn in range(1, ffn)]
    blocks = [
        same_half,
        from_turn(other_half, 1),
        from_turn(same_half, 2),
        from_turn(other_half, 3),
    ]

    stacked = qkv_call(step_index, x, modulation, jnp.transpose(qkv_weight, (1, 0, 2)), qk_gain)
    stacked = over_seq(stacked)
    stacked, out_rows = lax.optimization_barrier((stacked, out_rows))
    out_rows = jnp.concatenate(out_rows, axis=0)

    def from_lane(values, turn):
        pairs = [((i + turn * stride) % seq, i) for i in range(seq)]
        return lax.ppermute(values, "seq", pairs)

    out_blocks = [out_rows] + [from_lane(out_rows, turn) for turn in range(1, lanes)]
    attended = attention_call(stacked, position_count // seq, head_size)
    attended = over_seq(attended)
    attended, out_blocks = lax.optimization_barrier((attended, out_blocks))
    swap = [(i, i ^ 1) for i in range(seq)]
    out_blocks = out_blocks + [lax.ppermute(b, "seq", swap) for b in out_blocks]
    every = over_ffn(jnp.broadcast_to(attended[None], (ffn,) + attended.shape))
    outgoing, gates, share = mix_call(
        rank_arr, core.reshape(1), lane.reshape(1), step_index, every, out_blocks, x, modulation,
        jnp.transpose(router_weight, (1, 0)), picks_t, per, share_len,
    )
    expert_tokens = over_seq(outgoing)
    hidden = up_call(expert_tokens, up_full, per)
    hidden_other = lax.ppermute(hidden, "ffn", [(i, i ^ 1) for i in range(ffn)])
    own = over_seq(down_call(rank_arr, hidden, blocks, per))
    other = over_seq(down_call(rank_arr, hidden_other, blocks, per))
    mixture = combine_call(rank_arr, gates, picks_t, counts_t, own, other, per)
    parts = over_ffn(mixture).reshape(ffn, share_len, half)
    return final_call(step_index, share, modulation, parts)[None]


def solution(mesh):
    in_specs = (
        P("seq", None, None),
        P("seq"),
        P(),
        P(None, None, "ffn"),
        P(),
        P("ffn", None),
        P(),
        P("seq", None, "ffn"),
        P("seq", "ffn", None),
        P(None, "seq", None),
        P(None, "seq"),
    )
    out_specs = P("seq", "ffn", None)
    return jax.shard_map(
        on_device, mesh=mesh, in_specs=in_specs, out_specs=out_specs, check_vma=False
    )
```

```python
import functools

import jax
import jax.numpy as jnp
from jax import lax
from jax.experimental import pallas as pl
from jax.experimental.pallas import tpu as pltpu
from jax.sharding import PartitionSpec as P

BF16 = jnp.bfloat16
F32 = jnp.float32
MIB = 1 << 20


def dot(a, b):
    return jnp.dot(a, b, preferred_element_type=F32)


def dot_t(a, b):
    return lax.dot_general(a, b, (((1,), (1,)), ((), ())), preferred_element_type=F32)


def dot_l(a, b):
    return lax.dot_general(a, b, (((0,), (0,)), ((), ())), preferred_element_type=F32)


def layer_norm(values):
    mean = jnp.mean(values, -1, keepdims=True)
    centred = values - mean
    variance = jnp.mean(centred * centred, -1, keepdims=True)
    return centred * lax.rsqrt(variance + 1e-06)


def quotient(values, by):
    return lax.shift_right_logical(values, by.bit_length() - 1)


def remainder(values, by):
    return values & (by - 1)


def smem():
    return pl.BlockSpec(memory_space=pltpu.SMEM)


def params(mib, **kw):
    return pltpu.CompilerParams(vmem_limit_bytes=mib * MIB, **kw)


def qkv_kernel(step_ref, x_ref, mod_ref, w_ref, gain_ref, out_ref):
    step = step_ref[0]
    width = x_ref.shape[1]
    shift = mod_ref[pl.ds(step, 1), :width]
    scale = mod_ref[pl.ds(step, 1), width:]
    normed = (layer_norm(x_ref[...].astype(F32)) * (1.0 + scale) + shift).astype(BF16)
    inner = w_ref.shape[2]
    head = gain_ref.shape[1]
    for part in range(3):
        proj = dot(normed, w_ref[part])
        if part < 2:
            gain = gain_ref[part : part + 1, :]
            for h in range(inner // head):
                one = proj[:, h * head : (h + 1) * head]
                one = one * lax.rsqrt(jnp.mean(one * one, -1, keepdims=True) + 1e-06) * gain
                lo = part * inner + h * head
                out_ref[:, lo : lo + head] = one.astype(BF16)
        else:
            out_ref[:, part * inner : (part + 1) * inner] = proj.astype(BF16)


def qkv_call(step, x, modulation, w, gain):
    tokens, width = x.shape
    inner = w.shape[2]
    rows = 256
    return pl.pallas_call(
        qkv_kernel,
        grid=(tokens // rows,),
        in_specs=[
            smem(),
            pl.BlockSpec((rows, width), lambda i: (i, 0)),
            pl.BlockSpec((modulation.shape[0], 2 * width), lambda i: (0, 0)),
            pl.BlockSpec(w.shape, lambda i: (0, 0, 0)),
            pl.BlockSpec(gain.shape, lambda i: (0, 0)),
        ],
        out_specs=pl.BlockSpec((rows, 3 * inner), lambda i: (i, 0)),
        out_shape=jax.ShapeDtypeStruct((tokens, 3 * inner), BF16),
        compiler_params=params(60),
        name="qkv",
    )(step, x, modulation, w, gain)


def attention_kernel(few, head, in_ref, out_ref):
    rows = in_ref.shape[0]
    inner = out_ref.shape[1]
    row_pos = remainder(lax.broadcasted_iota(jnp.int32, (rows, rows), 0), few)
    col_pos = remainder(lax.broadcasted_iota(jnp.int32, (rows, rows), 1), few)
    same = row_pos == col_pos
    for h in range(inner // head):
        lo = h * head
        q = in_ref[:, lo : lo + head]
        k = in_ref[:, inner + lo : inner + lo + head]
        v = in_ref[:, 2 * inner + lo : 2 * inner + lo + head]
        raised = jnp.where(same, jnp.exp(dot_t(q, k) * head ** (-0.5)), 0.0)
        probs = (raised / jnp.sum(raised, -1, keepdims=True)).astype(BF16)
        out_ref[:, lo : lo + head] = dot(probs, v).astype(BF16)


def attention_call(stacked, few, head):
    rows, wide = stacked.shape
    return pl.pallas_call(
        functools.partial(attention_kernel, few, head),
        out_shape=jax.ShapeDtypeStruct((rows, wide // 3), BF16),
        compiler_params=params(16),
        name="attention",
    )(stacked)


def spread(values, per):
    experts = values.shape[1]
    shape = (experts, experts * per)
    expand = (
        quotient(lax.broadcasted_iota(jnp.int32, shape, 1), per)
        == lax.broadcasted_iota(jnp.int32, shape, 0)
    ).astype(F32)
    return jnp.dot(values, expand, precision=lax.Precision.HIGHEST, preferred_element_type=F32)


def slot_row(picks_f32, counts_f32, first, per):
    wide = spread(picks_f32, 2 * per)
    slot = lax.broadcasted_iota(jnp.int32, wide.shape, 0)
    wanted = first + remainder(lax.broadcasted_iota(jnp.int32, wide.shape, 1), per)
    mine = slot == wanted
    if counts_f32 is not None:
        limit = spread(counts_f32, 2 * per)
        wide = jnp.where(slot.astype(F32) < limit, wide, -1.0)
    return jnp.sum(jnp.where(mine, wide, 0.0), axis=0, keepdims=True).astype(jnp.int32)


def row_half(shape, per, dim):
    return remainder(quotient(lax.broadcasted_iota(jnp.int32, shape, dim), per), 2)


def ones_where(mask):
    return mask.astype(F32).astype(BF16)


def halves_to_rows(count, per, half):
    shape = (2 * count, count)
    row = lax.broadcasted_iota(jnp.int32, shape, 0)
    col = lax.broadcasted_iota(jnp.int32, shape, 1)
    wanted = (quotient(col, per) * 2 + half) * per + remainder(col, per)
    return ones_where(row == wanted)


def mix_kernel(
    per, pieces, rank_ref, core_ref, lane_ref, step_ref, att_ref, x_ref, gate_ref, shift_ref,
    scale_ref, router_ref, picks_ref, *refs
):
    blocks = refs[: 2 * pieces]
    disp_ref, gates_ref, share_ref, hidden_ref, normed_ref, w_ref, sems = refs[2 * pieces :]
    step = step_ref[0]
    rank = rank_ref[0]
    tile = pl.program_id(0)
    rows = x_ref.shape[0]
    parts = att_ref.shape[0]
    inner = att_ref.shape[2]

    @pl.when(tile == 0)
    def _():
        some = blocks[0].shape[0] // parts
        copies = []
        for number, block in enumerate(blocks):
            which, turn = divmod(number, pieces)
            half = lax.rem(core_ref[0] + which, 2)
            place = lax.rem(lane_ref[0] + turn, pieces)
            for part_turn in range(parts):
                part = lax.rem(rank + part_turn, parts)
                to = pl.multiple_of(part * inner + half * (inner // 2) + place * some, some)
                copies.append(
                    pltpu.make_async_copy(
                        block.at[pl.ds(part_turn * some, some), :],
                        w_ref.at[pl.ds(to, some), :],
                        sems.at[number * parts + part_turn],
                    )
                )
        for copy in copies:
            copy.start()
        for copy in copies:
            copy.wait()

    gate = gate_ref[pl.ds(step, 1), :]
    shift = shift_ref[pl.ds(step, 1), :]
    scale = scale_ref[pl.ds(step, 1), :]
    every = jnp.concatenate([att_ref[part] for part in range(parts)], axis=1)
    mixed = dot(every, w_ref[...])
    hidden = x_ref[...].astype(F32) + gate * mixed
    hidden_ref[...] = hidden
    normed = (layer_norm(hidden) * (1.0 + scale) + shift).astype(BF16)
    normed_ref[pl.ds(pl.multiple_of(tile * rows, rows), rows), :] = normed
    gates_ref[...] = jax.nn.sigmoid(dot_t(normed, router_ref[...]))
    share = share_ref.shape[0]
    each = rows // share

    @pl.when(tile == rank // each)
    def _():
        start = pl.multiple_of((rank % each) * share, share)
        share_ref[...] = hidden_ref[pl.ds(start, share), :]

    @pl.when(tile == pl.num_programs(0) - 1)
    def _():
        row = slot_row(picks_ref[...].astype(F32), None, rank * per, per)
        tokens = normed_ref.shape[0]
        shape = (tokens, row.shape[1])
        picked = lax.broadcasted_iota(jnp.int32, shape, 0) == row
        half = row_half(shape, per, 1)
        cols = disp_ref.shape[1]
        disp_ref[...] = (
            dot_l(ones_where(picked & (half == 0)), normed_ref[:, :cols])
            + dot_l(ones_where(picked & (half == 1)), normed_ref[:, cols:])
        ).astype(BF16)


def mix_call(
    rank, core, lane, step, att, blocks, x, modulation, router_t, picks_t, per, share
):
    tokens, width = x.shape
    parts, _, inner = att.shape
    experts = router_t.shape[0]
    steps = modulation.shape[0]
    rows = 256
    return pl.pallas_call(
        functools.partial(mix_kernel, per, len(blocks) // 2),
        grid=(tokens // rows,),
        in_specs=[smem()] * 4
        + [
            pl.BlockSpec((parts, rows, inner), lambda i: (0, i, 0)),
            pl.BlockSpec((rows, width), lambda i: (i, 0)),
            pl.BlockSpec((steps, width), lambda i: (0, 2)),
            pl.BlockSpec((steps, width), lambda i: (0, 3)),
            pl.BlockSpec((steps, width), lambda i: (0, 4)),
            pl.BlockSpec(router_t.shape, lambda i: (0, 0)),
            pl.BlockSpec(picks_t.shape, lambda i: (0, 0)),
        ]
        + [pl.BlockSpec(memory_space=pl.ANY)] * len(blocks),
        out_specs=[
            pl.BlockSpec((2 * experts * per, width // 2), lambda i: (0, 0)),
            pl.BlockSpec((rows, experts), lambda i: (i, 0)),
            pl.BlockSpec((share, width), lambda i: (0, 0)),
        ],
        out_shape=[
            jax.ShapeDtypeStruct((2 * experts * per, width // 2), BF16),
            jax.ShapeDtypeStruct((tokens, experts), F32),
            jax.ShapeDtypeStruct((share, width), F32),
        ],
        scratch_shapes=[
            pltpu.VMEM((rows, width), F32),
            pltpu.VMEM((tokens, width), BF16),
            pltpu.VMEM((parts * inner, width), BF16),
            pltpu.SemaphoreType.DMA((len(blocks) * parts,)),
        ],
        compiler_params=params(60),
        name="mix",
    )(
        rank, core, lane, step, att, x, modulation, modulation, modulation, router_t, picks_t,
        *blocks,
    )


def up_kernel(per, rows_ref, w_ref, out_ref, tok_ref):
    @pl.when(pl.program_id(0) == 0)
    def _():
        count = tok_ref.shape[0]
        cols = rows_ref.shape[1]
        for half in range(2):
            pick = halves_to_rows(count, per, half)
            tok_ref[:, half * cols : (half + 1) * cols] = dot_l(pick, rows_ref[...]).astype(BF16)

    out_ref[...] = jax.nn.gelu(dot(tok_ref[...], w_ref[0])).astype(BF16)


def up_call(rows, w, per):
    parts, width, units = w.shape
    count = rows.shape[0] // 2
    return pl.pallas_call(
        functools.partial(up_kernel, per),
        grid=(parts,),
        in_specs=[
            pl.BlockSpec(rows.shape, lambda i: (0, 0)),
            pl.BlockSpec((1, width, units), lambda i: (i, 0, 0)),
        ],
        out_specs=pl.BlockSpec((count, units), lambda i: (0, i)),
        out_shape=jax.ShapeDtypeStruct((count, parts * units), BF16),
        scratch_shapes=[pltpu.VMEM((count, width), BF16)],
        compiler_params=params(60),
        name="up",
    )(rows, w)


def down_kernel(per, rank_ref, hid_ref, *refs):
    out_ref = refs[-1]
    blocks = refs[:-1]
    units = blocks[0].shape[0]
    total = None
    for turn, block in enumerate(blocks):
        at = lax.rem(rank_ref[0] + turn, len(blocks))
        some = hid_ref[:, pl.ds(pl.multiple_of(at * units, units), units)]
        term = dot(some, block[...])
        total = term if total is None else total + term
    total = total.astype(BF16)
    count = total.shape[0]

    @pl.when(pl.program_id(0) == 0)
    def _():
        out_ref[...] = dot(halves_to_rows(count, per, 0), total).astype(BF16)

    @pl.when(pl.program_id(0) == 1)
    def _():
        out_ref[...] += dot(halves_to_rows(count, per, 1), total).astype(BF16)


def down_call(rank, hidden, blocks, per):
    rows, units = hidden.shape
    few, half = blocks[0].shape
    cols = half // 2
    return pl.pallas_call(
        functools.partial(down_kernel, per),
        grid=(2,),
        in_specs=[smem(), pl.BlockSpec((rows, units), lambda i: (0, 0))]
        + [pl.BlockSpec((few, cols), lambda i: (0, i))] * len(blocks),
        out_specs=pl.BlockSpec((2 * rows, cols), lambda i: (0, 0)),
        out_shape=jax.ShapeDtypeStruct((2 * rows, cols), BF16),
        compiler_params=params(60),
        name="down",
    )(rank, hidden, *blocks)


def combine_kernel(per, rank_ref, gates_ref, picks_ref, counts_ref, own_ref, other_ref, out_ref):
    rank = rank_ref[0]
    tokens = gates_ref.shape[0]
    experts = gates_ref.shape[1]
    picks = picks_ref[...].astype(F32)
    counts = counts_ref[...].astype(F32)
    shape = (experts, 2 * experts * per)
    expand = ones_where(
        quotient(lax.broadcasted_iota(jnp.int32, shape, 1), 2 * per)
        == lax.broadcasted_iota(jnp.int32, shape, 0)
    )
    wide = dot(gates_ref[...].astype(BF16), expand)
    token = lax.broadcasted_iota(jnp.int32, wide.shape, 0)
    which = row_half(wide.shape, per, 1)
    partner = rank + 1 - 2 * lax.rem(rank, 2)
    cols = own_ref.shape[1]
    sums = [None, None]
    for who, rows_ref in ((rank, own_ref), (partner, other_ref)):
        row = slot_row(picks, counts, who * per, per)
        weight = jnp.where(token == row, wide, 0.0)
        for half in range(2):
            term = dot(jnp.where(which == half, weight, 0.0).astype(BF16), rows_ref[...])
            sums[half] = term if sums[half] is None else sums[half] + term
    for half in range(2):
        out_ref[:, half * cols : (half + 1) * cols] = sums[half].astype(BF16)


def combine_call(rank, gates, picks_t, counts_t, own, other, per):
    half = 2 * own.shape[1]
    vmem = pl.BlockSpec(memory_space=pltpu.VMEM)
    return pl.pallas_call(
        functools.partial(combine_kernel, per),
        in_specs=[smem()] + [vmem] * 5,
        out_specs=vmem,
        out_shape=jax.ShapeDtypeStruct((gates.shape[0], half), BF16),
        compiler_params=params(16),
        name="combine",
    )(rank, gates, picks_t, counts_t, own, other)


def final_kernel(step_ref, share_ref, gate_ref, parts_ref, out_ref):
    gate = gate_ref[pl.ds(step_ref[0], 1), :]
    half = parts_ref.shape[2]
    for b in range(2):
        cols = slice(b * half, (b + 1) * half)
        mixture = parts_ref[b].astype(F32) + parts_ref[b + 2].astype(F32)
        out_ref[:, cols] = (share_ref[:, cols] + gate[:, cols] * mixture).astype(BF16)


def final_call(step, share, modulation, parts):
    rows, width = share.shape
    return pl.pallas_call(
        final_kernel,
        grid=(1,),
        in_specs=[
            smem(),
            pl.BlockSpec((rows, width), lambda i: (0, 0)),
            pl.BlockSpec((modulation.shape[0], width), lambda i: (0, 5)),
            pl.BlockSpec(parts.shape, lambda i: (0, 0, 0)),
        ],
        out_specs=pl.BlockSpec((rows, width), lambda i: (0, 0)),
        out_shape=jax.ShapeDtypeStruct((rows, width), BF16),
        compiler_params=params(16),
        name="final",
    )(step, share, modulation, parts)


def on_device(
    frames_in,
    step_index,
    modulation,
    qkv_weight,
    qk_gain,
    out_weight,
    router_weight,
    expert_up,
    expert_down,
    picks,
    counts,
):
    _, position_count, model_width = frames_in.shape
    ffn = lax.axis_size("ffn")
    seq = lax.axis_size("seq")
    rank = lax.axis_index("ffn").astype(jnp.int32)
    rank_arr = rank.reshape(1)
    head_size = qk_gain.shape[1]
    share_len = position_count // ffn
    slot_count = picks.shape[2]
    per = slot_count // ffn
    half = model_width // 2
    x = frames_in[0]
    picks_t = jnp.transpose(picks, (1, 2, 0))[0]
    counts_t = jnp.transpose(counts, (1, 0))

    def over_seq(values):
        return lax.all_to_all(values, "seq", split_axis=0, concat_axis=0, tiled=True)

    def over_ffn(values):
        return lax.all_to_all(values, "ffn", split_axis=0, concat_axis=0, tiled=True)

    place = lax.axis_index("seq").astype(jnp.int32)
    core = lax.rem(place, 2)
    lanes = 4
    stride = seq // lanes
    lane = place // stride
    some = out_weight.shape[0] // (2 * lanes)
    out_own = lax.dynamic_slice_in_dim(out_weight, (core * lanes + lane) * some, some, 0)
    up_full = lax.all_gather(expert_up, "ffn", axis=0, tiled=True)
    down = expert_down[0]
    side = lax.rem(rank, 2)
    same_half = lax.dynamic_slice_in_dim(down, side * half, half, 1)
    other_half = lax.dynamic_slice_in_dim(down, (1 - side) * half, half, 1)

    def from_turn(values, turn):
        return lax.ppermute(values, "ffn", [((i + turn) % ffn, i) for i in range(ffn)])

    out_rows = [out_own] + [from_turn(out_own, turn) for turn in range(1, ffn)]
    blocks = [
        same_half,
        from_turn(other_half, 1),
        from_turn(same_half, 2),
        from_turn(other_half, 3),
    ]

    stacked = qkv_call(step_index, x, modulation, jnp.transpose(qkv_weight, (1, 0, 2)), qk_gain)
    stacked = over_seq(stacked)
    stacked, out_rows = lax.optimization_barrier((stacked, out_rows))
    out_rows = jnp.concatenate(out_rows, axis=0)

    def from_lane(values, turn):
        pairs = [((i + turn * stride) % seq, i) for i in range(seq)]
        return lax.ppermute(values, "seq", pairs)

    out_blocks = [out_rows] + [from_lane(out_rows, turn) for turn in range(1, lanes)]
    attended = attention_call(stacked, position_count // seq, head_size)
    attended = over_seq(attended)
    near = (blocks[1], blocks[3])
    attended, out_blocks, near = lax.optimization_barrier((attended, out_blocks, near))
    blocks[1], blocks[3] = near
    swap = [(i, i ^ 1) for i in range(seq)]
    out_blocks = out_blocks + [lax.ppermute(b, "seq", swap) for b in out_blocks]
    every = over_ffn(jnp.broadcast_to(attended[None], (ffn,) + attended.shape))
    outgoing, gates, share = mix_call(
        rank_arr, core.reshape(1), lane.reshape(1), step_index, every, out_blocks, x, modulation,
        jnp.transpose(router_weight, (1, 0)), picks_t, per, share_len,
    )
    expert_tokens = over_seq(outgoing)
    hidden = up_call(expert_tokens, up_full, per)
    hidden_other = lax.ppermute(hidden, "ffn", [(i, i ^ 1) for i in range(ffn)])
    own = over_seq(down_call(rank_arr, hidden, blocks, per))
    other = over_seq(down_call(rank_arr, hidden_other, blocks, per))
    mixture = combine_call(rank_arr, gates, picks_t, counts_t, own, other, per)
    parts = over_ffn(mixture).reshape(ffn, share_len, half)
    return final_call(step_index, share, modulation, parts)[None]


def solution(mesh):
    in_specs = (
        P("seq", None, None),
        P("seq"),
        P(),
        P(None, None, "ffn"),
        P(),
        P("ffn", None),
        P(),
        P("seq", None, "ffn"),
        P("seq", "ffn", None),
        P(None, "seq", None),
        P(None, "seq"),
    )
    out_specs = P("seq", "ffn", None)
    return jax.shard_map(
        on_device, mesh=mesh, in_specs=in_specs, out_specs=out_specs, check_vma=False
    )
```

```python
import functools

import jax
import jax.numpy as jnp
from jax import lax
from jax.experimental import pallas as pl
from jax.experimental.pallas import tpu as pltpu
from jax.sharding import PartitionSpec as P

BF16 = jnp.bfloat16
F32 = jnp.float32
MIB = 1 << 20


def dot(a, b):
    return jnp.dot(a, b, preferred_element_type=F32)


def dot_t(a, b):
    return lax.dot_general(a, b, (((1,), (1,)), ((), ())), preferred_element_type=F32)


def dot_l(a, b):
    return lax.dot_general(a, b, (((0,), (0,)), ((), ())), preferred_element_type=F32)


def layer_norm(values):
    mean = jnp.mean(values, -1, keepdims=True)
    centred = values - mean
    variance = jnp.mean(centred * centred, -1, keepdims=True)
    return centred * lax.rsqrt(variance + 1e-06)


def quotient(values, by):
    return lax.shift_right_logical(values, by.bit_length() - 1)


def remainder(values, by):
    return values & (by - 1)


def smem():
    return pl.BlockSpec(memory_space=pltpu.SMEM)


def params(mib, **kw):
    return pltpu.CompilerParams(vmem_limit_bytes=mib * MIB, **kw)


def qkv_kernel(step_ref, x_ref, mod_ref, w_ref, gain_ref, out_ref):
    step = step_ref[0]
    width = x_ref.shape[1]
    shift = mod_ref[pl.ds(step, 1), :width]
    scale = mod_ref[pl.ds(step, 1), width:]
    normed = (layer_norm(x_ref[...].astype(F32)) * (1.0 + scale) + shift).astype(BF16)
    inner = w_ref.shape[2]
    head = gain_ref.shape[1]
    for part in range(3):
        proj = dot(normed, w_ref[part])
        if part < 2:
            gain = gain_ref[part : part + 1, :]
            for h in range(inner // head):
                one = proj[:, h * head : (h + 1) * head]
                one = one * lax.rsqrt(jnp.mean(one * one, -1, keepdims=True) + 1e-06) * gain
                lo = part * inner + h * head
                out_ref[:, lo : lo + head] = one.astype(BF16)
        else:
            out_ref[:, part * inner : (part + 1) * inner] = proj.astype(BF16)


def qkv_call(step, x, modulation, w, gain):
    tokens, width = x.shape
    inner = w.shape[2]
    rows = 256
    return pl.pallas_call(
        qkv_kernel,
        grid=(tokens // rows,),
        in_specs=[
            smem(),
            pl.BlockSpec((rows, width), lambda i: (i, 0)),
            pl.BlockSpec((modulation.shape[0], 2 * width), lambda i: (0, 0)),
            pl.BlockSpec(w.shape, lambda i: (0, 0, 0)),
            pl.BlockSpec(gain.shape, lambda i: (0, 0)),
        ],
        out_specs=pl.BlockSpec((rows, 3 * inner), lambda i: (i, 0)),
        out_shape=jax.ShapeDtypeStruct((tokens, 3 * inner), BF16),
        compiler_params=params(60),
        name="qkv",
    )(step, x, modulation, w, gain)


def attention_kernel(few, head, copies, in_ref, out_ref):
    rows = in_ref.shape[0]
    inner = out_ref.shape[1]
    row_pos = remainder(lax.broadcasted_iota(jnp.int32, (rows, rows), 0), few)
    col_pos = remainder(lax.broadcasted_iota(jnp.int32, (rows, rows), 1), few)
    same = row_pos == col_pos
    for h in range(inner // head):
        lo = h * head
        q = in_ref[:, lo : lo + head]
        k = in_ref[:, inner + lo : inner + lo + head]
        v = in_ref[:, 2 * inner + lo : 2 * inner + lo + head]
        raised = jnp.where(same, jnp.exp(dot_t(q, k) * head ** (-0.5)), 0.0)
        probs = (raised / jnp.sum(raised, -1, keepdims=True)).astype(BF16)
        each = dot(probs, v).reshape(rows // few, 1, few, head)
        each = jnp.broadcast_to(each, (rows // few, copies, few, head))
        out_ref[:, lo : lo + head] = each.reshape(copies * rows, head).astype(BF16)


def attention_call(stacked, few, head, copies):
    rows, wide = stacked.shape
    return pl.pallas_call(
        functools.partial(attention_kernel, few, head, copies),
        out_shape=jax.ShapeDtypeStruct((copies * rows, wide // 3), BF16),
        compiler_params=params(16),
        name="attention",
    )(stacked)


def spread(values, per):
    experts = values.shape[1]
    shape = (experts, experts * per)
    expand = (
        quotient(lax.broadcasted_iota(jnp.int32, shape, 1), per)
        == lax.broadcasted_iota(jnp.int32, shape, 0)
    ).astype(F32)
    return jnp.dot(values, expand, precision=lax.Precision.HIGHEST, preferred_element_type=F32)


def slot_row(picks_f32, counts_f32, first, per):
    wide = spread(picks_f32, 2 * per)
    slot = lax.broadcasted_iota(jnp.int32, wide.shape, 0)
    wanted = first + remainder(lax.broadcasted_iota(jnp.int32, wide.shape, 1), per)
    mine = slot == wanted
    if counts_f32 is not None:
        limit = spread(counts_f32, 2 * per)
        wide = jnp.where(slot.astype(F32) < limit, wide, -1.0)
    return jnp.sum(jnp.where(mine, wide, 0.0), axis=0, keepdims=True).astype(jnp.int32)


def row_half(shape, per, dim):
    return remainder(quotient(lax.broadcasted_iota(jnp.int32, shape, dim), per), 2)


def ones_where(mask):
    return mask.astype(F32).astype(BF16)


def halves_to_rows(count, per, half):
    shape = (2 * count, count)
    row = lax.broadcasted_iota(jnp.int32, shape, 0)
    col = lax.broadcasted_iota(jnp.int32, shape, 1)
    wanted = (quotient(col, per) * 2 + half) * per + remainder(col, per)
    return ones_where(row == wanted)


def mix_kernel(
    per, pieces, parts, few, rank_ref, core_ref, lane_ref, step_ref, att_ref, x_ref, gate_ref, shift_ref,
    scale_ref, router_ref, picks_ref, *refs
):
    blocks = refs[: 2 * pieces]
    disp_ref, gates_ref, share_ref, hidden_ref, normed_ref, w_ref, sems = refs[2 * pieces :]
    step = step_ref[0]
    rank = rank_ref[0]
    tile = pl.program_id(0)
    rows = x_ref.shape[0]
    inner = att_ref.shape[1]

    @pl.when(tile == 0)
    def _():
        some = blocks[0].shape[0] // parts
        copies = []
        for number, block in enumerate(blocks):
            which, turn = divmod(number, pieces)
            half = lax.rem(core_ref[0] + which, 2)
            place = lax.rem(lane_ref[0] + turn, pieces)
            for part_turn in range(parts):
                part = lax.rem(rank + part_turn, parts)
                to = pl.multiple_of(part * inner + half * (inner // 2) + place * some, some)
                copies.append(
                    pltpu.make_async_copy(
                        block.at[pl.ds(part_turn * some, some), :],
                        w_ref.at[pl.ds(to, some), :],
                        sems.at[number * parts + part_turn],
                    )
                )
        for copy in copies:
            copy.start()
        for copy in copies:
            copy.wait()

    gate = gate_ref[pl.ds(step, 1), :]
    shift = shift_ref[pl.ds(step, 1), :]
    scale = scale_ref[pl.ds(step, 1), :]
    split = att_ref[...].astype(F32).reshape(rows // few, parts, few, inner)
    every = jnp.concatenate(
        [split[:, part].reshape(rows, inner).astype(BF16) for part in range(parts)], axis=1
    )
    mixed = dot(every, w_ref[...])
    hidden = x_ref[...].astype(F32) + gate * mixed
    hidden_ref[...] = hidden
    normed = (layer_norm(hidden) * (1.0 + scale) + shift).astype(BF16)
    normed_ref[pl.ds(pl.multiple_of(tile * rows, rows), rows), :] = normed
    gates_ref[...] = jax.nn.sigmoid(dot_t(normed, router_ref[...]))
    share = share_ref.shape[0]
    each = rows // share

    @pl.when(tile == rank // each)
    def _():
        start = pl.multiple_of((rank % each) * share, share)
        share_ref[...] = hidden_ref[pl.ds(start, share), :]

    @pl.when(tile == pl.num_programs(0) - 1)
    def _():
        row = slot_row(picks_ref[...].astype(F32), None, rank * per, per)
        tokens = normed_ref.shape[0]
        shape = (tokens, row.shape[1])
        picked = lax.broadcasted_iota(jnp.int32, shape, 0) == row
        half = row_half(shape, per, 1)
        cols = disp_ref.shape[1]
        disp_ref[...] = (
            dot_l(ones_where(picked & (half == 0)), normed_ref[:, :cols])
            + dot_l(ones_where(picked & (half == 1)), normed_ref[:, cols:])
        ).astype(BF16)


def mix_call(
    rank, core, lane, step, att, blocks, x, modulation, router_t, picks_t, per, share, few
):
    tokens, width = x.shape
    parts = att.shape[0] // tokens
    inner = att.shape[1]
    experts = router_t.shape[0]
    steps = modulation.shape[0]
    rows = 256
    return pl.pallas_call(
        functools.partial(mix_kernel, per, len(blocks) // 2, parts, few),
        grid=(tokens // rows,),
        in_specs=[smem()] * 4
        + [
            pl.BlockSpec((parts * rows, inner), lambda i: (i, 0)),
            pl.BlockSpec((rows, width), lambda i: (i, 0)),
            pl.BlockSpec((steps, width), lambda i: (0, 2)),
            pl.BlockSpec((steps, width), lambda i: (0, 3)),
            pl.BlockSpec((steps, width), lambda i: (0, 4)),
            pl.BlockSpec(router_t.shape, lambda i: (0, 0)),
            pl.BlockSpec(picks_t.shape, lambda i: (0, 0)),
        ]
        + [pl.BlockSpec(memory_space=pl.ANY)] * len(blocks),
        out_specs=[
            pl.BlockSpec((2 * experts * per, width // 2), lambda i: (0, 0)),
            pl.BlockSpec((rows, experts), lambda i: (i, 0)),
            pl.BlockSpec((share, width), lambda i: (0, 0)),
        ],
        out_shape=[
            jax.ShapeDtypeStruct((2 * experts * per, width // 2), BF16),
            jax.ShapeDtypeStruct((tokens, experts), F32),
            jax.ShapeDtypeStruct((share, width), F32),
        ],
        scratch_shapes=[
            pltpu.VMEM((rows, width), F32),
            pltpu.VMEM((tokens, width), BF16),
            pltpu.VMEM((parts * inner, width), BF16),
            pltpu.SemaphoreType.DMA((len(blocks) * parts,)),
        ],
        compiler_params=params(60),
        name="mix",
    )(
        rank, core, lane, step, att, x, modulation, modulation, modulation, router_t, picks_t,
        *blocks,
    )


def up_kernel(per, rows_ref, w_ref, out_ref, tok_ref):
    @pl.when(pl.program_id(0) == 0)
    def _():
        count = tok_ref.shape[0]
        cols = rows_ref.shape[1]
        for half in range(2):
            pick = halves_to_rows(count, per, half)
            tok_ref[:, half * cols : (half + 1) * cols] = dot_l(pick, rows_ref[...]).astype(BF16)

    out_ref[...] = jax.nn.gelu(dot(tok_ref[...], w_ref[0])).astype(BF16)


def up_call(rows, w, per):
    parts, width, units = w.shape
    count = rows.shape[0] // 2
    return pl.pallas_call(
        functools.partial(up_kernel, per),
        grid=(parts,),
        in_specs=[
            pl.BlockSpec(rows.shape, lambda i: (0, 0)),
            pl.BlockSpec((1, width, units), lambda i: (i, 0, 0)),
        ],
        out_specs=pl.BlockSpec((count, units), lambda i: (0, i)),
        out_shape=jax.ShapeDtypeStruct((count, parts * units), BF16),
        scratch_shapes=[pltpu.VMEM((count, width), BF16)],
        compiler_params=params(60),
        name="up",
    )(rows, w)


def down_kernel(per, rank_ref, hid_ref, *refs):
    out_ref = refs[-1]
    blocks = refs[:-1]
    units = blocks[0].shape[0]
    total = None
    for turn, block in enumerate(blocks):
        at = lax.rem(rank_ref[0] + turn, len(blocks))
        some = hid_ref[:, pl.ds(pl.multiple_of(at * units, units), units)]
        term = dot(some, block[...])
        total = term if total is None else total + term
    total = total.astype(BF16)
    count = total.shape[0]

    @pl.when(pl.program_id(0) == 0)
    def _():
        out_ref[...] = dot(halves_to_rows(count, per, 0), total).astype(BF16)

    @pl.when(pl.program_id(0) == 1)
    def _():
        out_ref[...] += dot(halves_to_rows(count, per, 1), total).astype(BF16)


def down_call(rank, hidden, blocks, per):
    rows, units = hidden.shape
    few, half = blocks[0].shape
    cols = half // 2
    return pl.pallas_call(
        functools.partial(down_kernel, per),
        grid=(2,),
        in_specs=[smem(), pl.BlockSpec((rows, units), lambda i: (0, 0))]
        + [pl.BlockSpec((few, cols), lambda i: (0, i))] * len(blocks),
        out_specs=pl.BlockSpec((2 * rows, cols), lambda i: (0, 0)),
        out_shape=jax.ShapeDtypeStruct((2 * rows, cols), BF16),
        compiler_params=params(60),
        name="down",
    )(rank, hidden, *blocks)


def combine_kernel(per, rank_ref, gates_ref, picks_ref, counts_ref, own_ref, other_ref, out_ref):
    rank = rank_ref[0]
    tokens = gates_ref.shape[0]
    experts = gates_ref.shape[1]
    picks = picks_ref[...].astype(F32)
    counts = counts_ref[...].astype(F32)
    shape = (experts, 2 * experts * per)
    expand = ones_where(
        quotient(lax.broadcasted_iota(jnp.int32, shape, 1), 2 * per)
        == lax.broadcasted_iota(jnp.int32, shape, 0)
    )
    wide = dot(gates_ref[...].astype(BF16), expand)
    token = lax.broadcasted_iota(jnp.int32, wide.shape, 0)
    which = row_half(wide.shape, per, 1)
    partner = rank + 1 - 2 * lax.rem(rank, 2)
    cols = own_ref.shape[1]
    sums = [None, None]
    for who, rows_ref in ((rank, own_ref), (partner, other_ref)):
        row = slot_row(picks, counts, who * per, per)
        weight = jnp.where(token == row, wide, 0.0)
        for half in range(2):
            term = dot(jnp.where(which == half, weight, 0.0).astype(BF16), rows_ref[...])
            sums[half] = term if sums[half] is None else sums[half] + term
    for half in range(2):
        out_ref[:, half * cols : (half + 1) * cols] = sums[half].astype(BF16)


def combine_call(rank, gates, picks_t, counts_t, own, other, per):
    half = 2 * own.shape[1]
    vmem = pl.BlockSpec(memory_space=pltpu.VMEM)
    return pl.pallas_call(
        functools.partial(combine_kernel, per),
        in_specs=[smem()] + [vmem] * 5,
        out_specs=vmem,
        out_shape=jax.ShapeDtypeStruct((gates.shape[0], half), BF16),
        compiler_params=params(16),
        name="combine",
    )(rank, gates, picks_t, counts_t, own, other)


def final_kernel(step_ref, share_ref, gate_ref, parts_ref, out_ref):
    gate = gate_ref[pl.ds(step_ref[0], 1), :]
    half = parts_ref.shape[2]
    for b in range(2):
        cols = slice(b * half, (b + 1) * half)
        mixture = parts_ref[b].astype(F32) + parts_ref[b + 2].astype(F32)
        out_ref[:, cols] = (share_ref[:, cols] + gate[:, cols] * mixture).astype(BF16)


def final_call(step, share, modulation, parts):
    rows, width = share.shape
    return pl.pallas_call(
        final_kernel,
        grid=(1,),
        in_specs=[
            smem(),
            pl.BlockSpec((rows, width), lambda i: (0, 0)),
            pl.BlockSpec((modulation.shape[0], width), lambda i: (0, 5)),
            pl.BlockSpec(parts.shape, lambda i: (0, 0, 0)),
        ],
        out_specs=pl.BlockSpec((rows, width), lambda i: (0, 0)),
        out_shape=jax.ShapeDtypeStruct((rows, width), BF16),
        compiler_params=params(16),
        name="final",
    )(step, share, modulation, parts)


def on_device(
    frames_in,
    step_index,
    modulation,
    qkv_weight,
    qk_gain,
    out_weight,
    router_weight,
    expert_up,
    expert_down,
    picks,
    counts,
):
    _, position_count, model_width = frames_in.shape
    ffn = lax.axis_size("ffn")
    seq = lax.axis_size("seq")
    rank = lax.axis_index("ffn").astype(jnp.int32)
    rank_arr = rank.reshape(1)
    head_size = qk_gain.shape[1]
    share_len = position_count // ffn
    slot_count = picks.shape[2]
    per = slot_count // ffn
    half = model_width // 2
    x = frames_in[0]
    picks_t = jnp.transpose(picks, (1, 2, 0))[0]
    counts_t = jnp.transpose(counts, (1, 0))

    def over_seq(values):
        return lax.all_to_all(values, "seq", split_axis=0, concat_axis=0, tiled=True)

    def over_ffn(values):
        return lax.all_to_all(values, "ffn", split_axis=0, concat_axis=0, tiled=True)

    place = lax.axis_index("seq").astype(jnp.int32)
    core = lax.rem(place, 2)
    lanes = 4
    stride = seq // lanes
    lane = place // stride
    some = out_weight.shape[0] // (2 * lanes)
    out_own = lax.dynamic_slice_in_dim(out_weight, (core * lanes + lane) * some, some, 0)
    up_full = lax.all_gather(expert_up, "ffn", axis=0, tiled=True)
    down = expert_down[0]
    side = lax.rem(rank, 2)
    same_half = lax.dynamic_slice_in_dim(down, side * half, half, 1)
    other_half = lax.dynamic_slice_in_dim(down, (1 - side) * half, half, 1)

    def from_turn(values, turn):
        return lax.ppermute(values, "ffn", [((i + turn) % ffn, i) for i in range(ffn)])

    out_rows = [out_own] + [from_turn(out_own, turn) for turn in range(1, ffn)]
    blocks = [
        same_half,
        from_turn(other_half, 1),
        from_turn(same_half, 2),
        from_turn(other_half, 3),
    ]

    stacked = qkv_call(step_index, x, modulation, jnp.transpose(qkv_weight, (1, 0, 2)), qk_gain)
    stacked = over_seq(stacked)
    few = position_count // seq
    attended = attention_call(stacked, few, head_size, ffn)
    attended, out_rows = lax.optimization_barrier((attended, out_rows))
    out_rows = jnp.concatenate(out_rows, axis=0)

    def from_lane(values, turn):
        pairs = [((i + turn * stride) % seq, i) for i in range(seq)]
        return lax.ppermute(values, "seq", pairs)

    out_blocks = [out_rows] + [from_lane(out_rows, turn) for turn in range(1, lanes)]
    swap = [(i, i ^ 1) for i in range(seq)]
    out_blocks = out_blocks + [lax.ppermute(b, "seq", swap) for b in out_blocks]
    every = lax.all_to_all(attended, ("seq", "ffn"), split_axis=0, concat_axis=0, tiled=True)
    outgoing, gates, share = mix_call(
        rank_arr, core.reshape(1), lane.reshape(1), step_index, every, out_blocks, x, modulation,
        jnp.transpose(router_weight, (1, 0)), picks_t, per, share_len, few,
    )
    near = (blocks[1], blocks[3])
    outgoing, near = lax.optimization_barrier((outgoing, near))
    blocks[1], blocks[3] = near
    expert_tokens = over_seq(outgoing)
    hidden = up_call(expert_tokens, up_full, per)
    hidden_other = lax.ppermute(hidden, "ffn", [(i, i ^ 1) for i in range(ffn)])
    own = over_seq(down_call(rank_arr, hidden, blocks, per))
    other = over_seq(down_call(rank_arr, hidden_other, blocks, per))
    mixture = combine_call(rank_arr, gates, picks_t, counts_t, own, other, per)
    parts = over_ffn(mixture).reshape(ffn, share_len, half)
    return final_call(step_index, share, modulation, parts)[None]


def solution(mesh):
    in_specs = (
        P("seq", None, None),
        P("seq"),
        P(),
        P(None, None, "ffn"),
        P(),
        P("ffn", None),
        P(),
        P("seq", None, "ffn"),
        P("seq", "ffn", None),
        P(None, "seq", None),
        P(None, "seq"),
    )
    out_specs = P("seq", "ffn", None)
    return jax.shard_map(
        on_device, mesh=mesh, in_specs=in_specs, out_specs=out_specs, check_vma=False
    )
```

```python
import functools

import jax
import jax.numpy as jnp
from jax import lax
from jax.experimental import pallas as pl
from jax.experimental.pallas import tpu as pltpu
from jax.sharding import PartitionSpec as P

BF16 = jnp.bfloat16
F32 = jnp.float32
MIB = 1 << 20


def dot(a, b):
    return jnp.dot(a, b, preferred_element_type=F32)


def dot_t(a, b):
    return lax.dot_general(a, b, (((1,), (1,)), ((), ())), preferred_element_type=F32)


def dot_l(a, b):
    return lax.dot_general(a, b, (((0,), (0,)), ((), ())), preferred_element_type=F32)


def layer_norm(values):
    mean = jnp.mean(values, -1, keepdims=True)
    centred = values - mean
    variance = jnp.mean(centred * centred, -1, keepdims=True)
    return centred * lax.rsqrt(variance + 1e-06)


def quotient(values, by):
    return lax.shift_right_logical(values, by.bit_length() - 1)


def remainder(values, by):
    return values & (by - 1)


def smem():
    return pl.BlockSpec(memory_space=pltpu.SMEM)


def params(mib, **kw):
    return pltpu.CompilerParams(vmem_limit_bytes=mib * MIB, **kw)


def qkv_kernel(step_ref, x_ref, mod_ref, w_ref, gain_ref, out_ref):
    step = step_ref[0]
    width = x_ref.shape[1]
    shift = mod_ref[pl.ds(step, 1), :width]
    scale = mod_ref[pl.ds(step, 1), width:]
    normed = (layer_norm(x_ref[...].astype(F32)) * (1.0 + scale) + shift).astype(BF16)
    inner = w_ref.shape[2]
    head = gain_ref.shape[1]
    for part in range(3):
        proj = dot(normed, w_ref[part])
        if part < 2:
            gain = gain_ref[part : part + 1, :]
            for h in range(inner // head):
                one = proj[:, h * head : (h + 1) * head]
                one = one * lax.rsqrt(jnp.mean(one * one, -1, keepdims=True) + 1e-06) * gain
                lo = part * inner + h * head
                out_ref[:, lo : lo + head] = one.astype(BF16)
        else:
            out_ref[:, part * inner : (part + 1) * inner] = proj.astype(BF16)


def qkv_call(step, x, modulation, w, gain):
    tokens, width = x.shape
    inner = w.shape[2]
    rows = 256
    return pl.pallas_call(
        qkv_kernel,
        grid=(tokens // rows,),
        in_specs=[
            smem(),
            pl.BlockSpec((rows, width), lambda i: (i, 0)),
            pl.BlockSpec((modulation.shape[0], 2 * width), lambda i: (0, 0)),
            pl.BlockSpec(w.shape, lambda i: (0, 0, 0)),
            pl.BlockSpec(gain.shape, lambda i: (0, 0)),
        ],
        out_specs=pl.BlockSpec((rows, 3 * inner), lambda i: (i, 0)),
        out_shape=jax.ShapeDtypeStruct((tokens, 3 * inner), BF16),
        compiler_params=params(60),
        name="qkv",
    )(step, x, modulation, w, gain)


def attention_kernel(few, head, copies, in_ref, out_ref):
    rows = in_ref.shape[0]
    inner = out_ref.shape[1]
    row_pos = remainder(lax.broadcasted_iota(jnp.int32, (rows, rows), 0), few)
    col_pos = remainder(lax.broadcasted_iota(jnp.int32, (rows, rows), 1), few)
    same = row_pos == col_pos
    for h in range(inner // head):
        lo = h * head
        q = in_ref[:, lo : lo + head]
        k = in_ref[:, inner + lo : inner + lo + head]
        v = in_ref[:, 2 * inner + lo : 2 * inner + lo + head]
        raised = jnp.where(same, jnp.exp(dot_t(q, k) * head ** (-0.5)), 0.0)
        probs = (raised / jnp.sum(raised, -1, keepdims=True)).astype(BF16)
        each = dot(probs, v).reshape(rows // few, 1, few, head)
        each = jnp.broadcast_to(each, (rows // few, copies, few, head))
        out_ref[:, lo : lo + head] = each.reshape(copies * rows, head).astype(BF16)


def attention_call(stacked, few, head, copies):
    rows, wide = stacked.shape
    return pl.pallas_call(
        functools.partial(attention_kernel, few, head, copies),
        out_shape=jax.ShapeDtypeStruct((copies * rows, wide // 3), BF16),
        compiler_params=params(16),
        name="attention",
    )(stacked)


def spread(values, per):
    experts = values.shape[1]
    shape = (experts, experts * per)
    expand = (
        quotient(lax.broadcasted_iota(jnp.int32, shape, 1), per)
        == lax.broadcasted_iota(jnp.int32, shape, 0)
    ).astype(F32)
    return jnp.dot(values, expand, precision=lax.Precision.HIGHEST, preferred_element_type=F32)


def slot_row(picks_f32, counts_f32, first, per):
    wide = spread(picks_f32, 2 * per)
    slot = lax.broadcasted_iota(jnp.int32, wide.shape, 0)
    wanted = first + remainder(lax.broadcasted_iota(jnp.int32, wide.shape, 1), per)
    mine = slot == wanted
    if counts_f32 is not None:
        limit = spread(counts_f32, 2 * per)
        wide = jnp.where(slot.astype(F32) < limit, wide, -1.0)
    return jnp.sum(jnp.where(mine, wide, 0.0), axis=0, keepdims=True).astype(jnp.int32)


def row_half(shape, per, dim):
    return remainder(quotient(lax.broadcasted_iota(jnp.int32, shape, dim), per), 2)


def ones_where(mask):
    return mask.astype(F32).astype(BF16)


def halves_to_rows(count, per, half):
    shape = (2 * count, count)
    row = lax.broadcasted_iota(jnp.int32, shape, 0)
    col = lax.broadcasted_iota(jnp.int32, shape, 1)
    wanted = (quotient(col, per) * 2 + half) * per + remainder(col, per)
    return ones_where(row == wanted)


def mix_kernel(
    per, pieces, parts, few, rank_ref, core_ref, lane_ref, step_ref, att_ref, x_ref, gate_ref, shift_ref,
    scale_ref, router_ref, picks_ref, *refs
):
    blocks = refs[: 2 * pieces]
    disp_ref, gates_ref, share_ref, hidden_ref, normed_ref, w_ref, sems = refs[2 * pieces :]
    step = step_ref[0]
    rank = rank_ref[0]
    tile = pl.program_id(0)
    rows = x_ref.shape[0]
    inner = att_ref.shape[1]

    @pl.when(tile == 0)
    def _():
        some = blocks[0].shape[0] // parts
        copies = []
        for number, block in enumerate(blocks):
            which, turn = divmod(number, pieces)
            half = lax.rem(core_ref[0] + which, 2)
            place = lax.rem(lane_ref[0] + turn, pieces)
            for part_turn in range(parts):
                part = lax.rem(rank + part_turn, parts)
                to = pl.multiple_of(part * inner + half * (inner // 2) + place * some, some)
                copies.append(
                    pltpu.make_async_copy(
                        block.at[pl.ds(part_turn * some, some), :],
                        w_ref.at[pl.ds(to, some), :],
                        sems.at[number * parts + part_turn],
                    )
                )
        for copy in copies:
            copy.start()
        for copy in copies:
            copy.wait()

    gate = gate_ref[pl.ds(step, 1), :]
    shift = shift_ref[pl.ds(step, 1), :]
    scale = scale_ref[pl.ds(step, 1), :]
    split = att_ref[...].astype(F32).reshape(rows // few, parts, few, inner)
    every = jnp.concatenate(
        [split[:, part].reshape(rows, inner).astype(BF16) for part in range(parts)], axis=1
    )
    mixed = dot(every, w_ref[...])
    hidden = x_ref[...].astype(F32) + gate * mixed
    hidden_ref[...] = hidden
    normed = (layer_norm(hidden) * (1.0 + scale) + shift).astype(BF16)
    normed_ref[pl.ds(pl.multiple_of(tile * rows, rows), rows), :] = normed
    gates_ref[...] = jax.nn.sigmoid(dot_t(normed, router_ref[...]))
    share = share_ref.shape[0]
    each = rows // share

    @pl.when(tile == rank // each)
    def _():
        start = pl.multiple_of((rank % each) * share, share)
        share_ref[...] = hidden_ref[pl.ds(start, share), :]

    @pl.when(tile == pl.num_programs(0) - 1)
    def _():
        row = slot_row(picks_ref[...].astype(F32), None, rank * per, per)
        tokens = normed_ref.shape[0]
        shape = (tokens, row.shape[1])
        picked = lax.broadcasted_iota(jnp.int32, shape, 0) == row
        half = row_half(shape, per, 1)
        cols = disp_ref.shape[1]
        disp_ref[...] = (
            dot_l(ones_where(picked & (half == 0)), normed_ref[:, :cols])
            + dot_l(ones_where(picked & (half == 1)), normed_ref[:, cols:])
        ).astype(BF16)


def mix_call(
    rank, core, lane, step, att, blocks, x, modulation, router_t, picks_t, per, share, few
):
    tokens, width = x.shape
    parts = att.shape[0] // tokens
    inner = att.shape[1]
    experts = router_t.shape[0]
    steps = modulation.shape[0]
    rows = 256
    return pl.pallas_call(
        functools.partial(mix_kernel, per, len(blocks) // 2, parts, few),
        grid=(tokens // rows,),
        in_specs=[smem()] * 4
        + [
            pl.BlockSpec((parts * rows, inner), lambda i: (i, 0)),
            pl.BlockSpec((rows, width), lambda i: (i, 0)),
            pl.BlockSpec((steps, width), lambda i: (0, 2)),
            pl.BlockSpec((steps, width), lambda i: (0, 3)),
            pl.BlockSpec((steps, width), lambda i: (0, 4)),
            pl.BlockSpec(router_t.shape, lambda i: (0, 0)),
            pl.BlockSpec(picks_t.shape, lambda i: (0, 0)),
        ]
        + [pl.BlockSpec(memory_space=pl.ANY)] * len(blocks),
        out_specs=[
            pl.BlockSpec((2 * experts * per, width // 2), lambda i: (0, 0)),
            pl.BlockSpec((rows, experts), lambda i: (i, 0)),
            pl.BlockSpec((share, width), lambda i: (0, 0)),
        ],
        out_shape=[
            jax.ShapeDtypeStruct((2 * experts * per, width // 2), BF16),
            jax.ShapeDtypeStruct((tokens, experts), F32),
            jax.ShapeDtypeStruct((share, width), F32),
        ],
        scratch_shapes=[
            pltpu.VMEM((rows, width), F32),
            pltpu.VMEM((tokens, width), BF16),
            pltpu.VMEM((parts * inner, width), BF16),
            pltpu.SemaphoreType.DMA((len(blocks) * parts,)),
        ],
        compiler_params=params(60),
        name="mix",
    )(
        rank, core, lane, step, att, x, modulation, modulation, modulation, router_t, picks_t,
        *blocks,
    )


def up_kernel(per, rows_ref, w_ref, out_ref, tok_ref):
    @pl.when(pl.program_id(0) == 0)
    def _():
        count = tok_ref.shape[0]
        cols = rows_ref.shape[1]
        for half in range(2):
            pick = halves_to_rows(count, per, half)
            tok_ref[:, half * cols : (half + 1) * cols] = dot_l(pick, rows_ref[...]).astype(BF16)

    out_ref[...] = jax.nn.gelu(dot(tok_ref[...], w_ref[0])).astype(BF16)


def up_call(rows, w, per):
    parts, width, units = w.shape
    count = rows.shape[0] // 2
    return pl.pallas_call(
        functools.partial(up_kernel, per),
        grid=(parts,),
        in_specs=[
            pl.BlockSpec(rows.shape, lambda i: (0, 0)),
            pl.BlockSpec((1, width, units), lambda i: (i, 0, 0)),
        ],
        out_specs=pl.BlockSpec((count, units), lambda i: (0, i)),
        out_shape=jax.ShapeDtypeStruct((count, parts * units), BF16),
        scratch_shapes=[pltpu.VMEM((count, width), BF16)],
        compiler_params=params(60),
        name="up",
    )(rows, w)


def down_kernel(per, rank_ref, hid_ref, *refs):
    out_ref = refs[-1]
    blocks = refs[:-1]
    units = blocks[0].shape[0]
    total = None
    for turn, block in enumerate(blocks):
        at = lax.rem(rank_ref[0] + turn, len(blocks))
        some = hid_ref[:, pl.ds(pl.multiple_of(at * units, units), units)]
        term = dot(some, block[...])
        total = term if total is None else total + term
    total = total.astype(BF16)
    count = total.shape[0]

    @pl.when(pl.program_id(0) == 0)
    def _():
        out_ref[...] = dot(halves_to_rows(count, per, 0), total).astype(BF16)

    @pl.when(pl.program_id(0) == 1)
    def _():
        out_ref[...] += dot(halves_to_rows(count, per, 1), total).astype(BF16)


def down_call(rank, hidden, blocks, per):
    rows, units = hidden.shape
    few, half = blocks[0].shape
    cols = half // 2
    return pl.pallas_call(
        functools.partial(down_kernel, per),
        grid=(2,),
        in_specs=[smem(), pl.BlockSpec((rows, units), lambda i: (0, 0))]
        + [pl.BlockSpec((few, cols), lambda i: (0, i))] * len(blocks),
        out_specs=pl.BlockSpec((2 * rows, cols), lambda i: (0, 0)),
        out_shape=jax.ShapeDtypeStruct((2 * rows, cols), BF16),
        compiler_params=params(60),
        name="down",
    )(rank, hidden, *blocks)


def combine_kernel(per, rank_ref, gates_ref, picks_ref, counts_ref, own_ref, other_ref, out_ref):
    rank = rank_ref[0]
    tokens = gates_ref.shape[0]
    experts = gates_ref.shape[1]
    picks = picks_ref[...].astype(F32)
    counts = counts_ref[...].astype(F32)
    shape = (experts, 2 * experts * per)
    expand = ones_where(
        quotient(lax.broadcasted_iota(jnp.int32, shape, 1), 2 * per)
        == lax.broadcasted_iota(jnp.int32, shape, 0)
    )
    wide = dot(gates_ref[...].astype(BF16), expand)
    token = lax.broadcasted_iota(jnp.int32, wide.shape, 0)
    which = row_half(wide.shape, per, 1)
    partner = rank + 1 - 2 * lax.rem(rank, 2)
    cols = own_ref.shape[1]
    sums = [None, None]
    for who, rows_ref in ((rank, own_ref), (partner, other_ref)):
        row = slot_row(picks, counts, who * per, per)
        weight = jnp.where(token == row, wide, 0.0)
        for half in range(2):
            term = dot(jnp.where(which == half, weight, 0.0).astype(BF16), rows_ref[...])
            sums[half] = term if sums[half] is None else sums[half] + term
    for half in range(2):
        out_ref[:, half * cols : (half + 1) * cols] = sums[half].astype(BF16)


def combine_call(rank, gates, picks_t, counts_t, own, other, per):
    half = 2 * own.shape[1]
    vmem = pl.BlockSpec(memory_space=pltpu.VMEM)
    return pl.pallas_call(
        functools.partial(combine_kernel, per),
        in_specs=[smem()] + [vmem] * 5,
        out_specs=vmem,
        out_shape=jax.ShapeDtypeStruct((gates.shape[0], half), BF16),
        compiler_params=params(16),
        name="combine",
    )(rank, gates, picks_t, counts_t, own, other)


def final_kernel(step_ref, share_ref, gate_ref, parts_ref, out_ref):
    gate = gate_ref[pl.ds(step_ref[0], 1), :]
    half = parts_ref.shape[2]
    for b in range(2):
        cols = slice(b * half, (b + 1) * half)
        mixture = parts_ref[b].astype(F32) + parts_ref[b + 2].astype(F32)
        out_ref[:, cols] = (share_ref[:, cols] + gate[:, cols] * mixture).astype(BF16)


def final_call(step, share, modulation, parts):
    rows, width = share.shape
    return pl.pallas_call(
        final_kernel,
        grid=(1,),
        in_specs=[
            smem(),
            pl.BlockSpec((rows, width), lambda i: (0, 0)),
            pl.BlockSpec((modulation.shape[0], width), lambda i: (0, 5)),
            pl.BlockSpec(parts.shape, lambda i: (0, 0, 0)),
        ],
        out_specs=pl.BlockSpec((rows, width), lambda i: (0, 0)),
        out_shape=jax.ShapeDtypeStruct((rows, width), BF16),
        compiler_params=params(16),
        name="final",
    )(step, share, modulation, parts)


def on_device(
    frames_in,
    step_index,
    modulation,
    qkv_weight,
    qk_gain,
    out_weight,
    router_weight,
    expert_up,
    expert_down,
    picks,
    counts,
):
    _, position_count, model_width = frames_in.shape
    ffn = lax.axis_size("ffn")
    seq = lax.axis_size("seq")
    rank = lax.axis_index("ffn").astype(jnp.int32)
    rank_arr = rank.reshape(1)
    head_size = qk_gain.shape[1]
    share_len = position_count // ffn
    slot_count = picks.shape[2]
    per = slot_count // ffn
    half = model_width // 2
    x = frames_in[0]
    picks_t = jnp.transpose(picks, (1, 2, 0))[0]
    counts_t = jnp.transpose(counts, (1, 0))

    def over_seq(values):
        return lax.all_to_all(values, "seq", split_axis=0, concat_axis=0, tiled=True)

    def over_ffn(values):
        return lax.all_to_all(values, "ffn", split_axis=0, concat_axis=0, tiled=True)

    place = lax.axis_index("seq").astype(jnp.int32)
    core = lax.rem(place, 2)
    lanes = 4
    stride = seq // lanes
    lane = place // stride
    some = out_weight.shape[0] // (2 * lanes)
    out_own = lax.dynamic_slice_in_dim(out_weight, (core * lanes + lane) * some, some, 0)
    up_full = lax.all_gather(expert_up, "ffn", axis=0, tiled=True)
    down = expert_down[0]
    side = lax.rem(rank, 2)
    same_half = lax.dynamic_slice_in_dim(down, side * half, half, 1)
    other_half = lax.dynamic_slice_in_dim(down, (1 - side) * half, half, 1)

    def from_turn(values, turn):
        return lax.ppermute(values, "ffn", [((i + turn) % ffn, i) for i in range(ffn)])

    out_rows = [out_own] + [from_turn(out_own, turn) for turn in range(1, ffn)]
    blocks = [
        same_half,
        from_turn(other_half, 1),
        from_turn(same_half, 2),
        from_turn(other_half, 3),
    ]

    stacked = qkv_call(step_index, x, modulation, jnp.transpose(qkv_weight, (1, 0, 2)), qk_gain)
    stacked, out_rows = lax.optimization_barrier((stacked, out_rows))
    stacked = over_seq(stacked)
    few = position_count // seq
    attended = attention_call(stacked, few, head_size, ffn)
    out_rows = jnp.concatenate(out_rows, axis=0)

    def from_lane(values, turn):
        pairs = [((i + turn * stride) % seq, i) for i in range(seq)]
        return lax.ppermute(values, "seq", pairs)

    out_blocks = [out_rows] + [from_lane(out_rows, turn) for turn in range(1, lanes)]
    attended, out_blocks = lax.optimization_barrier((attended, out_blocks))
    swap = [(i, i ^ 1) for i in range(seq)]
    out_blocks = out_blocks + [lax.ppermute(b, "seq", swap) for b in out_blocks]
    every = lax.all_to_all(attended, ("seq", "ffn"), split_axis=0, concat_axis=0, tiled=True)
    outgoing, gates, share = mix_call(
        rank_arr, core.reshape(1), lane.reshape(1), step_index, every, out_blocks, x, modulation,
        jnp.transpose(router_weight, (1, 0)), picks_t, per, share_len, few,
    )
    outgoing, blocks[1] = lax.optimization_barrier((outgoing, blocks[1]))
    expert_tokens = over_seq(outgoing)
    hidden = up_call(expert_tokens, up_full, per)
    hidden_other = lax.ppermute(hidden, "ffn", [(i, i ^ 1) for i in range(ffn)])
    own = over_seq(down_call(rank_arr, hidden, blocks, per))
    other = over_seq(down_call(rank_arr, hidden_other, blocks, per))
    mixture = combine_call(rank_arr, gates, picks_t, counts_t, own, other, per)
    parts = over_ffn(mixture).reshape(ffn, share_len, half)
    return final_call(step_index, share, modulation, parts)[None]


def solution(mesh):
    in_specs = (
        P("seq", None, None),
        P("seq"),
        P(),
        P(None, None, "ffn"),
        P(),
        P("ffn", None),
        P(),
        P("seq", None, "ffn"),
        P("seq", "ffn", None),
        P(None, "seq", None),
        P(None, "seq"),
    )
    out_specs = P("seq", "ffn", None)
    return jax.shard_map(
        on_device, mesh=mesh, in_specs=in_specs, out_specs=out_specs, check_vma=False
    )
```

```python
import functools

import jax
import jax.numpy as jnp
from jax import lax
from jax.experimental import pallas as pl
from jax.experimental.pallas import tpu as pltpu
from jax.sharding import PartitionSpec as P

BF16 = jnp.bfloat16
F32 = jnp.float32
MIB = 1 << 20


def dot(a, b):
    return jnp.dot(a, b, preferred_element_type=F32)


def dot_t(a, b):
    return lax.dot_general(a, b, (((1,), (1,)), ((), ())), preferred_element_type=F32)


def layer_norm(values):
    mean = jnp.mean(values, -1, keepdims=True)
    centred = values - mean
    variance = jnp.mean(centred * centred, -1, keepdims=True)
    return centred * lax.rsqrt(variance + 1e-06)


def quotient(values, by):
    return lax.shift_right_logical(values, by.bit_length() - 1)


def remainder(values, by):
    return values & (by - 1)


def smem():
    return pl.BlockSpec(memory_space=pltpu.SMEM)


def params(mib, **kw):
    return pltpu.CompilerParams(vmem_limit_bytes=mib * MIB, **kw)


def qkv_kernel(step_ref, x_ref, mod_ref, w_ref, gain_ref, out_ref):
    step = step_ref[0]
    width = x_ref.shape[1]
    shift = mod_ref[pl.ds(step, 1), :width]
    scale = mod_ref[pl.ds(step, 1), width:]
    normed = (layer_norm(x_ref[...].astype(F32)) * (1.0 + scale) + shift).astype(BF16)
    inner = w_ref.shape[2]
    head = gain_ref.shape[1]
    for part in range(3):
        proj = dot(normed, w_ref[part])
        if part < 2:
            gain = gain_ref[part : part + 1, :]
            for h in range(inner // head):
                one = proj[:, h * head : (h + 1) * head]
                one = one * lax.rsqrt(jnp.mean(one * one, -1, keepdims=True) + 1e-06) * gain
                lo = part * inner + h * head
                out_ref[:, lo : lo + head] = one.astype(BF16)
        else:
            out_ref[:, part * inner : (part + 1) * inner] = proj.astype(BF16)


def qkv_call(step, x, modulation, w, gain):
    tokens, width = x.shape
    inner = w.shape[2]
    rows = 256
    return pl.pallas_call(
        qkv_kernel,
        grid=(tokens // rows,),
        in_specs=[
            smem(),
            pl.BlockSpec((rows, width), lambda i: (i, 0)),
            pl.BlockSpec((modulation.shape[0], 2 * width), lambda i: (0, 0)),
            pl.BlockSpec(w.shape, lambda i: (0, 0, 0)),
            pl.BlockSpec(gain.shape, lambda i: (0, 0)),
        ],
        out_specs=pl.BlockSpec((rows, 3 * inner), lambda i: (i, 0)),
        out_shape=jax.ShapeDtypeStruct((tokens, 3 * inner), BF16),
        compiler_params=params(60),
        name="qkv",
    )(step, x, modulation, w, gain)


def attention_kernel(few, head, copies, in_ref, out_ref):
    rows = in_ref.shape[0]
    inner = out_ref.shape[1]
    row_pos = remainder(lax.broadcasted_iota(jnp.int32, (rows, rows), 0), few)
    col_pos = remainder(lax.broadcasted_iota(jnp.int32, (rows, rows), 1), few)
    same = row_pos == col_pos
    for h in range(inner // head):
        lo = h * head
        q = in_ref[:, lo : lo + head]
        k = in_ref[:, inner + lo : inner + lo + head]
        v = in_ref[:, 2 * inner + lo : 2 * inner + lo + head]
        raised = jnp.where(same, jnp.exp(dot_t(q, k) * head ** (-0.5)), 0.0)
        probs = (raised / jnp.sum(raised, -1, keepdims=True)).astype(BF16)
        each = dot(probs, v).reshape(rows // few, 1, few, head)
        each = jnp.broadcast_to(each, (rows // few, copies, few, head))
        out_ref[:, lo : lo + head] = each.reshape(copies * rows, head).astype(BF16)


def attention_call(stacked, few, head, copies):
    rows, wide = stacked.shape
    return pl.pallas_call(
        functools.partial(attention_kernel, few, head, copies),
        out_shape=jax.ShapeDtypeStruct((copies * rows, wide // 3), BF16),
        compiler_params=params(16),
        name="attention",
    )(stacked)


def spread(values, per):
    experts = values.shape[1]
    shape = (experts, experts * per)
    expand = (
        quotient(lax.broadcasted_iota(jnp.int32, shape, 1), per)
        == lax.broadcasted_iota(jnp.int32, shape, 0)
    ).astype(F32)
    return jnp.dot(values, expand, precision=lax.Precision.HIGHEST, preferred_element_type=F32)


def slot_row(picks_f32, counts_f32, first, per):
    wide = spread(picks_f32, 2 * per)
    slot = lax.broadcasted_iota(jnp.int32, wide.shape, 0)
    wanted = first + remainder(lax.broadcasted_iota(jnp.int32, wide.shape, 1), per)
    limit = spread(counts_f32, 2 * per)
    wide = jnp.where(slot.astype(F32) < limit, wide, -1.0)
    return jnp.sum(jnp.where(slot == wanted, wide, 0.0), axis=0, keepdims=True).astype(jnp.int32)


def slot_column(picks_f32, first, per):
    experts = picks_f32.shape[1]
    shape = (experts * 2 * per, experts)
    expand = (
        quotient(lax.broadcasted_iota(jnp.int32, shape, 0), 2 * per)
        == lax.broadcasted_iota(jnp.int32, shape, 1)
    ).astype(F32)
    wide = lax.dot_general(
        expand, picks_f32, (((1,), (1,)), ((), ())),
        precision=lax.Precision.HIGHEST, preferred_element_type=F32,
    )
    wanted = first + remainder(lax.broadcasted_iota(jnp.int32, wide.shape, 0), per)
    mine = lax.broadcasted_iota(jnp.int32, wide.shape, 1) == wanted
    return jnp.sum(jnp.where(mine, wide, 0.0), axis=1, keepdims=True).astype(jnp.int32)


def rows_to_half(count, per, half):
    shape = (count, 2 * count)
    row = lax.broadcasted_iota(jnp.int32, shape, 0)
    col = lax.broadcasted_iota(jnp.int32, shape, 1)
    wanted = (quotient(row, per) * 2 + half) * per + remainder(row, per)
    return ones_where(col == wanted)


def row_half(shape, per, dim):
    return remainder(quotient(lax.broadcasted_iota(jnp.int32, shape, dim), per), 2)


def ones_where(mask):
    return mask.astype(F32).astype(BF16)


def halves_to_rows(count, per, half):
    shape = (2 * count, count)
    row = lax.broadcasted_iota(jnp.int32, shape, 0)
    col = lax.broadcasted_iota(jnp.int32, shape, 1)
    wanted = (quotient(col, per) * 2 + half) * per + remainder(col, per)
    return ones_where(row == wanted)


def mix_kernel(
    per, pieces, parts, few, rank_ref, core_ref, lane_ref, step_ref, att_ref, x_ref, gate_ref, shift_ref,
    scale_ref, router_ref, picks_ref, *refs
):
    blocks = refs[: 2 * pieces]
    disp_ref, gates_ref, share_ref, hidden_ref, normed_ref, w_ref, sems = refs[2 * pieces :]
    step = step_ref[0]
    rank = rank_ref[0]
    tile = pl.program_id(0)
    rows = x_ref.shape[0]
    inner = att_ref.shape[1]

    @pl.when(tile == 0)
    def _():
        some = blocks[0].shape[0] // parts
        copies = []
        for number, block in enumerate(blocks):
            which, turn = divmod(number, pieces)
            half = lax.rem(core_ref[0] + which, 2)
            place = lax.rem(lane_ref[0] + turn, pieces)
            for part_turn in range(parts):
                part = lax.rem(rank + part_turn, parts)
                to = pl.multiple_of(part * inner + half * (inner // 2) + place * some, some)
                copies.append(
                    pltpu.make_async_copy(
                        block.at[pl.ds(part_turn * some, some), :],
                        w_ref.at[pl.ds(to, some), :],
                        sems.at[number * parts + part_turn],
                    )
                )
        for copy in copies:
            copy.start()
        for copy in copies:
            copy.wait()

    gate = gate_ref[pl.ds(step, 1), :]
    shift = shift_ref[pl.ds(step, 1), :]
    scale = scale_ref[pl.ds(step, 1), :]
    split = att_ref[...].astype(F32).reshape(rows // few, parts, few, inner)
    every = jnp.concatenate(
        [split[:, part].reshape(rows, inner).astype(BF16) for part in range(parts)], axis=1
    )
    mixed = dot(every, w_ref[...])
    hidden = x_ref[...].astype(F32) + gate * mixed
    hidden_ref[...] = hidden
    normed = (layer_norm(hidden) * (1.0 + scale) + shift).astype(BF16)
    normed_ref[pl.ds(pl.multiple_of(tile * rows, rows), rows), :] = normed
    gates_ref[...] = jax.nn.sigmoid(dot_t(normed, router_ref[...]))
    share = share_ref.shape[0]
    each = rows // share

    @pl.when(tile == rank // each)
    def _():
        start = pl.multiple_of((rank % each) * share, share)
        share_ref[...] = hidden_ref[pl.ds(start, share), :]

    @pl.when(tile == pl.num_programs(0) - 1)
    def _():
        column = slot_column(picks_ref[...].astype(F32), rank * per, per)
        tokens = normed_ref.shape[0]
        shape = (column.shape[0], tokens)
        picked = lax.broadcasted_iota(jnp.int32, shape, 1) == column
        half = row_half(shape, per, 0)
        cols = disp_ref.shape[1]
        disp_ref[...] = (
            dot(ones_where(picked & (half == 0)), normed_ref[:, :cols])
            + dot(ones_where(picked & (half == 1)), normed_ref[:, cols:])
        ).astype(BF16)


def mix_call(
    rank, core, lane, step, att, blocks, x, modulation, router_t, picks_t, per, share, few
):
    tokens, width = x.shape
    parts = att.shape[0] // tokens
    inner = att.shape[1]
    experts = router_t.shape[0]
    steps = modulation.shape[0]
    rows = 256
    return pl.pallas_call(
        functools.partial(mix_kernel, per, len(blocks) // 2, parts, few),
        grid=(tokens // rows,),
        in_specs=[smem()] * 4
        + [
            pl.BlockSpec((parts * rows, inner), lambda i: (i, 0)),
            pl.BlockSpec((rows, width), lambda i: (i, 0)),
            pl.BlockSpec((steps, width), lambda i: (0, 2)),
            pl.BlockSpec((steps, width), lambda i: (0, 3)),
            pl.BlockSpec((steps, width), lambda i: (0, 4)),
            pl.BlockSpec(router_t.shape, lambda i: (0, 0)),
            pl.BlockSpec(picks_t.shape, lambda i: (0, 0)),
        ]
        + [pl.BlockSpec(memory_space=pl.ANY)] * len(blocks),
        out_specs=[
            pl.BlockSpec((2 * experts * per, width // 2), lambda i: (0, 0)),
            pl.BlockSpec((rows, experts), lambda i: (i, 0)),
            pl.BlockSpec((share, width), lambda i: (0, 0)),
        ],
        out_shape=[
            jax.ShapeDtypeStruct((2 * experts * per, width // 2), BF16),
            jax.ShapeDtypeStruct((tokens, experts), F32),
            jax.ShapeDtypeStruct((share, width), F32),
        ],
        scratch_shapes=[
            pltpu.VMEM((rows, width), F32),
            pltpu.VMEM((tokens, width), BF16),
            pltpu.VMEM((parts * inner, width), BF16),
            pltpu.SemaphoreType.DMA((len(blocks) * parts,)),
        ],
        compiler_params=params(62),
        name="mix",
    )(
        rank, core, lane, step, att, x, modulation, modulation, modulation, router_t, picks_t,
        *blocks,
    )


def up_kernel(per, rows_ref, w_ref, out_ref, tok_ref):
    @pl.when(pl.program_id(0) == 0)
    def _():
        count = tok_ref.shape[0]
        cols = rows_ref.shape[1]
        for half in range(2):
            pick = rows_to_half(count, per, half)
            tok_ref[:, half * cols : (half + 1) * cols] = dot(pick, rows_ref[...]).astype(BF16)

    out_ref[...] = jax.nn.gelu(dot(tok_ref[...], w_ref[0])).astype(BF16)


def up_call(rows, w, per):
    parts, width, units = w.shape
    count = rows.shape[0] // 2
    return pl.pallas_call(
        functools.partial(up_kernel, per),
        grid=(parts,),
        in_specs=[
            pl.BlockSpec(rows.shape, lambda i: (0, 0)),
            pl.BlockSpec((1, width, units), lambda i: (i, 0, 0)),
        ],
        out_specs=pl.BlockSpec((count, units), lambda i: (0, i)),
        out_shape=jax.ShapeDtypeStruct((count, parts * units), BF16),
        scratch_shapes=[pltpu.VMEM((count, width), BF16)],
        compiler_params=params(60),
        name="up",
    )(rows, w)


def down_kernel(per, places, rank_ref, hid_ref, *refs):
    out_ref = refs[-1]
    parts = 4
    units = hid_ref.shape[1] // parts
    total = None
    for (turn, row), block in zip(places, refs[:-1]):
        at = lax.rem(rank_ref[0] + turn, parts) * units + row
        some = hid_ref[:, pl.ds(pl.multiple_of(at, 128), block.shape[0])]
        term = dot(some, block[...])
        total = term if total is None else total + term
    total = total.astype(BF16)
    count = total.shape[0]

    @pl.when(pl.program_id(0) == 0)
    def _():
        out_ref[...] = dot(halves_to_rows(count, per, 0), total).astype(BF16)

    @pl.when(pl.program_id(0) == 1)
    def _():
        out_ref[...] += dot(halves_to_rows(count, per, 1), total).astype(BF16)


def down_call(rank, hidden, blocks, places, per):
    rows, units = hidden.shape
    half = blocks[0].shape[1]
    cols = half // 2
    return pl.pallas_call(
        functools.partial(down_kernel, per, places),
        grid=(2,),
        in_specs=[smem(), pl.BlockSpec((rows, units), lambda i: (0, 0))]
        + [pl.BlockSpec((block.shape[0], cols), lambda i: (0, i)) for block in blocks],
        out_specs=pl.BlockSpec((2 * rows, cols), lambda i: (0, 0)),
        out_shape=jax.ShapeDtypeStruct((2 * rows, cols), BF16),
        compiler_params=params(60),
        name="down",
    )(rank, hidden, *blocks)


def combine_kernel(per, rank_ref, gates_ref, picks_ref, counts_ref, own_ref, other_ref, out_ref):
    rank = rank_ref[0]
    tokens = gates_ref.shape[0]
    experts = gates_ref.shape[1]
    picks = picks_ref[...].astype(F32)
    counts = counts_ref[...].astype(F32)
    shape = (experts, 2 * experts * per)
    expand = ones_where(
        quotient(lax.broadcasted_iota(jnp.int32, shape, 1), 2 * per)
        == lax.broadcasted_iota(jnp.int32, shape, 0)
    )
    wide = dot(gates_ref[...].astype(BF16), expand)
    token = lax.broadcasted_iota(jnp.int32, wide.shape, 0)
    which = row_half(wide.shape, per, 1)
    partner = rank + 1 - 2 * lax.rem(rank, 2)
    cols = own_ref.shape[1]
    sums = [None, None]
    for who, rows_ref in ((rank, own_ref), (partner, other_ref)):
        row = slot_row(picks, counts, who * per, per)
        weight = jnp.where(token == row, wide, 0.0)
        for half in range(2):
            term = dot(jnp.where(which == half, weight, 0.0).astype(BF16), rows_ref[...])
            sums[half] = term if sums[half] is None else sums[half] + term
    for half in range(2):
        out_ref[:, half * cols : (half + 1) * cols] = sums[half].astype(BF16)


def combine_call(rank, gates, picks_t, counts_t, own, other, per):
    half = 2 * own.shape[1]
    vmem = pl.BlockSpec(memory_space=pltpu.VMEM)
    return pl.pallas_call(
        functools.partial(combine_kernel, per),
        in_specs=[smem()] + [vmem] * 5,
        out_specs=vmem,
        out_shape=jax.ShapeDtypeStruct((gates.shape[0], half), BF16),
        compiler_params=params(16),
        name="combine",
    )(rank, gates, picks_t, counts_t, own, other)


def final_kernel(step_ref, share_ref, gate_ref, parts_ref, out_ref):
    gate = gate_ref[pl.ds(step_ref[0], 1), :]
    half = parts_ref.shape[2]
    for b in range(2):
        cols = slice(b * half, (b + 1) * half)
        mixture = parts_ref[b].astype(F32) + parts_ref[b + 2].astype(F32)
        out_ref[:, cols] = (share_ref[:, cols] + gate[:, cols] * mixture).astype(BF16)


def final_call(step, share, modulation, parts):
    rows, width = share.shape
    return pl.pallas_call(
        final_kernel,
        grid=(1,),
        in_specs=[
            smem(),
            pl.BlockSpec((rows, width), lambda i: (0, 0)),
            pl.BlockSpec((modulation.shape[0], width), lambda i: (0, 5)),
            pl.BlockSpec(parts.shape, lambda i: (0, 0, 0)),
        ],
        out_specs=pl.BlockSpec((rows, width), lambda i: (0, 0)),
        out_shape=jax.ShapeDtypeStruct((rows, width), BF16),
        compiler_params=params(16),
        name="final",
    )(step, share, modulation, parts)


def on_device(
    frames_in,
    step_index,
    modulation,
    qkv_weight,
    qk_gain,
    out_weight,
    router_weight,
    expert_up,
    expert_down,
    picks,
    counts,
):
    _, position_count, model_width = frames_in.shape
    ffn = lax.axis_size("ffn")
    seq = lax.axis_size("seq")
    rank = lax.axis_index("ffn").astype(jnp.int32)
    rank_arr = rank.reshape(1)
    head_size = qk_gain.shape[1]
    share_len = position_count // ffn
    slot_count = picks.shape[2]
    per = slot_count // ffn
    half = model_width // 2
    x = frames_in[0]
    picks_t = jnp.transpose(picks, (1, 2, 0))[0]
    counts_t = jnp.transpose(counts, (1, 0))

    def over_seq(values):
        return lax.all_to_all(values, "seq", split_axis=0, concat_axis=0, tiled=True)

    def over_ffn(values):
        return lax.all_to_all(values, "ffn", split_axis=0, concat_axis=0, tiled=True)

    place = lax.axis_index("seq").astype(jnp.int32)
    core = lax.rem(place, 2)
    lanes = 4
    stride = seq // lanes
    lane = place // stride
    some = out_weight.shape[0] // (2 * lanes)
    out_own = lax.dynamic_slice_in_dim(out_weight, (core * lanes + lane) * some, some, 0)
    up_full = lax.all_gather(expert_up, "ffn", axis=0, tiled=True)
    down = expert_down[0]
    side = lax.rem(rank, 2)
    same_half = lax.dynamic_slice_in_dim(down, side * half, half, 1)

    def from_turn(values, turn):
        return lax.ppermute(values, "ffn", [((i + turn) % ffn, i) for i in range(ffn)])

    out_rows = [out_own] + [from_turn(out_own, turn) for turn in range(1, ffn)]
    few_units = down.shape[0] // 2
    first, second = (
        lax.dynamic_slice(down, (at, (1 - side) * half), (few_units, half))
        for at in (0, few_units)
    )
    places = ((0, 0), (1, 0), (3, 0), (2, 0), (1, few_units), (3, few_units))
    early = (from_turn(first, 1), from_turn(first, 3))
    late = (from_turn(same_half, 2), from_turn(second, 1), from_turn(second, 3))

    stacked = qkv_call(step_index, x, modulation, jnp.transpose(qkv_weight, (1, 0, 2)), qk_gain)
    stacked = over_seq(stacked)
    few = position_count // seq
    attended = attention_call(stacked, few, head_size, ffn)
    out_rows = jnp.concatenate(out_rows, axis=0)
    attended, out_rows = lax.optimization_barrier((attended, out_rows))

    def from_lane(values, turn):
        pairs = [((i + turn * stride) % seq, i) for i in range(seq)]
        return lax.ppermute(values, "seq", pairs)

    out_blocks = [out_rows] + [from_lane(out_rows, turn) for turn in range(1, lanes)]
    swap = [(i, i ^ 1) for i in range(seq)]
    out_blocks = out_blocks + [lax.ppermute(b, "seq", swap) for b in out_blocks]
    every = lax.all_to_all(attended, ("seq", "ffn"), split_axis=0, concat_axis=0, tiled=True)
    every, early = lax.optimization_barrier((every, early))
    outgoing, gates, share = mix_call(
        rank_arr, core.reshape(1), lane.reshape(1), step_index, every, out_blocks, x, modulation,
        jnp.transpose(router_weight, (1, 0)), picks_t, per, share_len, few,
    )
    expert_tokens = over_seq(outgoing)
    blocks = (same_half,) + tuple(early) + late
    hidden = up_call(expert_tokens, up_full, per)
    hidden_other = lax.ppermute(hidden, "ffn", [(i, i ^ 1) for i in range(ffn)])
    own = over_seq(down_call(rank_arr, hidden, blocks, places, per))
    other = over_seq(down_call(rank_arr, hidden_other, blocks, places, per))
    mixture = combine_call(rank_arr, gates, picks_t, counts_t, own, other, per)
    parts = over_ffn(mixture).reshape(ffn, share_len, half)
    return final_call(step_index, share, modulation, parts)[None]


def solution(mesh):
    in_specs = (
        P("seq", None, None),
        P("seq"),
        P(),
        P(None, None, "ffn"),
        P(),
        P("ffn", None),
        P(),
        P("seq", None, "ffn"),
        P("seq", "ffn", None),
        P(None, "seq", None),
        P(None, "seq"),
    )
    out_specs = P("seq", "ffn", None)
    return jax.shard_map(
        on_device, mesh=mesh, in_specs=in_specs, out_specs=out_specs, check_vma=False
    )
```

```python
import functools

import jax
import jax.numpy as jnp
from jax import lax
from jax.experimental import pallas as pl
from jax.experimental.pallas import tpu as pltpu
from jax.sharding import PartitionSpec as P

BF16 = jnp.bfloat16
F32 = jnp.float32
MIB = 1 << 20


def dot(a, b):
    return jnp.dot(a, b, preferred_element_type=F32)


def dot_t(a, b):
    return lax.dot_general(a, b, (((1,), (1,)), ((), ())), preferred_element_type=F32)


def layer_norm(values):
    mean = jnp.mean(values, -1, keepdims=True)
    centred = values - mean
    variance = jnp.mean(centred * centred, -1, keepdims=True)
    return centred * lax.rsqrt(variance + 1e-06)


def quotient(values, by):
    return lax.shift_right_logical(values, by.bit_length() - 1)


def remainder(values, by):
    return values & (by - 1)


def smem():
    return pl.BlockSpec(memory_space=pltpu.SMEM)


def params(mib, **kw):
    return pltpu.CompilerParams(vmem_limit_bytes=mib * MIB, **kw)


def qkv_kernel(step_ref, x_ref, mod_ref, w_ref, gain_ref, out_ref):
    step = step_ref[0]
    width = x_ref.shape[1]
    shift = mod_ref[pl.ds(step, 1), :width]
    scale = mod_ref[pl.ds(step, 1), width:]
    normed = (layer_norm(x_ref[...].astype(F32)) * (1.0 + scale) + shift).astype(BF16)
    inner = w_ref.shape[2]
    head = gain_ref.shape[1]
    for part in range(3):
        proj = dot(normed, w_ref[part])
        if part < 2:
            gain = gain_ref[part : part + 1, :]
            for h in range(inner // head):
                one = proj[:, h * head : (h + 1) * head]
                one = one * lax.rsqrt(jnp.mean(one * one, -1, keepdims=True) + 1e-06) * gain
                lo = part * inner + h * head
                out_ref[:, lo : lo + head] = one.astype(BF16)
        else:
            out_ref[:, part * inner : (part + 1) * inner] = proj.astype(BF16)


def qkv_call(step, x, modulation, w, gain):
    tokens, width = x.shape
    inner = w.shape[2]
    rows = 256
    return pl.pallas_call(
        qkv_kernel,
        grid=(tokens // rows,),
        in_specs=[
            smem(),
            pl.BlockSpec((rows, width), lambda i: (i, 0)),
            pl.BlockSpec((modulation.shape[0], 2 * width), lambda i: (0, 0)),
            pl.BlockSpec(w.shape, lambda i: (0, 0, 0)),
            pl.BlockSpec(gain.shape, lambda i: (0, 0)),
        ],
        out_specs=pl.BlockSpec((rows, 3 * inner), lambda i: (i, 0)),
        out_shape=jax.ShapeDtypeStruct((tokens, 3 * inner), BF16),
        compiler_params=params(60),
        name="qkv",
    )(step, x, modulation, w, gain)


def attention_kernel(few, head, copies, in_ref, out_ref):
    rows = in_ref.shape[0]
    inner = out_ref.shape[1]
    row_pos = remainder(lax.broadcasted_iota(jnp.int32, (rows, rows), 0), few)
    col_pos = remainder(lax.broadcasted_iota(jnp.int32, (rows, rows), 1), few)
    same = row_pos == col_pos
    for h in range(inner // head):
        lo = h * head
        q = in_ref[:, lo : lo + head]
        k = in_ref[:, inner + lo : inner + lo + head]
        v = in_ref[:, 2 * inner + lo : 2 * inner + lo + head]
        raised = jnp.where(same, jnp.exp(dot_t(q, k) * head ** (-0.5)), 0.0)
        probs = (raised / jnp.sum(raised, -1, keepdims=True)).astype(BF16)
        each = dot(probs, v).reshape(rows // few, 1, few, head)
        each = jnp.broadcast_to(each, (rows // few, copies, few, head))
        out_ref[:, lo : lo + head] = each.reshape(copies * rows, head).astype(BF16)


def attention_call(stacked, few, head, copies):
    rows, wide = stacked.shape
    return pl.pallas_call(
        functools.partial(attention_kernel, few, head, copies),
        out_shape=jax.ShapeDtypeStruct((copies * rows, wide // 3), BF16),
        compiler_params=params(16),
        name="attention",
    )(stacked)


def spread(values, per):
    experts = values.shape[1]
    shape = (experts, experts * per)
    expand = (
        quotient(lax.broadcasted_iota(jnp.int32, shape, 1), per)
        == lax.broadcasted_iota(jnp.int32, shape, 0)
    ).astype(F32)
    return jnp.dot(values, expand, precision=lax.Precision.HIGHEST, preferred_element_type=F32)


def slot_row(picks_f32, counts_f32, first, per):
    wide = spread(picks_f32, 2 * per)
    slot = lax.broadcasted_iota(jnp.int32, wide.shape, 0)
    wanted = first + remainder(lax.broadcasted_iota(jnp.int32, wide.shape, 1), per)
    limit = spread(counts_f32, 2 * per)
    wide = jnp.where(slot.astype(F32) < limit, wide, -1.0)
    return jnp.sum(jnp.where(slot == wanted, wide, 0.0), axis=0, keepdims=True).astype(jnp.int32)


def slot_column(picks_f32, first, per):
    experts = picks_f32.shape[1]
    shape = (experts * 2 * per, experts)
    expand = (
        quotient(lax.broadcasted_iota(jnp.int32, shape, 0), 2 * per)
        == lax.broadcasted_iota(jnp.int32, shape, 1)
    ).astype(F32)
    wide = lax.dot_general(
        expand, picks_f32, (((1,), (1,)), ((), ())),
        precision=lax.Precision.HIGHEST, preferred_element_type=F32,
    )
    wanted = first + remainder(lax.broadcasted_iota(jnp.int32, wide.shape, 0), per)
    mine = lax.broadcasted_iota(jnp.int32, wide.shape, 1) == wanted
    return jnp.sum(jnp.where(mine, wide, 0.0), axis=1, keepdims=True).astype(jnp.int32)


def rows_to_half(count, per, half):
    shape = (count, 2 * count)
    row = lax.broadcasted_iota(jnp.int32, shape, 0)
    col = lax.broadcasted_iota(jnp.int32, shape, 1)
    wanted = (quotient(row, per) * 2 + half) * per + remainder(row, per)
    return ones_where(col == wanted)


def row_half(shape, per, dim):
    return remainder(quotient(lax.broadcasted_iota(jnp.int32, shape, dim), per), 2)


def ones_where(mask):
    return mask.astype(F32).astype(BF16)


def halves_to_rows(count, per, half):
    shape = (2 * count, count)
    row = lax.broadcasted_iota(jnp.int32, shape, 0)
    col = lax.broadcasted_iota(jnp.int32, shape, 1)
    wanted = (quotient(col, per) * 2 + half) * per + remainder(col, per)
    return ones_where(row == wanted)


def mix_kernel(
    per, pieces, parts, few, rank_ref, core_ref, lane_ref, step_ref, att_ref, x_ref, gate_ref, shift_ref,
    scale_ref, router_ref, picks_ref, *refs
):
    blocks = refs[: 2 * pieces]
    (disp_ref, gates_ref, share_ref, hidden_ref, normed_ref, w_ref, every_ref, pick_ref,
     sems) = refs[2 * pieces :]
    step = step_ref[0]
    rank = rank_ref[0]
    tile = pl.program_id(0)
    rows = x_ref.shape[0]
    inner = att_ref.shape[1]

    def weight_copies():
        some = blocks[0].shape[0] // parts
        for number, block in enumerate(blocks):
            which, turn = divmod(number, pieces)
            half = lax.rem(core_ref[0] + which, 2)
            place = lax.rem(lane_ref[0] + turn, pieces)
            for part_turn in range(parts):
                part = lax.rem(rank + part_turn, parts)
                to = pl.multiple_of(part * inner + half * (inner // 2) + place * some, some)
                yield pltpu.make_async_copy(
                    block.at[pl.ds(part_turn * some, some), :],
                    w_ref.at[pl.ds(to, some), :],
                    sems.at[number * parts + part_turn],
                )

    def pick_matrices():
        column = slot_column(picks_ref[...].astype(F32), rank * per, per)
        shape = (column.shape[0], normed_ref.shape[0])
        picked = lax.broadcasted_iota(jnp.int32, shape, 1) == column
        half = row_half(shape, per, 0)
        for which in range(2):
            pick_ref[which] = ones_where(picked & (half == which))

    def join():
        split = att_ref[...].astype(F32).reshape(rows // few, parts, few, inner)
        for part in range(parts):
            every_ref[:, part * inner : (part + 1) * inner] = (
                split[:, part].reshape(rows, inner).astype(BF16)
            )

    @pl.when(tile == 0)
    def _():
        copies = list(weight_copies())
        for copy in copies:
            copy.start()
        join()
        pick_matrices()
        for copy in copies:
            copy.wait()

    @pl.when(tile > 0)
    def _():
        join()

    gate = gate_ref[pl.ds(step, 1), :]
    shift = shift_ref[pl.ds(step, 1), :]
    scale = scale_ref[pl.ds(step, 1), :]
    mixed = dot(every_ref[...], w_ref[...])
    hidden = x_ref[...].astype(F32) + gate * mixed
    hidden_ref[...] = hidden
    normed = (layer_norm(hidden) * (1.0 + scale) + shift).astype(BF16)
    normed_ref[pl.ds(pl.multiple_of(tile * rows, rows), rows), :] = normed
    gates_ref[...] = jax.nn.sigmoid(dot_t(normed, router_ref[...]))
    share = share_ref.shape[0]
    each = rows // share

    @pl.when(tile == rank // each)
    def _():
        start = pl.multiple_of((rank % each) * share, share)
        share_ref[...] = hidden_ref[pl.ds(start, share), :]

    @pl.when(tile == pl.num_programs(0) - 1)
    def _():
        cols = disp_ref.shape[1]
        disp_ref[...] = (
            dot(pick_ref[0], normed_ref[:, :cols]) + dot(pick_ref[1], normed_ref[:, cols:])
        ).astype(BF16)


def mix_call(
    rank, core, lane, step, att, blocks, x, modulation, router_t, picks_t, per, share, few
):
    tokens, width = x.shape
    parts = att.shape[0] // tokens
    inner = att.shape[1]
    experts = router_t.shape[0]
    steps = modulation.shape[0]
    rows = 256
    return pl.pallas_call(
        functools.partial(mix_kernel, per, len(blocks) // 2, parts, few),
        grid=(tokens // rows,),
        in_specs=[smem()] * 4
        + [
            pl.BlockSpec((parts * rows, inner), lambda i: (i, 0)),
            pl.BlockSpec((rows, width), lambda i: (i, 0)),
            pl.BlockSpec((steps, width), lambda i: (0, 2)),
            pl.BlockSpec((steps, width), lambda i: (0, 3)),
            pl.BlockSpec((steps, width), lambda i: (0, 4)),
            pl.BlockSpec(router_t.shape, lambda i: (0, 0)),
            pl.BlockSpec(picks_t.shape, lambda i: (0, 0)),
        ]
        + [pl.BlockSpec(memory_space=pl.ANY)] * len(blocks),
        out_specs=[
            pl.BlockSpec((2 * experts * per, width // 2), lambda i: (0, 0)),
            pl.BlockSpec((rows, experts), lambda i: (i, 0)),
            pl.BlockSpec((share, width), lambda i: (0, 0)),
        ],
        out_shape=[
            jax.ShapeDtypeStruct((2 * experts * per, width // 2), BF16),
            jax.ShapeDtypeStruct((tokens, experts), F32),
            jax.ShapeDtypeStruct((share, width), F32),
        ],
        scratch_shapes=[
            pltpu.VMEM((rows, width), F32),
            pltpu.VMEM((tokens, width), BF16),
            pltpu.VMEM((parts * inner, width), BF16),
            pltpu.VMEM((rows, parts * inner), BF16),
            pltpu.VMEM((2, 2 * experts * per, tokens), BF16),
            pltpu.SemaphoreType.DMA((len(blocks) * parts,)),
        ],
        compiler_params=params(62),
        name="mix",
    )(
        rank, core, lane, step, att, x, modulation, modulation, modulation, router_t, picks_t,
        *blocks,
    )


def up_kernel(per, rows_ref, w_ref, out_ref, tok_ref):
    @pl.when(pl.program_id(0) == 0)
    def _():
        count = tok_ref.shape[0]
        cols = rows_ref.shape[1]
        for half in range(2):
            pick = rows_to_half(count, per, half)
            tok_ref[:, half * cols : (half + 1) * cols] = dot(pick, rows_ref[...]).astype(BF16)

    out_ref[...] = jax.nn.gelu(dot(tok_ref[...], w_ref[0])).astype(BF16)


def up_call(rows, w, per):
    parts, width, units = w.shape
    count = rows.shape[0] // 2
    return pl.pallas_call(
        functools.partial(up_kernel, per),
        grid=(parts,),
        in_specs=[
            pl.BlockSpec(rows.shape, lambda i: (0, 0)),
            pl.BlockSpec((1, width, units), lambda i: (i, 0, 0)),
        ],
        out_specs=pl.BlockSpec((count, units), lambda i: (0, i)),
        out_shape=jax.ShapeDtypeStruct((count, parts * units), BF16),
        scratch_shapes=[pltpu.VMEM((count, width), BF16)],
        compiler_params=params(60),
        name="up",
    )(rows, w)


def down_kernel(per, places, rank_ref, hid_ref, *refs):
    out_ref = refs[-1]
    parts = 4
    units = hid_ref.shape[1] // parts
    total = None
    for (turn, row), block in zip(places, refs[:-1]):
        at = lax.rem(rank_ref[0] + turn, parts) * units + row
        some = hid_ref[:, pl.ds(pl.multiple_of(at, 128), block.shape[0])]
        term = dot(some, block[...])
        total = term if total is None else total + term
    total = total.astype(BF16)
    count = total.shape[0]

    @pl.when(pl.program_id(0) == 0)
    def _():
        out_ref[...] = dot(halves_to_rows(count, per, 0), total).astype(BF16)

    @pl.when(pl.program_id(0) == 1)
    def _():
        out_ref[...] += dot(halves_to_rows(count, per, 1), total).astype(BF16)


def down_call(rank, hidden, blocks, places, per):
    rows, units = hidden.shape
    half = blocks[0].shape[1]
    cols = half // 2
    return pl.pallas_call(
        functools.partial(down_kernel, per, places),
        grid=(2,),
        in_specs=[smem(), pl.BlockSpec((rows, units), lambda i: (0, 0))]
        + [pl.BlockSpec((block.shape[0], cols), lambda i: (0, i)) for block in blocks],
        out_specs=pl.BlockSpec((2 * rows, cols), lambda i: (0, 0)),
        out_shape=jax.ShapeDtypeStruct((2 * rows, cols), BF16),
        compiler_params=params(60),
        name="down",
    )(rank, hidden, *blocks)


def combine_kernel(per, rank_ref, gates_ref, picks_ref, counts_ref, own_ref, other_ref, out_ref):
    rank = rank_ref[0]
    tokens = gates_ref.shape[0]
    experts = gates_ref.shape[1]
    picks = picks_ref[...].astype(F32)
    counts = counts_ref[...].astype(F32)
    shape = (experts, 2 * experts * per)
    expand = ones_where(
        quotient(lax.broadcasted_iota(jnp.int32, shape, 1), 2 * per)
        == lax.broadcasted_iota(jnp.int32, shape, 0)
    )
    wide = dot(gates_ref[...].astype(BF16), expand)
    token = lax.broadcasted_iota(jnp.int32, wide.shape, 0)
    which = row_half(wide.shape, per, 1)
    partner = rank + 1 - 2 * lax.rem(rank, 2)
    cols = own_ref.shape[1]
    sums = [None, None]
    for who, rows_ref in ((rank, own_ref), (partner, other_ref)):
        row = slot_row(picks, counts, who * per, per)
        weight = jnp.where(token == row, wide, 0.0)
        for half in range(2):
            term = dot(jnp.where(which == half, weight, 0.0).astype(BF16), rows_ref[...])
            sums[half] = term if sums[half] is None else sums[half] + term
    for half in range(2):
        out_ref[:, half * cols : (half + 1) * cols] = sums[half].astype(BF16)


def combine_call(rank, gates, picks_t, counts_t, own, other, per):
    half = 2 * own.shape[1]
    vmem = pl.BlockSpec(memory_space=pltpu.VMEM)
    return pl.pallas_call(
        functools.partial(combine_kernel, per),
        in_specs=[smem()] + [vmem] * 5,
        out_specs=vmem,
        out_shape=jax.ShapeDtypeStruct((gates.shape[0], half), BF16),
        compiler_params=params(16),
        name="combine",
    )(rank, gates, picks_t, counts_t, own, other)


def final_kernel(step_ref, share_ref, gate_ref, parts_ref, out_ref):
    gate = gate_ref[pl.ds(step_ref[0], 1), :]
    half = parts_ref.shape[2]
    for b in range(2):
        cols = slice(b * half, (b + 1) * half)
        mixture = parts_ref[b].astype(F32) + parts_ref[b + 2].astype(F32)
        out_ref[:, cols] = (share_ref[:, cols] + gate[:, cols] * mixture).astype(BF16)


def final_call(step, share, modulation, parts):
    rows, width = share.shape
    return pl.pallas_call(
        final_kernel,
        grid=(1,),
        in_specs=[
            smem(),
            pl.BlockSpec((rows, width), lambda i: (0, 0)),
            pl.BlockSpec((modulation.shape[0], width), lambda i: (0, 5)),
            pl.BlockSpec(parts.shape, lambda i: (0, 0, 0)),
        ],
        out_specs=pl.BlockSpec((rows, width), lambda i: (0, 0)),
        out_shape=jax.ShapeDtypeStruct((rows, width), BF16),
        compiler_params=params(16),
        name="final",
    )(step, share, modulation, parts)


def on_device(
    frames_in,
    step_index,
    modulation,
    qkv_weight,
    qk_gain,
    out_weight,
    router_weight,
    expert_up,
    expert_down,
    picks,
    counts,
):
    _, position_count, model_width = frames_in.shape
    ffn = lax.axis_size("ffn")
    seq = lax.axis_size("seq")
    rank = lax.axis_index("ffn").astype(jnp.int32)
    rank_arr = rank.reshape(1)
    head_size = qk_gain.shape[1]
    share_len = position_count // ffn
    slot_count = picks.shape[2]
    per = slot_count // ffn
    half = model_width // 2
    x = frames_in[0]
    picks_t = jnp.transpose(picks, (1, 2, 0))[0]
    counts_t = jnp.transpose(counts, (1, 0))

    def over_seq(values):
        return lax.all_to_all(values, "seq", split_axis=0, concat_axis=0, tiled=True)

    def over_ffn(values):
        return lax.all_to_all(values, "ffn", split_axis=0, concat_axis=0, tiled=True)

    place = lax.axis_index("seq").astype(jnp.int32)
    core = lax.rem(place, 2)
    lanes = 4
    stride = seq // lanes
    lane = place // stride
    some = out_weight.shape[0] // (2 * lanes)
    out_own = lax.dynamic_slice_in_dim(out_weight, (core * lanes + lane) * some, some, 0)
    up_full = lax.all_gather(expert_up, "ffn", axis=0, tiled=True)
    down = expert_down[0]
    side = lax.rem(rank, 2)
    same_half = lax.dynamic_slice_in_dim(down, side * half, half, 1)

    def from_turn(values, turn):
        return lax.ppermute(values, "ffn", [((i + turn) % ffn, i) for i in range(ffn)])

    out_rows = [out_own] + [from_turn(out_own, turn) for turn in range(1, ffn)]
    few_units = down.shape[0] // 2
    first, second = (
        lax.dynamic_slice(down, (at, (1 - side) * half), (few_units, half))
        for at in (0, few_units)
    )
    places = ((0, 0), (1, 0), (3, 0), (2, 0), (1, few_units), (3, few_units))
    early = (from_turn(first, 1), from_turn(first, 3))
    late = (from_turn(same_half, 2), from_turn(second, 1), from_turn(second, 3))

    stacked = qkv_call(step_index, x, modulation, jnp.transpose(qkv_weight, (1, 0, 2)), qk_gain)
    stacked, out_rows = lax.optimization_barrier((stacked, out_rows))
    stacked = over_seq(stacked)
    few = position_count // seq
    attended = attention_call(stacked, few, head_size, ffn)
    out_rows = jnp.concatenate(out_rows, axis=0)

    def from_lane(values, turn):
        pairs = [((i + turn * stride) % seq, i) for i in range(seq)]
        return lax.ppermute(values, "seq", pairs)

    out_blocks = [out_rows] + [from_lane(out_rows, turn) for turn in range(1, lanes)]
    attended, out_blocks[2] = lax.optimization_barrier((attended, out_blocks[2]))
    swap = [(i, i ^ 1) for i in range(seq)]
    out_blocks = out_blocks + [lax.ppermute(b, "seq", swap) for b in out_blocks]
    every = lax.all_to_all(attended, ("seq", "ffn"), split_axis=0, concat_axis=0, tiled=True)
    outgoing, gates, share = mix_call(
        rank_arr, core.reshape(1), lane.reshape(1), step_index, every, out_blocks, x, modulation,
        jnp.transpose(router_weight, (1, 0)), picks_t, per, share_len, few,
    )
    outgoing, early = lax.optimization_barrier((outgoing, early))
    expert_tokens = over_seq(outgoing)
    blocks = (same_half,) + tuple(early) + late
    hidden = up_call(expert_tokens, up_full, per)
    hidden_other = lax.ppermute(hidden, "ffn", [(i, i ^ 1) for i in range(ffn)])
    own = over_seq(down_call(rank_arr, hidden, blocks, places, per))
    other = over_seq(down_call(rank_arr, hidden_other, blocks, places, per))
    mixture = combine_call(rank_arr, gates, picks_t, counts_t, own, other, per)
    parts = over_ffn(mixture).reshape(ffn, share_len, half)
    return final_call(step_index, share, modulation, parts)[None]


def solution(mesh):
    in_specs = (
        P("seq", None, None),
        P("seq"),
        P(),
        P(None, None, "ffn"),
        P(),
        P("ffn", None),
        P(),
        P("seq", None, "ffn"),
        P("seq", "ffn", None),
        P(None, "seq", None),
        P(None, "seq"),
    )
    out_specs = P("seq", "ffn", None)
    return jax.shard_map(
        on_device, mesh=mesh, in_specs=in_specs, out_specs=out_specs, check_vma=False
    )
```

```python
import functools

import jax
import jax.numpy as jnp
from jax import lax
from jax.experimental import pallas as pl
from jax.experimental.pallas import tpu as pltpu
from jax.sharding import PartitionSpec as P

BF16 = jnp.bfloat16
F32 = jnp.float32
MIB = 1 << 20


def dot(a, b):
    return jnp.dot(a, b, preferred_element_type=F32)


def dot_t(a, b):
    return lax.dot_general(a, b, (((1,), (1,)), ((), ())), preferred_element_type=F32)


def layer_norm(values):
    mean = jnp.mean(values, -1, keepdims=True)
    centred = values - mean
    variance = jnp.mean(centred * centred, -1, keepdims=True)
    return centred * lax.rsqrt(variance + 1e-06)


def quotient(values, by):
    return lax.shift_right_logical(values, by.bit_length() - 1)


def remainder(values, by):
    return values & (by - 1)


def smem():
    return pl.BlockSpec(memory_space=pltpu.SMEM)


def params(mib, **kw):
    return pltpu.CompilerParams(vmem_limit_bytes=mib * MIB, **kw)


def qkv_kernel(step_ref, x_ref, mod_ref, w_ref, gain_ref, out_ref):
    step = step_ref[0]
    width = x_ref.shape[1]
    shift = mod_ref[pl.ds(step, 1), :width]
    scale = mod_ref[pl.ds(step, 1), width:]
    normed = (layer_norm(x_ref[...].astype(F32)) * (1.0 + scale) + shift).astype(BF16)
    inner = w_ref.shape[2]
    head = gain_ref.shape[1]
    for part in range(3):
        proj = dot(normed, w_ref[part])
        if part < 2:
            gain = gain_ref[part : part + 1, :]
            for h in range(inner // head):
                one = proj[:, h * head : (h + 1) * head]
                one = one * lax.rsqrt(jnp.mean(one * one, -1, keepdims=True) + 1e-06) * gain
                lo = part * inner + h * head
                out_ref[:, lo : lo + head] = one.astype(BF16)
        else:
            out_ref[:, part * inner : (part + 1) * inner] = proj.astype(BF16)


def qkv_call(step, x, modulation, w, gain):
    tokens, width = x.shape
    inner = w.shape[2]
    rows = 256
    return pl.pallas_call(
        qkv_kernel,
        grid=(tokens // rows,),
        in_specs=[
            smem(),
            pl.BlockSpec((rows, width), lambda i: (i, 0)),
            pl.BlockSpec((modulation.shape[0], 2 * width), lambda i: (0, 0)),
            pl.BlockSpec(w.shape, lambda i: (0, 0, 0)),
            pl.BlockSpec(gain.shape, lambda i: (0, 0)),
        ],
        out_specs=pl.BlockSpec((rows, 3 * inner), lambda i: (i, 0)),
        out_shape=jax.ShapeDtypeStruct((tokens, 3 * inner), BF16),
        compiler_params=params(60),
        name="qkv",
    )(step, x, modulation, w, gain)


def attention_kernel(few, head, copies, in_ref, out_ref):
    rows = in_ref.shape[0]
    inner = out_ref.shape[1]
    row_pos = remainder(lax.broadcasted_iota(jnp.int32, (rows, rows), 0), few)
    col_pos = remainder(lax.broadcasted_iota(jnp.int32, (rows, rows), 1), few)
    same = row_pos == col_pos
    for h in range(inner // head):
        lo = h * head
        q = in_ref[:, lo : lo + head]
        k = in_ref[:, inner + lo : inner + lo + head]
        v = in_ref[:, 2 * inner + lo : 2 * inner + lo + head]
        raised = jnp.where(same, jnp.exp(dot_t(q, k) * head ** (-0.5)), 0.0)
        probs = (raised / jnp.sum(raised, -1, keepdims=True)).astype(BF16)
        each = dot(probs, v).reshape(rows // few, 1, few, head)
        each = jnp.broadcast_to(each, (rows // few, copies, few, head))
        out_ref[:, lo : lo + head] = each.reshape(copies * rows, head).astype(BF16)


def attention_call(stacked, few, head, copies):
    rows, wide = stacked.shape
    return pl.pallas_call(
        functools.partial(attention_kernel, few, head, copies),
        out_shape=jax.ShapeDtypeStruct((copies * rows, wide // 3), BF16),
        compiler_params=params(16),
        name="attention",
    )(stacked)


def spread(values, per):
    experts = values.shape[1]
    shape = (experts, experts * per)
    expand = (
        quotient(lax.broadcasted_iota(jnp.int32, shape, 1), per)
        == lax.broadcasted_iota(jnp.int32, shape, 0)
    ).astype(F32)
    return jnp.dot(values, expand, precision=lax.Precision.HIGHEST, preferred_element_type=F32)


def slot_row(picks_f32, counts_f32, first, per):
    wide = spread(picks_f32, 2 * per)
    slot = lax.broadcasted_iota(jnp.int32, wide.shape, 0)
    wanted = first + remainder(lax.broadcasted_iota(jnp.int32, wide.shape, 1), per)
    limit = spread(counts_f32, 2 * per)
    wide = jnp.where(slot.astype(F32) < limit, wide, -1.0)
    return jnp.sum(jnp.where(slot == wanted, wide, 0.0), axis=0, keepdims=True).astype(jnp.int32)


def slot_column(picks_f32, first, per):
    experts = picks_f32.shape[1]
    shape = (experts * 2 * per, experts)
    expand = (
        quotient(lax.broadcasted_iota(jnp.int32, shape, 0), 2 * per)
        == lax.broadcasted_iota(jnp.int32, shape, 1)
    ).astype(F32)
    wide = lax.dot_general(
        expand, picks_f32, (((1,), (1,)), ((), ())),
        precision=lax.Precision.HIGHEST, preferred_element_type=F32,
    )
    wanted = first + remainder(lax.broadcasted_iota(jnp.int32, wide.shape, 0), per)
    mine = lax.broadcasted_iota(jnp.int32, wide.shape, 1) == wanted
    return jnp.sum(jnp.where(mine, wide, 0.0), axis=1, keepdims=True).astype(jnp.int32)


def rows_to_half(count, per, half):
    shape = (count, 2 * count)
    row = lax.broadcasted_iota(jnp.int32, shape, 0)
    col = lax.broadcasted_iota(jnp.int32, shape, 1)
    wanted = (quotient(row, per) * 2 + half) * per + remainder(row, per)
    return ones_where(col == wanted)


def row_half(shape, per, dim):
    return remainder(quotient(lax.broadcasted_iota(jnp.int32, shape, dim), per), 2)


def ones_where(mask):
    return mask.astype(F32).astype(BF16)


def halves_to_rows(count, per, half):
    shape = (2 * count, count)
    row = lax.broadcasted_iota(jnp.int32, shape, 0)
    col = lax.broadcasted_iota(jnp.int32, shape, 1)
    wanted = (quotient(col, per) * 2 + half) * per + remainder(col, per)
    return ones_where(row == wanted)


def mix_kernel(
    per, pieces, parts, few, rank_ref, core_ref, lane_ref, step_ref, att_ref, x_ref, gate_ref, shift_ref,
    scale_ref, router_ref, picks_ref, *refs
):
    blocks = refs[: 2 * pieces]
    (disp_ref, gates_ref, share_ref, hidden_ref, normed_ref, w_ref, every_ref, pick_ref,
     sems) = refs[2 * pieces :]
    step = step_ref[0]
    rank = rank_ref[0]
    tile = pl.program_id(0)
    rows = x_ref.shape[0]
    inner = att_ref.shape[1]

    def weight_copies():
        some = blocks[0].shape[0] // parts
        for number, block in enumerate(blocks):
            which, turn = divmod(number, pieces)
            half = lax.rem(core_ref[0] + which, 2)
            place = lax.rem(lane_ref[0] + turn, pieces)
            for part_turn in range(parts):
                part = lax.rem(rank + part_turn, parts)
                to = pl.multiple_of(part * inner + half * (inner // 2) + place * some, some)
                yield pltpu.make_async_copy(
                    block.at[pl.ds(part_turn * some, some), :],
                    w_ref.at[pl.ds(to, some), :],
                    sems.at[number * parts + part_turn],
                )

    def pick_matrices():
        column = slot_column(picks_ref[...].astype(F32), rank * per, per)
        shape = (column.shape[0], normed_ref.shape[0])
        picked = lax.broadcasted_iota(jnp.int32, shape, 1) == column
        half = row_half(shape, per, 0)
        for which in range(2):
            pick_ref[which] = ones_where(picked & (half == which))

    def join():
        split = att_ref[...].astype(F32).reshape(rows // few, parts, few, inner)
        for part in range(parts):
            every_ref[:, part * inner : (part + 1) * inner] = (
                split[:, part].reshape(rows, inner).astype(BF16)
            )

    @pl.when(tile == 0)
    def _():
        copies = list(weight_copies())
        for copy in copies:
            copy.start()
        join()
        pick_matrices()
        for copy in copies:
            copy.wait()

    @pl.when(tile > 0)
    def _():
        join()

    gate = gate_ref[pl.ds(step, 1), :]
    shift = shift_ref[pl.ds(step, 1), :]
    scale = scale_ref[pl.ds(step, 1), :]
    mixed = dot(every_ref[...], w_ref[...])
    hidden = x_ref[...].astype(F32) + gate * mixed
    hidden_ref[...] = hidden
    normed = (layer_norm(hidden) * (1.0 + scale) + shift).astype(BF16)
    normed_ref[pl.ds(pl.multiple_of(tile * rows, rows), rows), :] = normed
    gates_ref[...] = jax.nn.sigmoid(dot_t(normed, router_ref[...]))
    share = share_ref.shape[0]
    each = rows // share

    @pl.when(tile == rank // each)
    def _():
        start = pl.multiple_of((rank % each) * share, share)
        share_ref[...] = hidden_ref[pl.ds(start, share), :]

    @pl.when(tile == pl.num_programs(0) - 1)
    def _():
        cols = disp_ref.shape[1]
        disp_ref[...] = (
            dot(pick_ref[0], normed_ref[:, :cols]) + dot(pick_ref[1], normed_ref[:, cols:])
        ).astype(BF16)


def mix_call(
    rank, core, lane, step, att, blocks, x, modulation, router_t, picks_t, per, share, few
):
    tokens, width = x.shape
    parts = att.shape[0] // tokens
    inner = att.shape[1]
    experts = router_t.shape[0]
    steps = modulation.shape[0]
    rows = 256
    return pl.pallas_call(
        functools.partial(mix_kernel, per, len(blocks) // 2, parts, few),
        grid=(tokens // rows,),
        in_specs=[smem()] * 4
        + [
            pl.BlockSpec((parts * rows, inner), lambda i: (i, 0)),
            pl.BlockSpec((rows, width), lambda i: (i, 0)),
            pl.BlockSpec((steps, width), lambda i: (0, 2)),
            pl.BlockSpec((steps, width), lambda i: (0, 3)),
            pl.BlockSpec((steps, width), lambda i: (0, 4)),
            pl.BlockSpec(router_t.shape, lambda i: (0, 0)),
            pl.BlockSpec(picks_t.shape, lambda i: (0, 0)),
        ]
        + [pl.BlockSpec(memory_space=pl.ANY)] * len(blocks),
        out_specs=[
            pl.BlockSpec((2 * experts * per, width // 2), lambda i: (0, 0)),
            pl.BlockSpec((rows, experts), lambda i: (i, 0)),
            pl.BlockSpec((share, width), lambda i: (0, 0)),
        ],
        out_shape=[
            jax.ShapeDtypeStruct((2 * experts * per, width // 2), BF16),
            jax.ShapeDtypeStruct((tokens, experts), F32),
            jax.ShapeDtypeStruct((share, width), F32),
        ],
        scratch_shapes=[
            pltpu.VMEM((rows, width), F32),
            pltpu.VMEM((tokens, width), BF16),
            pltpu.VMEM((parts * inner, width), BF16),
            pltpu.VMEM((rows, parts * inner), BF16),
            pltpu.VMEM((2, 2 * experts * per, tokens), BF16),
            pltpu.SemaphoreType.DMA((len(blocks) * parts,)),
        ],
        compiler_params=params(62),
        name="mix",
    )(
        rank, core, lane, step, att, x, modulation, modulation, modulation, router_t, picks_t,
        *blocks,
    )


def up_kernel(per, rows_ref, w_ref, out_ref, tok_ref):
    @pl.when(pl.program_id(0) == 0)
    def _():
        count = tok_ref.shape[0]
        cols = rows_ref.shape[1]
        for half in range(2):
            pick = rows_to_half(count, per, half)
            tok_ref[:, half * cols : (half + 1) * cols] = dot(pick, rows_ref[...]).astype(BF16)

    out_ref[...] = jax.nn.gelu(dot(tok_ref[...], w_ref[0])).astype(BF16)


def up_call(rows, w, per):
    parts, width, units = w.shape
    count = rows.shape[0] // 2
    return pl.pallas_call(
        functools.partial(up_kernel, per),
        grid=(parts,),
        in_specs=[
            pl.BlockSpec(rows.shape, lambda i: (0, 0)),
            pl.BlockSpec((1, width, units), lambda i: (i, 0, 0)),
        ],
        out_specs=pl.BlockSpec((count, units), lambda i: (0, i)),
        out_shape=jax.ShapeDtypeStruct((count, parts * units), BF16),
        scratch_shapes=[pltpu.VMEM((count, width), BF16)],
        compiler_params=params(62),
        name="up",
    )(rows, w)


def down_kernel(per, places, rank_ref, hid_ref, *refs):
    out_ref = refs[-1]
    parts = 4
    units = hid_ref.shape[1] // parts
    total = None
    for (turn, row), block in zip(places, refs[:-1]):
        at = lax.rem(rank_ref[0] + turn, parts) * units + row
        some = hid_ref[:, pl.ds(pl.multiple_of(at, 128), block.shape[0])]
        term = dot(some, block[...])
        total = term if total is None else total + term
    total = total.astype(BF16)
    count = total.shape[0]

    @pl.when(pl.program_id(0) == 0)
    def _():
        out_ref[...] = dot(halves_to_rows(count, per, 0), total).astype(BF16)

    @pl.when(pl.program_id(0) == 1)
    def _():
        out_ref[...] += dot(halves_to_rows(count, per, 1), total).astype(BF16)


def down_call(rank, hidden, blocks, places, per):
    rows, units = hidden.shape
    half = blocks[0].shape[1]
    cols = half // 2
    return pl.pallas_call(
        functools.partial(down_kernel, per, places),
        grid=(2,),
        in_specs=[smem(), pl.BlockSpec((rows, units), lambda i: (0, 0))]
        + [pl.BlockSpec((block.shape[0], cols), lambda i: (0, i)) for block in blocks],
        out_specs=pl.BlockSpec((2 * rows, cols), lambda i: (0, 0)),
        out_shape=jax.ShapeDtypeStruct((2 * rows, cols), BF16),
        compiler_params=params(62),
        name="down",
    )(rank, hidden, *blocks)


def combine_kernel(per, rank_ref, gates_ref, picks_ref, counts_ref, own_ref, other_ref, out_ref):
    rank = rank_ref[0]
    tokens = gates_ref.shape[0]
    experts = gates_ref.shape[1]
    picks = picks_ref[...].astype(F32)
    counts = counts_ref[...].astype(F32)
    shape = (experts, 2 * experts * per)
    expand = ones_where(
        quotient(lax.broadcasted_iota(jnp.int32, shape, 1), 2 * per)
        == lax.broadcasted_iota(jnp.int32, shape, 0)
    )
    wide = dot(gates_ref[...].astype(BF16), expand)
    token = lax.broadcasted_iota(jnp.int32, wide.shape, 0)
    which = row_half(wide.shape, per, 1)
    partner = rank + 1 - 2 * lax.rem(rank, 2)
    cols = own_ref.shape[1]
    sums = [None, None]
    for who, rows_ref in ((rank, own_ref), (partner, other_ref)):
        row = slot_row(picks, counts, who * per, per)
        weight = jnp.where(token == row, wide, 0.0)
        for half in range(2):
            term = dot(jnp.where(which == half, weight, 0.0).astype(BF16), rows_ref[...])
            sums[half] = term if sums[half] is None else sums[half] + term
    for half in range(2):
        out_ref[:, half * cols : (half + 1) * cols] = sums[half].astype(BF16)


def combine_call(rank, gates, picks_t, counts_t, own, other, per):
    half = 2 * own.shape[1]
    vmem = pl.BlockSpec(memory_space=pltpu.VMEM)
    return pl.pallas_call(
        functools.partial(combine_kernel, per),
        in_specs=[smem()] + [vmem] * 5,
        out_specs=vmem,
        out_shape=jax.ShapeDtypeStruct((gates.shape[0], half), BF16),
        compiler_params=params(16),
        name="combine",
    )(rank, gates, picks_t, counts_t, own, other)


def final_kernel(step_ref, share_ref, gate_ref, parts_ref, out_ref):
    gate = gate_ref[pl.ds(step_ref[0], 1), :]
    half = parts_ref.shape[2]
    for b in range(2):
        cols = slice(b * half, (b + 1) * half)
        mixture = parts_ref[b].astype(F32) + parts_ref[b + 2].astype(F32)
        out_ref[:, cols] = (share_ref[:, cols] + gate[:, cols] * mixture).astype(BF16)


def final_call(step, share, modulation, parts):
    rows, width = share.shape
    return pl.pallas_call(
        final_kernel,
        grid=(1,),
        in_specs=[
            smem(),
            pl.BlockSpec((rows, width), lambda i: (0, 0)),
            pl.BlockSpec((modulation.shape[0], width), lambda i: (0, 5)),
            pl.BlockSpec(parts.shape, lambda i: (0, 0, 0)),
        ],
        out_specs=pl.BlockSpec((rows, width), lambda i: (0, 0)),
        out_shape=jax.ShapeDtypeStruct((rows, width), BF16),
        compiler_params=params(16),
        name="final",
    )(step, share, modulation, parts)


def on_device(
    frames_in,
    step_index,
    modulation,
    qkv_weight,
    qk_gain,
    out_weight,
    router_weight,
    expert_up,
    expert_down,
    picks,
    counts,
):
    _, position_count, model_width = frames_in.shape
    ffn = lax.axis_size("ffn")
    seq = lax.axis_size("seq")
    rank = lax.axis_index("ffn").astype(jnp.int32)
    rank_arr = rank.reshape(1)
    head_size = qk_gain.shape[1]
    share_len = position_count // ffn
    slot_count = picks.shape[2]
    per = slot_count // ffn
    half = model_width // 2
    x = frames_in[0]
    picks_t = jnp.transpose(picks, (1, 2, 0))[0]
    counts_t = jnp.transpose(counts, (1, 0))

    def over_seq(values):
        return lax.all_to_all(values, "seq", split_axis=0, concat_axis=0, tiled=True)

    def over_ffn(values):
        return lax.all_to_all(values, "ffn", split_axis=0, concat_axis=0, tiled=True)

    place = lax.axis_index("seq").astype(jnp.int32)
    core = lax.rem(place, 2)
    lanes = 4
    stride = seq // lanes
    lane = place // stride
    some = out_weight.shape[0] // (2 * lanes)
    out_own = lax.dynamic_slice_in_dim(out_weight, (core * lanes + lane) * some, some, 0)
    up_full = lax.all_gather(expert_up, "ffn", axis=0, tiled=True)
    down = expert_down[0]
    side = lax.rem(rank, 2)
    same_half = lax.dynamic_slice_in_dim(down, side * half, half, 1)

    def from_turn(values, turn):
        return lax.ppermute(values, "ffn", [((i + turn) % ffn, i) for i in range(ffn)])

    out_rows = [out_own] + [from_turn(out_own, turn) for turn in range(1, ffn)]
    few_units = down.shape[0] // 2
    first, second = (
        lax.dynamic_slice(down, (at, (1 - side) * half), (few_units, half))
        for at in (0, few_units)
    )
    places = ((0, 0), (1, 0), (3, 0), (2, 0), (1, few_units), (3, few_units))
    early = (from_turn(first, 1), from_turn(first, 3))
    late = (from_turn(same_half, 2), from_turn(second, 1), from_turn(second, 3))

    stacked = qkv_call(step_index, x, modulation, jnp.transpose(qkv_weight, (1, 0, 2)), qk_gain)
    stacked, out_rows = lax.optimization_barrier((stacked, out_rows))
    stacked = over_seq(stacked)
    few = position_count // seq
    attended = attention_call(stacked, few, head_size, ffn)
    out_rows = jnp.concatenate(out_rows, axis=0)

    def from_lane(values, turn):
        pairs = [((i + turn * stride) % seq, i) for i in range(seq)]
        return lax.ppermute(values, "seq", pairs)

    out_blocks = [out_rows] + [from_lane(out_rows, turn) for turn in range(1, lanes)]
    attended, out_blocks[2] = lax.optimization_barrier((attended, out_blocks[2]))
    swap = [(i, i ^ 1) for i in range(seq)]
    out_blocks = out_blocks + [lax.ppermute(b, "seq", swap) for b in out_blocks]
    every = lax.all_to_all(attended, ("seq", "ffn"), split_axis=0, concat_axis=0, tiled=True)
    every, early = lax.optimization_barrier((every, early))
    outgoing, gates, share = mix_call(
        rank_arr, core.reshape(1), lane.reshape(1), step_index, every, out_blocks, x, modulation,
        jnp.transpose(router_weight, (1, 0)), picks_t, per, share_len, few,
    )
    expert_tokens = over_seq(outgoing)
    blocks = (same_half,) + tuple(early) + late
    hidden = up_call(expert_tokens, up_full, per)
    hidden_other = lax.ppermute(hidden, "ffn", [(i, i ^ 1) for i in range(ffn)])
    own = over_seq(down_call(rank_arr, hidden, blocks, places, per))
    other = over_seq(down_call(rank_arr, hidden_other, blocks, places, per))
    mixture = combine_call(rank_arr, gates, picks_t, counts_t, own, other, per)
    parts = over_ffn(mixture).reshape(ffn, share_len, half)
    return final_call(step_index, share, modulation, parts)[None]


def solution(mesh):
    in_specs = (
        P("seq", None, None),
        P("seq"),
        P(),
        P(None, None, "ffn"),
        P(),
        P("ffn", None),
        P(),
        P("seq", None, "ffn"),
        P("seq", "ffn", None),
        P(None, "seq", None),
        P(None, "seq"),
    )
    out_specs = P("seq", "ffn", None)
    return jax.shard_map(
        on_device, mesh=mesh, in_specs=in_specs, out_specs=out_specs, check_vma=False
    )
```

```python
import functools

import jax
import jax.numpy as jnp
from jax import lax
from jax.experimental import pallas as pl
from jax.experimental.pallas import tpu as pltpu
from jax.sharding import PartitionSpec as P

BF16 = jnp.bfloat16
F32 = jnp.float32
MIB = 1 << 20


def dot(a, b):
    return jnp.dot(a, b, preferred_element_type=F32)


def dot_t(a, b):
    return lax.dot_general(a, b, (((1,), (1,)), ((), ())), preferred_element_type=F32)


def layer_norm(values):
    mean = jnp.mean(values, -1, keepdims=True)
    centred = values - mean
    variance = jnp.mean(centred * centred, -1, keepdims=True)
    return centred * lax.rsqrt(variance + 1e-06)


def quotient(values, by):
    return lax.shift_right_logical(values, by.bit_length() - 1)


def remainder(values, by):
    return values & (by - 1)


def smem():
    return pl.BlockSpec(memory_space=pltpu.SMEM)


def params(mib, **kw):
    return pltpu.CompilerParams(vmem_limit_bytes=mib * MIB, **kw)


def qkv_kernel(step_ref, x_ref, mod_ref, w_ref, gain_ref, out_ref):
    step = step_ref[0]
    width = x_ref.shape[1]
    shift = mod_ref[pl.ds(step, 1), :width]
    scale = mod_ref[pl.ds(step, 1), width:]
    normed = (layer_norm(x_ref[...].astype(F32)) * (1.0 + scale) + shift).astype(BF16)
    inner = w_ref.shape[2]
    head = gain_ref.shape[1]
    for part in range(3):
        proj = dot(normed, w_ref[part])
        if part < 2:
            gain = gain_ref[part : part + 1, :]
            for h in range(inner // head):
                one = proj[:, h * head : (h + 1) * head]
                one = one * lax.rsqrt(jnp.mean(one * one, -1, keepdims=True) + 1e-06) * gain
                lo = part * inner + h * head
                out_ref[:, lo : lo + head] = one.astype(BF16)
        else:
            out_ref[:, part * inner : (part + 1) * inner] = proj.astype(BF16)


def qkv_call(step, x, modulation, w, gain):
    tokens, width = x.shape
    inner = w.shape[2]
    rows = 256
    return pl.pallas_call(
        qkv_kernel,
        grid=(tokens // rows,),
        in_specs=[
            smem(),
            pl.BlockSpec((rows, width), lambda i: (i, 0)),
            pl.BlockSpec((modulation.shape[0], 2 * width), lambda i: (0, 0)),
            pl.BlockSpec(w.shape, lambda i: (0, 0, 0)),
            pl.BlockSpec(gain.shape, lambda i: (0, 0)),
        ],
        out_specs=pl.BlockSpec((rows, 3 * inner), lambda i: (i, 0)),
        out_shape=jax.ShapeDtypeStruct((tokens, 3 * inner), BF16),
        compiler_params=params(60),
        name="qkv",
    )(step, x, modulation, w, gain)


def attention_kernel(few, head, copies, in_ref, out_ref):
    rows = in_ref.shape[0]
    inner = out_ref.shape[1]
    row_pos = remainder(lax.broadcasted_iota(jnp.int32, (rows, rows), 0), few)
    col_pos = remainder(lax.broadcasted_iota(jnp.int32, (rows, rows), 1), few)
    same = row_pos == col_pos
    for h in range(inner // head):
        lo = h * head
        q = in_ref[:, lo : lo + head]
        k = in_ref[:, inner + lo : inner + lo + head]
        v = in_ref[:, 2 * inner + lo : 2 * inner + lo + head]
        raised = jnp.where(same, jnp.exp(dot_t(q, k) * head ** (-0.5)), 0.0)
        probs = (raised / jnp.sum(raised, -1, keepdims=True)).astype(BF16)
        each = dot(probs, v).reshape(rows // few, 1, few, head)
        each = jnp.broadcast_to(each, (rows // few, copies, few, head))
        out_ref[:, lo : lo + head] = each.reshape(copies * rows, head).astype(BF16)


def attention_call(stacked, few, head, copies):
    rows, wide = stacked.shape
    return pl.pallas_call(
        functools.partial(attention_kernel, few, head, copies),
        out_shape=jax.ShapeDtypeStruct((copies * rows, wide // 3), BF16),
        compiler_params=params(16),
        name="attention",
    )(stacked)


def spread(values, per):
    experts = values.shape[1]
    shape = (experts, experts * per)
    expand = (
        quotient(lax.broadcasted_iota(jnp.int32, shape, 1), per)
        == lax.broadcasted_iota(jnp.int32, shape, 0)
    ).astype(F32)
    return jnp.dot(values, expand, precision=lax.Precision.HIGHEST, preferred_element_type=F32)


def slot_row(picks_f32, counts_f32, first, per):
    wide = spread(picks_f32, 2 * per)
    slot = lax.broadcasted_iota(jnp.int32, wide.shape, 0)
    wanted = first + remainder(lax.broadcasted_iota(jnp.int32, wide.shape, 1), per)
    limit = spread(counts_f32, 2 * per)
    wide = jnp.where(slot.astype(F32) < limit, wide, -1.0)
    return jnp.sum(jnp.where(slot == wanted, wide, 0.0), axis=0, keepdims=True).astype(jnp.int32)


def slot_column(picks_f32, first, per):
    experts = picks_f32.shape[1]
    shape = (experts * 2 * per, experts)
    expand = (
        quotient(lax.broadcasted_iota(jnp.int32, shape, 0), 2 * per)
        == lax.broadcasted_iota(jnp.int32, shape, 1)
    ).astype(F32)
    wide = lax.dot_general(
        expand, picks_f32, (((1,), (1,)), ((), ())),
        precision=lax.Precision.HIGHEST, preferred_element_type=F32,
    )
    wanted = first + remainder(lax.broadcasted_iota(jnp.int32, wide.shape, 0), per)
    mine = lax.broadcasted_iota(jnp.int32, wide.shape, 1) == wanted
    return jnp.sum(jnp.where(mine, wide, 0.0), axis=1, keepdims=True).astype(jnp.int32)


def rows_to_half(count, per, half):
    shape = (count, 2 * count)
    row = lax.broadcasted_iota(jnp.int32, shape, 0)
    col = lax.broadcasted_iota(jnp.int32, shape, 1)
    wanted = (quotient(row, per) * 2 + half) * per + remainder(row, per)
    return ones_where(col == wanted)


def row_half(shape, per, dim):
    return remainder(quotient(lax.broadcasted_iota(jnp.int32, shape, dim), per), 2)


def ones_where(mask):
    return mask.astype(F32).astype(BF16)


def halves_to_rows(count, per, half):
    shape = (2 * count, count)
    row = lax.broadcasted_iota(jnp.int32, shape, 0)
    col = lax.broadcasted_iota(jnp.int32, shape, 1)
    wanted = (quotient(col, per) * 2 + half) * per + remainder(col, per)
    return ones_where(row == wanted)


def mix_kernel(
    per, pieces, parts, few, rank_ref, core_ref, lane_ref, step_ref, att_ref, x_ref, gate_ref, shift_ref,
    scale_ref, router_ref, picks_ref, *refs
):
    blocks = refs[: 2 * pieces]
    (disp_ref, gates_ref, share_ref, hidden_ref, normed_ref, w_ref, every_ref, pick_ref,
     sems) = refs[2 * pieces :]
    step = step_ref[0]
    rank = rank_ref[0]
    tile = pl.program_id(0)
    rows = x_ref.shape[0]
    inner = att_ref.shape[1]

    def weight_copies():
        some = blocks[0].shape[0] // parts
        for number, block in enumerate(blocks):
            which, turn = divmod(number, pieces)
            half = lax.rem(core_ref[0] + which, 2)
            place = lax.rem(lane_ref[0] + turn, pieces)
            for part_turn in range(parts):
                part = lax.rem(rank + part_turn, parts)
                to = pl.multiple_of(part * inner + half * (inner // 2) + place * some, some)
                yield pltpu.make_async_copy(
                    block.at[pl.ds(part_turn * some, some), :],
                    w_ref.at[pl.ds(to, some), :],
                    sems.at[number * parts + part_turn],
                )

    def pick_matrices():
        column = slot_column(picks_ref[...].astype(F32), rank * per, per)
        shape = (column.shape[0], normed_ref.shape[0])
        picked = lax.broadcasted_iota(jnp.int32, shape, 1) == column
        half = row_half(shape, per, 0)
        for which in range(2):
            pick_ref[which] = ones_where(picked & (half == which))

    def join():
        split = att_ref[...].astype(F32).reshape(rows // few, parts, few, inner)
        for part in range(parts):
            every_ref[:, part * inner : (part + 1) * inner] = (
                split[:, part].reshape(rows, inner).astype(BF16)
            )

    @pl.when(tile == 0)
    def _():
        copies = list(weight_copies())
        for copy in copies:
            copy.start()
        join()
        pick_matrices()
        for copy in copies:
            copy.wait()

    @pl.when(tile > 0)
    def _():
        join()

    gate = gate_ref[pl.ds(step, 1), :]
    shift = shift_ref[pl.ds(step, 1), :]
    scale = scale_ref[pl.ds(step, 1), :]
    mixed = dot(every_ref[...], w_ref[...])
    hidden = x_ref[...].astype(F32) + gate * mixed
    hidden_ref[...] = hidden
    normed = (layer_norm(hidden) * (1.0 + scale) + shift).astype(BF16)
    normed_ref[pl.ds(pl.multiple_of(tile * rows, rows), rows), :] = normed
    gates_ref[...] = jax.nn.sigmoid(dot_t(normed, router_ref[...]))
    share = share_ref.shape[0]
    each = rows // share

    @pl.when(tile == rank // each)
    def _():
        start = pl.multiple_of((rank % each) * share, share)
        share_ref[...] = hidden_ref[pl.ds(start, share), :]

    @pl.when(tile == pl.num_programs(0) - 1)
    def _():
        cols = disp_ref.shape[1]
        disp_ref[...] = (
            dot(pick_ref[0], normed_ref[:, :cols]) + dot(pick_ref[1], normed_ref[:, cols:])
        ).astype(BF16)


def mix_call(
    rank, core, lane, step, att, blocks, x, modulation, router_t, picks_t, per, share, few
):
    tokens, width = x.shape
    parts = att.shape[0] // tokens
    inner = att.shape[1]
    experts = router_t.shape[0]
    steps = modulation.shape[0]
    rows = 256
    return pl.pallas_call(
        functools.partial(mix_kernel, per, len(blocks) // 2, parts, few),
        grid=(tokens // rows,),
        in_specs=[smem()] * 4
        + [
            pl.BlockSpec((parts * rows, inner), lambda i: (i, 0)),
            pl.BlockSpec((rows, width), lambda i: (i, 0)),
            pl.BlockSpec((steps, width), lambda i: (0, 2)),
            pl.BlockSpec((steps, width), lambda i: (0, 3)),
            pl.BlockSpec((steps, width), lambda i: (0, 4)),
            pl.BlockSpec(router_t.shape, lambda i: (0, 0)),
            pl.BlockSpec(picks_t.shape, lambda i: (0, 0)),
        ]
        + [pl.BlockSpec(memory_space=pl.ANY)] * len(blocks),
        out_specs=[
            pl.BlockSpec((2 * experts * per, width // 2), lambda i: (0, 0)),
            pl.BlockSpec((rows, experts), lambda i: (i, 0)),
            pl.BlockSpec((share, width), lambda i: (0, 0)),
        ],
        out_shape=[
            jax.ShapeDtypeStruct((2 * experts * per, width // 2), BF16),
            jax.ShapeDtypeStruct((tokens, experts), F32),
            jax.ShapeDtypeStruct((share, width), F32),
        ],
        scratch_shapes=[
            pltpu.VMEM((rows, width), F32),
            pltpu.VMEM((tokens, width), BF16),
            pltpu.VMEM((parts * inner, width), BF16),
            pltpu.VMEM((rows, parts * inner), BF16),
            pltpu.VMEM((2, 2 * experts * per, tokens), BF16),
            pltpu.SemaphoreType.DMA((len(blocks) * parts,)),
        ],
        compiler_params=params(62),
        name="mix",
    )(
        rank, core, lane, step, att, x, modulation, modulation, modulation, router_t, picks_t,
        *blocks,
    )


def up_kernel(per, rows_ref, w_ref, out_ref, tok_ref):
    @pl.when(pl.program_id(0) == 0)
    def _():
        count = tok_ref.shape[0]
        cols = rows_ref.shape[1]
        for half in range(2):
            pick = rows_to_half(count, per, half)
            tok_ref[:, half * cols : (half + 1) * cols] = dot(pick, rows_ref[...]).astype(BF16)

    out_ref[...] = jax.nn.gelu(dot(tok_ref[...], w_ref[0])).astype(BF16)


def up_call(rows, w, per):
    parts, width, units = w.shape
    count = rows.shape[0] // 2
    return pl.pallas_call(
        functools.partial(up_kernel, per),
        grid=(parts,),
        in_specs=[
            pl.BlockSpec(rows.shape, lambda i: (0, 0)),
            pl.BlockSpec((1, width, units), lambda i: (i, 0, 0)),
        ],
        out_specs=pl.BlockSpec((count, units), lambda i: (0, i)),
        out_shape=jax.ShapeDtypeStruct((count, parts * units), BF16),
        scratch_shapes=[pltpu.VMEM((count, width), BF16)],
        compiler_params=params(62),
        name="up",
    )(rows, w)


def down_terms(places, rank_ref, hid_ref, blocks, total):
    parts = 4
    units = hid_ref.shape[1] // parts
    for (turn, row), block in zip(places, blocks):
        at = lax.rem(rank_ref[0] + turn, parts) * units + row
        some = hid_ref[:, pl.ds(pl.multiple_of(at, 128), block.shape[0])]
        term = dot(some, block[...])
        total = term if total is None else total + term
    return total


def begin_kernel(places, rank_ref, hid_ref, *refs):
    refs[-1][...] = down_terms(places, rank_ref, hid_ref, refs[:-1], None)


def begin_call(rank, hidden, blocks, places):
    rows, units = hidden.shape
    half = blocks[0].shape[1]
    cols = half // 2
    return pl.pallas_call(
        functools.partial(begin_kernel, places),
        grid=(2,),
        in_specs=[smem(), pl.BlockSpec((rows, units), lambda i: (0, 0))]
        + [pl.BlockSpec((block.shape[0], cols), lambda i: (0, i)) for block in blocks],
        out_specs=pl.BlockSpec((rows, cols), lambda i: (0, i)),
        out_shape=jax.ShapeDtypeStruct((rows, half), F32),
        compiler_params=params(62),
        name="begin",
    )(rank, hidden, *blocks)


def down_kernel(per, places, begun, rank_ref, hid_ref, *refs):
    out_ref = refs[-1]
    total = refs[0][...] if begun else None
    total = down_terms(places, rank_ref, hid_ref, refs[1 if begun else 0 : -1], total)
    total = total.astype(BF16)
    count = total.shape[0]

    @pl.when(pl.program_id(0) == 0)
    def _():
        out_ref[...] = dot(halves_to_rows(count, per, 0), total).astype(BF16)

    @pl.when(pl.program_id(0) == 1)
    def _():
        out_ref[...] += dot(halves_to_rows(count, per, 1), total).astype(BF16)


def down_call(rank, hidden, blocks, places, per, begun=()):
    rows, units = hidden.shape
    half = blocks[0].shape[1]
    cols = half // 2
    return pl.pallas_call(
        functools.partial(down_kernel, per, places, len(begun) > 0),
        grid=(2,),
        in_specs=[smem(), pl.BlockSpec((rows, units), lambda i: (0, 0))]
        + [pl.BlockSpec((part.shape[0], cols), lambda i: (0, i)) for part in (*begun, *blocks)],
        out_specs=pl.BlockSpec((2 * rows, cols), lambda i: (0, 0)),
        out_shape=jax.ShapeDtypeStruct((2 * rows, cols), BF16),
        compiler_params=params(62),
        name="down",
    )(rank, hidden, *begun, *blocks)


def combine_kernel(per, rank_ref, gates_ref, picks_ref, counts_ref, own_ref, other_ref, out_ref):
    rank = rank_ref[0]
    tokens = gates_ref.shape[0]
    experts = gates_ref.shape[1]
    picks = picks_ref[...].astype(F32)
    counts = counts_ref[...].astype(F32)
    shape = (experts, 2 * experts * per)
    expand = ones_where(
        quotient(lax.broadcasted_iota(jnp.int32, shape, 1), 2 * per)
        == lax.broadcasted_iota(jnp.int32, shape, 0)
    )
    wide = dot(gates_ref[...].astype(BF16), expand)
    token = lax.broadcasted_iota(jnp.int32, wide.shape, 0)
    which = row_half(wide.shape, per, 1)
    partner = rank + 1 - 2 * lax.rem(rank, 2)
    cols = own_ref.shape[1]
    sums = [None, None]
    for who, rows_ref in ((rank, own_ref), (partner, other_ref)):
        row = slot_row(picks, counts, who * per, per)
        weight = jnp.where(token == row, wide, 0.0)
        for half in range(2):
            term = dot(jnp.where(which == half, weight, 0.0).astype(BF16), rows_ref[...])
            sums[half] = term if sums[half] is None else sums[half] + term
    for half in range(2):
        out_ref[:, half * cols : (half + 1) * cols] = sums[half].astype(BF16)


def combine_call(rank, gates, picks_t, counts_t, own, other, per):
    half = 2 * own.shape[1]
    vmem = pl.BlockSpec(memory_space=pltpu.VMEM)
    return pl.pallas_call(
        functools.partial(combine_kernel, per),
        in_specs=[smem()] + [vmem] * 5,
        out_specs=vmem,
        out_shape=jax.ShapeDtypeStruct((gates.shape[0], half), BF16),
        compiler_params=params(16),
        name="combine",
    )(rank, gates, picks_t, counts_t, own, other)


def final_kernel(step_ref, share_ref, gate_ref, parts_ref, out_ref):
    gate = gate_ref[pl.ds(step_ref[0], 1), :]
    half = parts_ref.shape[2]
    for b in range(2):
        cols = slice(b * half, (b + 1) * half)
        mixture = parts_ref[b].astype(F32) + parts_ref[b + 2].astype(F32)
        out_ref[:, cols] = (share_ref[:, cols] + gate[:, cols] * mixture).astype(BF16)


def final_call(step, share, modulation, parts):
    rows, width = share.shape
    return pl.pallas_call(
        final_kernel,
        grid=(1,),
        in_specs=[
            smem(),
            pl.BlockSpec((rows, width), lambda i: (0, 0)),
            pl.BlockSpec((modulation.shape[0], width), lambda i: (0, 5)),
            pl.BlockSpec(parts.shape, lambda i: (0, 0, 0)),
        ],
        out_specs=pl.BlockSpec((rows, width), lambda i: (0, 0)),
        out_shape=jax.ShapeDtypeStruct((rows, width), BF16),
        compiler_params=params(16),
        name="final",
    )(step, share, modulation, parts)


def on_device(
    frames_in,
    step_index,
    modulation,
    qkv_weight,
    qk_gain,
    out_weight,
    router_weight,
    expert_up,
    expert_down,
    picks,
    counts,
):
    _, position_count, model_width = frames_in.shape
    ffn = lax.axis_size("ffn")
    seq = lax.axis_size("seq")
    rank = lax.axis_index("ffn").astype(jnp.int32)
    rank_arr = rank.reshape(1)
    head_size = qk_gain.shape[1]
    share_len = position_count // ffn
    slot_count = picks.shape[2]
    per = slot_count // ffn
    half = model_width // 2
    x = frames_in[0]
    picks_t = jnp.transpose(picks, (1, 2, 0))[0]
    counts_t = jnp.transpose(counts, (1, 0))

    def over_seq(values):
        return lax.all_to_all(values, "seq", split_axis=0, concat_axis=0, tiled=True)

    def over_ffn(values):
        return lax.all_to_all(values, "ffn", split_axis=0, concat_axis=0, tiled=True)

    place = lax.axis_index("seq").astype(jnp.int32)
    core = lax.rem(place, 2)
    lanes = 4
    stride = seq // lanes
    lane = place // stride
    some = out_weight.shape[0] // (2 * lanes)
    out_own = lax.dynamic_slice_in_dim(out_weight, (core * lanes + lane) * some, some, 0)
    up_full = lax.all_gather(expert_up, "ffn", axis=0, tiled=True)
    down = expert_down[0]
    side = lax.rem(rank, 2)
    same_half = lax.dynamic_slice_in_dim(down, side * half, half, 1)

    def from_turn(values, turn):
        return lax.ppermute(values, "ffn", [((i + turn) % ffn, i) for i in range(ffn)])

    out_rows = [out_own] + [from_turn(out_own, turn) for turn in range(1, ffn)]
    few_units = down.shape[0] // 2
    first, second = (
        lax.dynamic_slice(down, (at, (1 - side) * half), (few_units, half))
        for at in (0, few_units)
    )
    places = ((0, 0), (1, 0), (3, 0), (2, 0), (1, few_units), (3, few_units))
    early = (from_turn(first, 1), from_turn(first, 3))
    late = (from_turn(same_half, 2), from_turn(second, 1), from_turn(second, 3))

    stacked = qkv_call(step_index, x, modulation, jnp.transpose(qkv_weight, (1, 0, 2)), qk_gain)
    stacked = over_seq(stacked)
    few = position_count // seq
    attended = attention_call(stacked, few, head_size, ffn)
    out_rows = jnp.concatenate(out_rows, axis=0)
    attended, out_rows = lax.optimization_barrier((attended, out_rows))

    def from_lane(values, turn):
        pairs = [((i + turn * stride) % seq, i) for i in range(seq)]
        return lax.ppermute(values, "seq", pairs)

    out_blocks = [out_rows] + [from_lane(out_rows, turn) for turn in range(1, lanes)]
    swap = [(i, i ^ 1) for i in range(seq)]
    out_blocks = out_blocks + [lax.ppermute(b, "seq", swap) for b in out_blocks]
    every = lax.all_to_all(attended, ("seq", "ffn"), split_axis=0, concat_axis=0, tiled=True)
    every, early = lax.optimization_barrier((every, early))
    outgoing, gates, share = mix_call(
        rank_arr, core.reshape(1), lane.reshape(1), step_index, every, out_blocks, x, modulation,
        jnp.transpose(router_weight, (1, 0)), picks_t, per, share_len, few,
    )
    expert_tokens = over_seq(outgoing)
    blocks = (same_half,) + tuple(early) + late
    hidden = up_call(expert_tokens, up_full, per)
    hidden_other = lax.ppermute(hidden, "ffn", [(i, i ^ 1) for i in range(ffn)])
    begun = begin_call(rank_arr, hidden, blocks[:3], places[:3])
    own = over_seq(down_call(rank_arr, hidden, blocks[3:], places[3:], per, (begun,)))
    other = over_seq(down_call(rank_arr, hidden_other, blocks, places, per))
    mixture = combine_call(rank_arr, gates, picks_t, counts_t, own, other, per)
    parts = over_ffn(mixture).reshape(ffn, share_len, half)
    return final_call(step_index, share, modulation, parts)[None]


def solution(mesh):
    in_specs = (
        P("seq", None, None),
        P("seq"),
        P(),
        P(None, None, "ffn"),
        P(),
        P("ffn", None),
        P(),
        P("seq", None, "ffn"),
        P("seq", "ffn", None),
        P(None, "seq", None),
        P(None, "seq"),
    )
    out_specs = P("seq", "ffn", None)
    return jax.shard_map(
        on_device, mesh=mesh, in_specs=in_specs, out_specs=out_specs, check_vma=False
    )
```

```python
import functools

import jax
import jax.numpy as jnp
from jax import lax
from jax.experimental import pallas as pl
from jax.experimental.pallas import tpu as pltpu
from jax.sharding import PartitionSpec as P

BF16 = jnp.bfloat16
F32 = jnp.float32
MIB = 1 << 20


def dot(a, b):
    return jnp.dot(a, b, preferred_element_type=F32)


def dot_t(a, b):
    return lax.dot_general(a, b, (((1,), (1,)), ((), ())), preferred_element_type=F32)


def layer_norm(values):
    mean = jnp.mean(values, -1, keepdims=True)
    centred = values - mean
    variance = jnp.mean(centred * centred, -1, keepdims=True)
    return centred * lax.rsqrt(variance + 1e-06)


def quotient(values, by):
    return lax.shift_right_logical(values, by.bit_length() - 1)


def remainder(values, by):
    return values & (by - 1)


def smem():
    return pl.BlockSpec(memory_space=pltpu.SMEM)


def params(mib, **kw):
    return pltpu.CompilerParams(vmem_limit_bytes=mib * MIB, **kw)


def qkv_kernel(step_ref, x_ref, mod_ref, w_ref, gain_ref, out_ref):
    step = step_ref[0]
    width = x_ref.shape[1]
    shift = mod_ref[pl.ds(step, 1), :width]
    scale = mod_ref[pl.ds(step, 1), width:]
    normed = (layer_norm(x_ref[...].astype(F32)) * (1.0 + scale) + shift).astype(BF16)
    inner = w_ref.shape[2]
    head = gain_ref.shape[1]
    for part in range(3):
        proj = dot(normed, w_ref[part])
        if part < 2:
            gain = gain_ref[part : part + 1, :]
            for h in range(inner // head):
                one = proj[:, h * head : (h + 1) * head]
                one = one * lax.rsqrt(jnp.mean(one * one, -1, keepdims=True) + 1e-06) * gain
                lo = part * inner + h * head
                out_ref[:, lo : lo + head] = one.astype(BF16)
        else:
            out_ref[:, part * inner : (part + 1) * inner] = proj.astype(BF16)


def qkv_call(step, x, modulation, w, gain):
    tokens, width = x.shape
    inner = w.shape[2]
    rows = 256
    return pl.pallas_call(
        qkv_kernel,
        grid=(tokens // rows,),
        in_specs=[
            smem(),
            pl.BlockSpec((rows, width), lambda i: (i, 0)),
            pl.BlockSpec((modulation.shape[0], 2 * width), lambda i: (0, 0)),
            pl.BlockSpec(w.shape, lambda i: (0, 0, 0)),
            pl.BlockSpec(gain.shape, lambda i: (0, 0)),
        ],
        out_specs=pl.BlockSpec((rows, 3 * inner), lambda i: (i, 0)),
        out_shape=jax.ShapeDtypeStruct((tokens, 3 * inner), BF16),
        compiler_params=params(60),
        name="qkv",
    )(step, x, modulation, w, gain)


def attention_kernel(few, head, copies, in_ref, out_ref):
    rows = in_ref.shape[0]
    inner = out_ref.shape[1]
    row_pos = remainder(lax.broadcasted_iota(jnp.int32, (rows, rows), 0), few)
    col_pos = remainder(lax.broadcasted_iota(jnp.int32, (rows, rows), 1), few)
    same = row_pos == col_pos
    for h in range(inner // head):
        lo = h * head
        q = in_ref[:, lo : lo + head]
        k = in_ref[:, inner + lo : inner + lo + head]
        v = in_ref[:, 2 * inner + lo : 2 * inner + lo + head]
        raised = jnp.where(same, jnp.exp(dot_t(q, k) * head ** (-0.5)), 0.0)
        probs = (raised / jnp.sum(raised, -1, keepdims=True)).astype(BF16)
        each = dot(probs, v).reshape(rows // few, 1, few, head)
        each = jnp.broadcast_to(each, (rows // few, copies, few, head))
        out_ref[:, lo : lo + head] = each.reshape(copies * rows, head).astype(BF16)


def attention_call(stacked, few, head, copies):
    rows, wide = stacked.shape
    return pl.pallas_call(
        functools.partial(attention_kernel, few, head, copies),
        out_shape=jax.ShapeDtypeStruct((copies * rows, wide // 3), BF16),
        compiler_params=params(16),
        name="attention",
    )(stacked)


def spread(values, per):
    experts = values.shape[1]
    shape = (experts, experts * per)
    expand = (
        quotient(lax.broadcasted_iota(jnp.int32, shape, 1), per)
        == lax.broadcasted_iota(jnp.int32, shape, 0)
    ).astype(F32)
    return jnp.dot(values, expand, precision=lax.Precision.HIGHEST, preferred_element_type=F32)


def slot_row(picks_f32, counts_f32, first, per):
    wide = spread(picks_f32, 2 * per)
    slot = lax.broadcasted_iota(jnp.int32, wide.shape, 0)
    wanted = first + remainder(lax.broadcasted_iota(jnp.int32, wide.shape, 1), per)
    limit = spread(counts_f32, 2 * per)
    wide = jnp.where(slot.astype(F32) < limit, wide, -1.0)
    return jnp.sum(jnp.where(slot == wanted, wide, 0.0), axis=0, keepdims=True).astype(jnp.int32)


def slot_column(picks_f32, first, per):
    experts = picks_f32.shape[1]
    shape = (experts * 2 * per, experts)
    expand = (
        quotient(lax.broadcasted_iota(jnp.int32, shape, 0), 2 * per)
        == lax.broadcasted_iota(jnp.int32, shape, 1)
    ).astype(F32)
    wide = lax.dot_general(
        expand, picks_f32, (((1,), (1,)), ((), ())),
        precision=lax.Precision.HIGHEST, preferred_element_type=F32,
    )
    wanted = first + remainder(lax.broadcasted_iota(jnp.int32, wide.shape, 0), per)
    mine = lax.broadcasted_iota(jnp.int32, wide.shape, 1) == wanted
    return jnp.sum(jnp.where(mine, wide, 0.0), axis=1, keepdims=True).astype(jnp.int32)


def rows_to_half(count, per, half):
    shape = (count, 2 * count)
    row = lax.broadcasted_iota(jnp.int32, shape, 0)
    col = lax.broadcasted_iota(jnp.int32, shape, 1)
    wanted = (quotient(row, per) * 2 + half) * per + remainder(row, per)
    return ones_where(col == wanted)


def row_half(shape, per, dim):
    return remainder(quotient(lax.broadcasted_iota(jnp.int32, shape, dim), per), 2)


def ones_where(mask):
    return mask.astype(F32).astype(BF16)


def halves_to_rows(count, per, half):
    shape = (2 * count, count)
    row = lax.broadcasted_iota(jnp.int32, shape, 0)
    col = lax.broadcasted_iota(jnp.int32, shape, 1)
    wanted = (quotient(col, per) * 2 + half) * per + remainder(col, per)
    return ones_where(row == wanted)


def mix_kernel(
    per, pieces, parts, few, rank_ref, core_ref, lane_ref, step_ref, att_ref, x_ref, gate_ref, shift_ref,
    scale_ref, router_ref, picks_ref, *refs
):
    blocks = refs[: 2 * pieces]
    (disp_ref, gates_ref, share_ref, hidden_ref, normed_ref, w_ref, every_ref, pick_ref,
     sems) = refs[2 * pieces :]
    step = step_ref[0]
    rank = rank_ref[0]
    tile = pl.program_id(0)
    rows = x_ref.shape[0]
    inner = att_ref.shape[1]

    def weight_copies():
        some = blocks[0].shape[0] // parts
        for number, block in enumerate(blocks):
            which, turn = divmod(number, pieces)
            half = lax.rem(core_ref[0] + which, 2)
            place = lax.rem(lane_ref[0] + turn, pieces)
            for part_turn in range(parts):
                part = lax.rem(rank + part_turn, parts)
                to = pl.multiple_of(part * inner + half * (inner // 2) + place * some, some)
                yield pltpu.make_async_copy(
                    block.at[pl.ds(part_turn * some, some), :],
                    w_ref.at[pl.ds(to, some), :],
                    sems.at[number * parts + part_turn],
                )

    def pick_matrices():
        column = slot_column(picks_ref[...].astype(F32), rank * per, per)
        shape = (column.shape[0], normed_ref.shape[0])
        picked = lax.broadcasted_iota(jnp.int32, shape, 1) == column
        half = row_half(shape, per, 0)
        for which in range(2):
            pick_ref[which] = ones_where(picked & (half == which))

    def join():
        split = att_ref[...].astype(F32).reshape(rows // few, parts, few, inner)
        for part in range(parts):
            every_ref[:, part * inner : (part + 1) * inner] = (
                split[:, part].reshape(rows, inner).astype(BF16)
            )

    @pl.when(tile == 0)
    def _():
        copies = list(weight_copies())
        for copy in copies:
            copy.start()
        join()
        pick_matrices()
        for copy in copies:
            copy.wait()

    @pl.when(tile > 0)
    def _():
        join()

    gate = gate_ref[pl.ds(step, 1), :]
    shift = shift_ref[pl.ds(step, 1), :]
    scale = scale_ref[pl.ds(step, 1), :]
    mixed = dot(every_ref[...], w_ref[...])
    hidden = x_ref[...].astype(F32) + gate * mixed
    hidden_ref[...] = hidden
    normed = (layer_norm(hidden) * (1.0 + scale) + shift).astype(BF16)
    normed_ref[pl.ds(pl.multiple_of(tile * rows, rows), rows), :] = normed
    gates_ref[...] = jax.nn.sigmoid(dot_t(normed, router_ref[...]))
    share = share_ref.shape[0]
    each = rows // share

    @pl.when(tile == rank // each)
    def _():
        start = pl.multiple_of((rank % each) * share, share)
        share_ref[...] = hidden_ref[pl.ds(start, share), :]

    @pl.when(tile == pl.num_programs(0) - 1)
    def _():
        cols = disp_ref.shape[1]
        disp_ref[...] = (
            dot(pick_ref[0], normed_ref[:, :cols]) + dot(pick_ref[1], normed_ref[:, cols:])
        ).astype(BF16)


def mix_call(
    rank, core, lane, step, att, blocks, x, modulation, router_t, picks_t, per, share, few
):
    tokens, width = x.shape
    parts = att.shape[0] // tokens
    inner = att.shape[1]
    experts = router_t.shape[0]
    steps = modulation.shape[0]
    rows = 512
    return pl.pallas_call(
        functools.partial(mix_kernel, per, len(blocks) // 2, parts, few),
        grid=(tokens // rows,),
        in_specs=[smem()] * 4
        + [
            pl.BlockSpec((parts * rows, inner), lambda i: (i, 0)),
            pl.BlockSpec((rows, width), lambda i: (i, 0)),
            pl.BlockSpec((steps, width), lambda i: (0, 2)),
            pl.BlockSpec((steps, width), lambda i: (0, 3)),
            pl.BlockSpec((steps, width), lambda i: (0, 4)),
            pl.BlockSpec(router_t.shape, lambda i: (0, 0)),
            pl.BlockSpec(picks_t.shape, lambda i: (0, 0)),
        ]
        + [pl.BlockSpec(memory_space=pl.ANY)] * len(blocks),
        out_specs=[
            pl.BlockSpec((2 * experts * per, width // 2), lambda i: (0, 0)),
            pl.BlockSpec((rows, experts), lambda i: (i, 0)),
            pl.BlockSpec((share, width), lambda i: (0, 0)),
        ],
        out_shape=[
            jax.ShapeDtypeStruct((2 * experts * per, width // 2), BF16),
            jax.ShapeDtypeStruct((tokens, experts), F32),
            jax.ShapeDtypeStruct((share, width), F32),
        ],
        scratch_shapes=[
            pltpu.VMEM((rows, width), F32),
            pltpu.VMEM((tokens, width), BF16),
            pltpu.VMEM((parts * inner, width), BF16),
            pltpu.VMEM((rows, parts * inner), BF16),
            pltpu.VMEM((2, 2 * experts * per, tokens), BF16),
            pltpu.SemaphoreType.DMA((len(blocks) * parts,)),
        ],
        compiler_params=params(62),
        name="mix",
    )(
        rank, core, lane, step, att, x, modulation, modulation, modulation, router_t, picks_t,
        *blocks,
    )


def up_kernel(per, rows_ref, w_ref, out_ref, tok_ref):
    @pl.when(pl.program_id(0) == 0)
    def _():
        count = tok_ref.shape[0]
        cols = rows_ref.shape[1]
        for half in range(2):
            pick = rows_to_half(count, per, half)
            tok_ref[:, half * cols : (half + 1) * cols] = dot(pick, rows_ref[...]).astype(BF16)

    out_ref[...] = jax.nn.gelu(dot(tok_ref[...], w_ref[0])).astype(BF16)


def up_call(rows, w, per):
    parts, width, units = w.shape
    count = rows.shape[0] // 2
    return pl.pallas_call(
        functools.partial(up_kernel, per),
        grid=(parts,),
        in_specs=[
            pl.BlockSpec(rows.shape, lambda i: (0, 0)),
            pl.BlockSpec((1, width, units), lambda i: (i, 0, 0)),
        ],
        out_specs=pl.BlockSpec((count, units), lambda i: (0, i)),
        out_shape=jax.ShapeDtypeStruct((count, parts * units), BF16),
        scratch_shapes=[pltpu.VMEM((count, width), BF16)],
        compiler_params=params(62),
        name="up",
    )(rows, w)


def down_terms(places, rank_ref, hid_ref, blocks, total):
    parts = 4
    units = hid_ref.shape[1] // parts
    for (turn, row), block in zip(places, blocks):
        at = lax.rem(rank_ref[0] + turn, parts) * units + row
        some = hid_ref[:, pl.ds(pl.multiple_of(at, 128), block.shape[0])]
        term = dot(some, block[...])
        total = term if total is None else total + term
    return total


def begin_kernel(places, rank_ref, hid_ref, *refs):
    refs[-1][...] = down_terms(places, rank_ref, hid_ref, refs[:-1], None)


def begin_call(rank, hidden, blocks, places):
    rows, units = hidden.shape
    half = blocks[0].shape[1]
    cols = half // 2
    return pl.pallas_call(
        functools.partial(begin_kernel, places),
        grid=(2,),
        in_specs=[smem(), pl.BlockSpec((rows, units), lambda i: (0, 0))]
        + [pl.BlockSpec((block.shape[0], cols), lambda i: (0, i)) for block in blocks],
        out_specs=pl.BlockSpec((rows, cols), lambda i: (0, i)),
        out_shape=jax.ShapeDtypeStruct((rows, half), F32),
        compiler_params=params(62),
        name="begin",
    )(rank, hidden, *blocks)


def down_kernel(per, places, begun, rank_ref, hid_ref, *refs):
    out_ref = refs[-1]
    total = refs[0][...] if begun else None
    total = down_terms(places, rank_ref, hid_ref, refs[1 if begun else 0 : -1], total)
    total = total.astype(BF16)
    count = total.shape[0]

    @pl.when(pl.program_id(0) == 0)
    def _():
        out_ref[...] = dot(halves_to_rows(count, per, 0), total).astype(BF16)

    @pl.when(pl.program_id(0) == 1)
    def _():
        out_ref[...] += dot(halves_to_rows(count, per, 1), total).astype(BF16)


def down_call(rank, hidden, blocks, places, per, begun=()):
    rows, units = hidden.shape
    half = blocks[0].shape[1]
    cols = half // 2
    return pl.pallas_call(
        functools.partial(down_kernel, per, places, len(begun) > 0),
        grid=(2,),
        in_specs=[smem(), pl.BlockSpec((rows, units), lambda i: (0, 0))]
        + [pl.BlockSpec((part.shape[0], cols), lambda i: (0, i)) for part in (*begun, *blocks)],
        out_specs=pl.BlockSpec((2 * rows, cols), lambda i: (0, 0)),
        out_shape=jax.ShapeDtypeStruct((2 * rows, cols), BF16),
        compiler_params=params(62),
        name="down",
    )(rank, hidden, *begun, *blocks)


def combine_kernel(per, rank_ref, gates_ref, picks_ref, counts_ref, own_ref, other_ref, out_ref):
    rank = rank_ref[0]
    tokens = gates_ref.shape[0]
    experts = gates_ref.shape[1]
    picks = picks_ref[...].astype(F32)
    counts = counts_ref[...].astype(F32)
    shape = (experts, 2 * experts * per)
    expand = ones_where(
        quotient(lax.broadcasted_iota(jnp.int32, shape, 1), 2 * per)
        == lax.broadcasted_iota(jnp.int32, shape, 0)
    )
    wide = dot(gates_ref[...].astype(BF16), expand)
    token = lax.broadcasted_iota(jnp.int32, wide.shape, 0)
    which = row_half(wide.shape, per, 1)
    partner = rank + 1 - 2 * lax.rem(rank, 2)
    cols = own_ref.shape[1]
    sums = [None, None]
    for who, rows_ref in ((rank, own_ref), (partner, other_ref)):
        row = slot_row(picks, counts, who * per, per)
        weight = jnp.where(token == row, wide, 0.0)
        for half in range(2):
            term = dot(jnp.where(which == half, weight, 0.0).astype(BF16), rows_ref[...])
            sums[half] = term if sums[half] is None else sums[half] + term
    for half in range(2):
        out_ref[:, half * cols : (half + 1) * cols] = sums[half].astype(BF16)


def combine_call(rank, gates, picks_t, counts_t, own, other, per):
    half = 2 * own.shape[1]
    vmem = pl.BlockSpec(memory_space=pltpu.VMEM)
    return pl.pallas_call(
        functools.partial(combine_kernel, per),
        in_specs=[smem()] + [vmem] * 5,
        out_specs=vmem,
        out_shape=jax.ShapeDtypeStruct((gates.shape[0], half), BF16),
        compiler_params=params(16),
        name="combine",
    )(rank, gates, picks_t, counts_t, own, other)


def final_kernel(step_ref, share_ref, gate_ref, parts_ref, out_ref):
    gate = gate_ref[pl.ds(step_ref[0], 1), :]
    half = parts_ref.shape[2]
    for b in range(2):
        cols = slice(b * half, (b + 1) * half)
        mixture = parts_ref[b].astype(F32) + parts_ref[b + 2].astype(F32)
        out_ref[:, cols] = (share_ref[:, cols] + gate[:, cols] * mixture).astype(BF16)


def final_call(step, share, modulation, parts):
    rows, width = share.shape
    return pl.pallas_call(
        final_kernel,
        grid=(1,),
        in_specs=[
            smem(),
            pl.BlockSpec((rows, width), lambda i: (0, 0)),
            pl.BlockSpec((modulation.shape[0], width), lambda i: (0, 5)),
            pl.BlockSpec(parts.shape, lambda i: (0, 0, 0)),
        ],
        out_specs=pl.BlockSpec((rows, width), lambda i: (0, 0)),
        out_shape=jax.ShapeDtypeStruct((rows, width), BF16),
        compiler_params=params(16),
        name="final",
    )(step, share, modulation, parts)


def on_device(
    frames_in,
    step_index,
    modulation,
    qkv_weight,
    qk_gain,
    out_weight,
    router_weight,
    expert_up,
    expert_down,
    picks,
    counts,
):
    _, position_count, model_width = frames_in.shape
    ffn = lax.axis_size("ffn")
    seq = lax.axis_size("seq")
    rank = lax.axis_index("ffn").astype(jnp.int32)
    rank_arr = rank.reshape(1)
    head_size = qk_gain.shape[1]
    share_len = position_count // ffn
    slot_count = picks.shape[2]
    per = slot_count // ffn
    half = model_width // 2
    x = frames_in[0]
    picks_t = jnp.transpose(picks, (1, 2, 0))[0]
    counts_t = jnp.transpose(counts, (1, 0))

    def over_seq(values):
        return lax.all_to_all(values, "seq", split_axis=0, concat_axis=0, tiled=True)

    def over_ffn(values):
        return lax.all_to_all(values, "ffn", split_axis=0, concat_axis=0, tiled=True)

    place = lax.axis_index("seq").astype(jnp.int32)
    core = lax.rem(place, 2)
    lanes = 4
    stride = seq // lanes
    lane = place // stride
    some = out_weight.shape[0] // (2 * lanes)
    out_own = lax.dynamic_slice_in_dim(out_weight, (core * lanes + lane) * some, some, 0)
    up_full = lax.all_gather(expert_up, "ffn", axis=0, tiled=True)
    down = expert_down[0]
    side = lax.rem(rank, 2)
    same_half = lax.dynamic_slice_in_dim(down, side * half, half, 1)

    def from_turn(values, turn):
        return lax.ppermute(values, "ffn", [((i + turn) % ffn, i) for i in range(ffn)])

    out_rows = [out_own] + [from_turn(out_own, turn) for turn in range(1, ffn)]
    few_units = down.shape[0] // 2
    first, second = (
        lax.dynamic_slice(down, (at, (1 - side) * half), (few_units, half))
        for at in (0, few_units)
    )
    places = ((0, 0), (1, 0), (3, 0), (2, 0), (1, few_units), (3, few_units))
    early = (from_turn(first, 1), from_turn(first, 3))
    late = (from_turn(same_half, 2), from_turn(second, 1), from_turn(second, 3))

    stacked = qkv_call(step_index, x, modulation, jnp.transpose(qkv_weight, (1, 0, 2)), qk_gain)
    stacked = over_seq(stacked)
    few = position_count // seq
    attended = attention_call(stacked, few, head_size, ffn)
    out_rows = jnp.concatenate(out_rows, axis=0)
    attended, out_rows = lax.optimization_barrier((attended, out_rows))

    def from_lane(values, turn):
        pairs = [((i + turn * stride) % seq, i) for i in range(seq)]
        return lax.ppermute(values, "seq", pairs)

    out_blocks = [out_rows] + [from_lane(out_rows, turn) for turn in range(1, lanes)]
    swap = [(i, i ^ 1) for i in range(seq)]
    out_blocks = out_blocks + [lax.ppermute(b, "seq", swap) for b in out_blocks]
    every = lax.all_to_all(attended, ("seq", "ffn"), split_axis=0, concat_axis=0, tiled=True)
    every, early = lax.optimization_barrier((every, early))
    outgoing, gates, share = mix_call(
        rank_arr, core.reshape(1), lane.reshape(1), step_index, every, out_blocks, x, modulation,
        jnp.transpose(router_weight, (1, 0)), picks_t, per, share_len, few,
    )
    expert_tokens = over_seq(outgoing)
    blocks = (same_half,) + tuple(early) + late
    hidden = up_call(expert_tokens, up_full, per)
    hidden_other = lax.ppermute(hidden, "ffn", [(i, i ^ 1) for i in range(ffn)])
    begun = begin_call(rank_arr, hidden, blocks[:3], places[:3])
    own = over_seq(down_call(rank_arr, hidden, blocks[3:], places[3:], per, (begun,)))
    other = over_seq(down_call(rank_arr, hidden_other, blocks, places, per))
    mixture = combine_call(rank_arr, gates, picks_t, counts_t, own, other, per)
    parts = over_ffn(mixture).reshape(ffn, share_len, half)
    return final_call(step_index, share, modulation, parts)[None]


def solution(mesh):
    in_specs = (
        P("seq", None, None),
        P("seq"),
        P(),
        P(None, None, "ffn"),
        P(),
        P("ffn", None),
        P(),
        P("seq", None, "ffn"),
        P("seq", "ffn", None),
        P(None, "seq", None),
        P(None, "seq"),
    )
    out_specs = P("seq", "ffn", None)
    return jax.shard_map(
        on_device, mesh=mesh, in_specs=in_specs, out_specs=out_specs, check_vma=False
    )
```
